32 devices in a mesh: ctx: 8 (over z, core), fsdp: 4 (over y, x).
Axes of the slice: x: 2, y: 2, z: 4, core: 2. Of those that a mesh axis runs over, the one named last changes fastest.
Arguments:
- tokens: bfloat16 [4, 1536, 2048], P('fsdp', 'ctx'), may hold values from -6 to 6
- cotangent: bfloat16 [4, 1536, 2048], P('fsdp', 'ctx'), may hold values from -6 to 6
- seq_lengths: int32 [4, 4], P('fsdp'), may hold values from 1 to 768, 1536 in all within a row
- token_order: int32 [4, 1536], P('fsdp'), may hold values from 0 to 1535, as said below
- ln_gain: bfloat16 [2048], P('fsdp'), may hold values from 0.5 to 1.5
- ln_bias: bfloat16 [2048], P('fsdp'), may hold values from -1.1953125 to 1.1953125
- w_qkv: bfloat16 [2048, 6144], P('fsdp'), may hold values from -0.125 to 0.125
- q_bias: bfloat16 [2048], P('fsdp'), may hold values from -3 to 3
- k_bias: bfloat16 [1024], P('fsdp'), may hold values from -3 to 3
- v_bias: bfloat16 [2048], P('fsdp'), may hold values from -3 to 3
- w_out: bfloat16 [2048, 2048], P('fsdp'), may hold values from -0.5 to 0.5
- out_bias: bfloat16 [2048], P('fsdp'), may hold values from -4 to 4
- w_up: bfloat16 [2048, 8192], P('fsdp'), may hold values from -0.125 to 0.125
- up_bias: bfloat16 [8192], P('fsdp'), may hold values from -1.1953125 to 1.1953125
- w_down: bfloat16 [8192, 2048], P('fsdp'), may hold values from -0.125 to 0.125
- down_bias: bfloat16 [2048], P('fsdp'), may hold values from -4 to 4
Outputs:
- out_act: bfloat16 [4, 1536, 2048], P('fsdp', 'ctx')
- d_tokens: float32 [4, 1536, 2048], P('fsdp', 'ctx')
- layernorm_gain_gradient: float32 [2048], P('fsdp')
- d_ln_bias: float32 [2048], P('fsdp')
- d_w_qkv: float32 [2048, 6144], P('fsdp')
- d_q_bias: float32 [2048], P('fsdp')
- d_k_bias: float32 [1024], P('fsdp')
- d_v_bias: float32 [2048], P('fsdp')
- d_w_out: float32 [2048, 2048], P('fsdp')
- d_out_bias: float32 [2048], P('fsdp')
- d_w_up: float32 [2048, 8192], P('fsdp')
- d_up_bias: float32 [8192], P('fsdp')
- d_w_down: float32 [8192, 2048], P('fsdp')
- d_down_bias: float32 [2048], P('fsdp')
The draws below stay inside these ranges and needn't reach their ends.
Inputs may be any that keep to these rules, and one draw needn't show every extreme that they name: `seq_lengths`: lengths of a group's 4 sequences in the order in which they are laid end to end; each row sums to 1536. `token_order`: each row is a permutation; slots run device after device along ctx, 192 a device. Tokens r * (8) to (r + 1) * 8 - 1 lie on different devices.
All inputs are finite; a program needn't handle non-finite values.
Results may differ from the reference program's by a relative error of at most 0.035.
Values may be sent and summed in bfloat16 or wider, within the bound.
A program may use at most 576 MiB of HBM per device.

```python
import math
import jax
import jax.numpy as jnp
import numpy as np
from jax import lax

D = 2048
HEADS = 32
HD = 64
ROT = 32
FF = 8192
TOK_DEV = 192
SEQS = 4
CTX_TOK = 1536
MAX_LEN = 768
GROUPS = 4


def draw_token_order(key, part):
    rounds = TOK_DEV
    dealers = CTX_TOK // TOK_DEV
    key_deal, key_slot = jax.random.split(jax.random.fold_in(key, 11))
    deal_scores = jax.random.randint(key_deal, (GROUPS, rounds, dealers), 0, 1 << 20) * dealers + jnp.arange(dealers, dtype=jnp.int32)[None, None, :]
    device = jnp.argsort(deal_scores, axis=-1, stable=True).astype(jnp.int32)
    slot_scores = jax.random.randint(key_slot, (GROUPS, dealers, rounds), 0, 1 << 20) * rounds + jnp.arange(rounds, dtype=jnp.int32)[None, None, :]
    slot = jnp.argsort(slot_scores, axis=-1, stable=True).astype(jnp.int32)
    slot_of = jnp.take_along_axis(jnp.transpose(slot, (0, 2, 1)), device, axis=2)
    place = (device * rounds + slot_of).reshape(GROUPS, CTX_TOK)
    initial = (jnp.arange(rounds, dtype=jnp.int32)[:, None] * dealers + jnp.arange(dealers, dtype=jnp.int32)[None, :]).reshape(CTX_TOK)
    initial = jnp.broadcast_to(initial[None, :], (GROUPS, CTX_TOK))
    rows_index = jnp.broadcast_to(jnp.arange(GROUPS, dtype=jnp.int32)[:, None], (GROUPS, CTX_TOK))
    result = jnp.zeros((GROUPS, CTX_TOK), jnp.int32).at[rows_index, place].set(initial)
    return result


def steps_of(stream_key, extent, cuts, smallest, top_value):
    loudness, own = 1.0, jax.random.fold_in(stream_key, 6)
    for axis_at, blocks in cuts:
        steps = jnp.exp(jax.random.uniform(jax.random.fold_in(own, axis_at), (blocks,), jnp.float32, smallest / len(cuts), top_value / len(cuts)))
        loudness = loudness * jnp.repeat(steps, extent[axis_at] // blocks).reshape([-1 if axis == axis_at else 1 for axis in range(len(extent))])
    return loudness


def split_up(count, total, most, slope):
    portions = [(1 << 20) // math.isqrt(rank ** slope) + 1 for rank in range(2, count + 1)]
    rest, holding = total - most - (count - 1), [1] * (count - 1)
    while rest > 0:
        movable = [i for i in range(count - 1) if holding[i] < most]
        mass, left = sum([portions[i] for i in movable]), rest
        for i in movable:
            addition = min(most - holding[i], max(1, left * portions[i] // mass), rest)
            holding[i] = holding[i] + addition
            rest = rest - addition
    return np.array([most] + holding)


def ragged_sizes(stream_key, number_of, total, bound, skew):
    if number_of == 2:
        one = jax.random.randint(stream_key, (), max(1, total - bound), min(bound, total - 1) + 1)
        return jnp.stack([one, total - one])
    sizes = jnp.asarray(split_up(number_of, total, bound, skew), jnp.int32)
    twos = (number_of - 1) // 2
    source_of, receiver = sizes[1:1 + 2 * twos:2], sizes[2:2 + 2 * twos:2]
    margin = jnp.minimum(source_of - 1, bound - receiver)
    passed = jax.random.randint(jax.random.fold_in(stream_key, 1), (twos,), 0, 1 << 20) % (margin + 1)
    sizes = sizes.at[1:1 + 2 * twos:2].set(source_of - passed).at[2:2 + 2 * twos:2].set(receiver + passed)
    return sizes[jax.random.permutation(jax.random.fold_in(stream_key, 2), number_of)]


def normal_values(own_key, dims, spread, bound, cuts=(), kind=jnp.bfloat16):
    drawn = spread * jax.random.normal(own_key, dims, jnp.float32)
    if cuts:
        drawn = drawn * steps_of(own_key, dims, cuts, -0.22, 0.18)
    return jnp.clip(drawn, -bound, bound).astype(kind)


def setup_inputs(seed: int = 0) -> dict:
    splits = jax.random.split(jax.random.key(seed), 17)
    tokens = normal_values(splits[0], (GROUPS, CTX_TOK, D), 1.0, 6.0, ((0, 4), (1, 8)))
    cotangent = normal_values(splits[1], (GROUPS, CTX_TOK, D), 1.0, 6.0, ((0, 4), (1, 8)))
    seq_lengths = jax.vmap(lambda own: ragged_sizes(own, SEQS, CTX_TOK, MAX_LEN, 2))(jax.random.split(splits[2], GROUPS)).reshape((GROUPS, SEQS)).astype(jnp.int32)
    token_order = draw_token_order(jax.random.fold_in(splits[16], 71), 0)
    ln_gain = jnp.clip(1.0 + 0.1 * jax.random.normal(splits[4], (D,), jnp.float32), 0.5, 1.5).astype(jnp.bfloat16)
    ln_bias = normal_values(splits[5], (D,), 0.2, 1.1953125, ((0, 4),))
    w_qkv = normal_values(splits[6], (D, 3 * D), D ** -0.5, 0.125, ((0, 4),))
    q_bias = normal_values(splits[7], (D,), 0.5, 3.0, ((0, 4),))
    k_bias = normal_values(splits[8], (HEADS * ROT,), 0.5, 3.0, ((0, 4),))
    v_bias = normal_values(splits[9], (D,), 0.5, 3.0, ((0, 4),))
    w_out = normal_values(splits[10], (D, D), (max(D // 16, 1)) ** -0.5, 0.5, ((0, 4),))
    out_bias = normal_values(splits[11], (D,), 0.7, 4.0, ((0, 4),))
    w_up = normal_values(splits[12], (D, FF), D ** -0.5, 0.125, ((0, 4),))
    up_bias = normal_values(splits[13], (FF,), 0.2, 1.1953125, ((0, 4),))
    w_down = normal_values(splits[14], (FF, D), (FF // 4) ** -0.5, 0.125, ((0, 4),))
    down_bias = normal_values(splits[15], (D,), 0.7, 4.0, ((0, 4),))
    return dict(tokens=tokens, cotangent=cotangent, seq_lengths=seq_lengths, token_order=token_order, ln_gain=ln_gain, ln_bias=ln_bias, w_qkv=w_qkv, q_bias=q_bias, k_bias=k_bias, v_bias=v_bias, w_out=w_out, out_bias=out_bias, w_up=w_up, up_bias=up_bias, w_down=w_down, down_bias=down_bias)


@jax.custom_vjp
def low(v):
    return lax.optimization_barrier(v.astype(jnp.bfloat16)).astype(jnp.float32)

@jax.custom_vjp
def low_back(v):
    return v

def low_keep(v):
    return (low(v), None)

def low_pass(kept, grad):
    return (grad,)

def back_keep(v):
    return (v, None)

def back_low(kept, grad):
    return (low(grad),)
low.defvjp(low_keep, low_pass)
low_back.defvjp(back_keep, back_low)
highest = lax.Precision.HIGHEST

def token_tables(length_row, order_row):
    bounds = jnp.cumsum(length_row).astype(jnp.int32)
    starts = (bounds - length_row).astype(jnp.int32)
    segment = lax.optimization_barrier(jnp.sum((order_row[:, None] >= bounds[None, :]).astype(jnp.int32), axis=1)).astype(jnp.int32)
    member = segment[:, None] == jnp.arange(length_row.shape[0], dtype=jnp.int32)[None, :]
    offset = lax.optimization_barrier(jnp.sum(jnp.where(member, starts[None, :], 0), axis=1)).astype(jnp.int32)
    return (segment, (order_row - offset).astype(jnp.int32))

def rotary_tables(position):
    frequency = 10000.0 ** (-jnp.arange(ROT // 2, dtype=jnp.float32) * 2.0 / ROT)
    angles = position.astype(jnp.float32)[:, None] * frequency[None, :]
    return (jnp.cos(angles), jnp.sin(angles))

def rotate(values, cosine_table, sine_table):
    half = ROT // 2
    front_half = values[..., :half]
    back_half = values[..., half:ROT]
    remainder = values[..., ROT:]
    cosine_part = cosine_table[:, None, :]
    sine_part = sine_table[:, None, :]
    return jnp.concatenate([front_half * cosine_part - back_half * sine_part, back_half * cosine_part + front_half * sine_part, remainder], axis=-1)

def layer_group(params, tokens_f, segment, position, order_row):
    ln_gain, ln_bias, w_qkv, q_bias, k_bias, v_bias, w_out, out_bias, w_up, up_bias, w_down, down_bias = params
    row_count = tokens_f.shape[0]
    average = lax.optimization_barrier(jnp.mean(tokens_f, axis=-1, keepdims=True))
    centered_input = tokens_f - average
    variance = lax.optimization_barrier(jnp.mean(centered_input * centered_input, axis=-1, keepdims=True))
    normed = centered_input * lax.rsqrt(variance + 1e-05) * ln_gain + ln_bias
    normalized_reduced_precision = low(normed)
    key_pad = jnp.pad(k_bias.reshape(HEADS, ROT), ((0, 0), (0, HD - ROT))).reshape(D)
    bias_all = jnp.concatenate([q_bias, key_pad, v_bias])
    projected = low_back(jnp.dot(normalized_reduced_precision, w_qkv, precision=highest) + bias_all)
    cosine_table, sine_table = rotary_tables(position)
    queries = low(rotate(projected[:, :D].reshape(row_count, HEADS, HD), cosine_table, sine_table))
    keys = low(rotate(projected[:, D:2 * D].reshape(row_count, HEADS, HD), cosine_table, sine_table))
    values = low(projected[:, 2 * D:].reshape(row_count, HEADS, HD))
    block = 512 if row_count % 512 == 0 else row_count
    blocks = row_count // block

    def attend(pieces):
        query_block, order_block, segment_block = pieces
        scores = 0.125 * jnp.einsum('qhd,khd->hqk', query_block, keys, precision=highest)
        scores = low_back(scores)
        allowed = (segment_block[:, None] == segment[None, :]) & (order_row[None, :] <= order_block[:, None])
        scores = jnp.where(allowed[None], scores, -1e+30)
        probs = low(jax.nn.softmax(scores, axis=-1))
        return jnp.einsum('hqk,khd->qhd', probs, values, precision=highest)
    mixed = lax.map(jax.checkpoint(attend), (queries.reshape(blocks, block, HEADS, HD), order_row.reshape(blocks, block), segment.reshape(blocks, block)))
    attended = low_back(low(mixed.reshape(row_count, D)))
    attn_branch = jnp.dot(attended, w_out, precision=highest) + out_bias
    hidden = low_back(jnp.dot(normalized_reduced_precision, w_up, precision=highest) + up_bias)
    activated = low(jax.nn.gelu(hidden, approximate=True))
    mlp_branch = jnp.dot(activated, w_down, precision=highest) + down_bias
    return tokens_f + attn_branch + mlp_branch

def reference(tokens, cotangent, seq_lengths, token_order, ln_gain, ln_bias, w_qkv, q_bias, k_bias, v_bias, w_out, out_bias, w_up, up_bias, w_down, down_bias):
    params = (ln_gain.astype(jnp.float32), ln_bias.astype(jnp.float32), w_qkv.astype(jnp.float32), q_bias.astype(jnp.float32), k_bias.astype(jnp.float32), v_bias.astype(jnp.float32), w_out.astype(jnp.float32), out_bias.astype(jnp.float32), w_up.astype(jnp.float32), up_bias.astype(jnp.float32), w_down.astype(jnp.float32), down_bias.astype(jnp.float32))
    segments, positions = jax.vmap(token_tables)(seq_lengths, token_order)
    tokens_f = tokens.astype(jnp.float32)

    def forward(weights, inputs):

        def one_group(pieces):
            group_tokens, group_segment, group_position, group_order = pieces
            return layer_group(weights, group_tokens, group_segment, group_position, group_order)
        return lax.map(jax.checkpoint(one_group), (inputs, segments, positions, token_order))
    outputs, pullback = jax.vjp(forward, params, tokens_f)
    grad_params, grad_tokens = pullback(cotangent.astype(jnp.float32))
    return (outputs.astype(jnp.bfloat16), grad_tokens, grad_params[0], grad_params[1], grad_params[2], grad_params[3], grad_params[4], grad_params[5], grad_params[6], grad_params[7], grad_params[8], grad_params[9], grad_params[10], grad_params[11])
```

```python
import functools

import jax
import jax.numpy as jnp
from jax import lax
from jax.experimental import pallas as pl
from jax.experimental.pallas import tpu as pltpu
from jax.sharding import PartitionSpec as P

D = 2048
HEADS = 32
HD = 64
ROT = 32
FF = 8192
LANES = 128
BF = jnp.bfloat16
F32 = jnp.float32


def dot_nn(a, b):
    return lax.dot_general(a, b, (((1,), (0,)), ((), ())), preferred_element_type=F32)


def dot_nt(a, b):
    return lax.dot_general(a, b, (((1,), (1,)), ((), ())), preferred_element_type=F32)


def dot_tn(a, b):
    return lax.dot_general(a, b, (((0,), (0,)), ((), ())), preferred_element_type=F32)


def wide(table, width):
    return jnp.concatenate([table] * (width // LANES), axis=1)


def partner(values):
    width = values.shape[1]
    lane = lax.broadcasted_iota(jnp.int32, values.shape, 1) % HD
    half = ROT // 2
    return jnp.where(
        lane < half, pltpu.roll(values, width - half, 1), pltpu.roll(values, half, 1)
    )


def sort_norm_project(
    x_ref, rank_ref, gain_ref, shift_ref, w_ref, bias_ref, cos_ref, sin_ref,
    normed_ref, q_ref, k_ref, v_ref,
):
    rows = x_ref.shape[1]
    width = q_ref.shape[2]
    place = lax.broadcasted_iota(jnp.int32, (rows, rows), 0)
    pick = jnp.where(rank_ref[0] == place, 1.0, 0.0).astype(BF)
    x = dot_nn(pick, x_ref[0])
    mean = jnp.mean(x, axis=1, keepdims=True)
    centered = x - mean
    variance = jnp.mean(centered * centered, axis=1, keepdims=True)
    normed = (centered * lax.rsqrt(variance + 1e-05) * gain_ref[...] + shift_ref[...]).astype(BF)
    normed_ref[0] = normed
    projected = dot_nn(normed, w_ref[...]) + bias_ref[...]
    cosine, sine = wide(cos_ref[0], width), wide(sin_ref[0], width)
    q = projected[:, :width]
    k = projected[:, width : 2 * width]
    q = (q * cosine + partner(q) * sine).astype(BF)
    q_ref[0] = (q.astype(F32) * 0.125).astype(BF)
    k_ref[0] = (k * cosine + partner(k) * sine).astype(BF)
    v_ref[0] = projected[:, 2 * width :].astype(BF)


def qkv_call(x_all, rank, gain, shift, weights, bias, cosine, sine):
    dealers, rows, _ = x_all.shape
    width = weights.shape[1] // 3
    whole = lambda *shape: pl.BlockSpec(shape, lambda i: (0,) * len(shape))
    each = lambda *shape: pl.BlockSpec((1,) + shape, lambda i: (i, 0, 0))
    out = lambda w: jax.ShapeDtypeStruct((dealers, rows, w), BF)
    return pl.pallas_call(
        sort_norm_project,
        name="sort_norm_project",
        grid=(dealers,),
        in_specs=[
            each(rows, D), each(1, rows), whole(1, D), whole(1, D),
            whole(D, 3 * width), whole(1, 3 * width), each(rows, LANES), each(rows, LANES),
        ],
        out_specs=[each(rows, D)] + [each(rows, width)] * 3,
        out_shape=[out(D), out(width), out(width), out(width)],
        compiler_params=pltpu.CompilerParams(vmem_limit_bytes=48 * 2**20),
    )(x_all, rank, gain, shift, weights, bias, cosine, sine)


def flash_forward(low_ref, q_ref, col_ref, row_ref, k_ref, v_ref, o_ref, of_ref, lse_ref):
    block = pl.program_id(0)
    dealers, rounds, width = q_ref.shape
    size = dealers * rounds
    heads = width // HD
    q = q_ref[...].reshape(size, width)
    col = col_ref[...].reshape(size, 2)
    top, bottom = col[:, 0:1], col[:, 1:2]
    head_of = lax.broadcasted_iota(jnp.int32, (size, width), 1) // HD
    q_of = [jnp.where(head_of == h, q, jnp.zeros_like(q)) for h in range(heads)]

    def step(j, carry):
        at = block - j
        running, total, mixed = carry
        window = pl.ds(pl.multiple_of(at * rounds, rounds), rounds)
        k = k_ref[:, window, :].reshape(size, width)
        v = v_ref[:, window, :].reshape(size, width)
        order = row_ref[at]
        allowed = (order <= top) & (order >= bottom)
        new_running, new_total = [], []
        for h in range(heads):
            scores = jnp.where(allowed, dot_nt(q_of[h], k), -1e30)
            peak = jnp.maximum(running[h], jnp.max(scores, axis=1, keepdims=True))
            probs = jnp.exp(scores - peak)
            scale = jnp.exp(running[h] - peak)
            new_running.append(peak)
            new_total.append(total[h] * scale + jnp.sum(probs, axis=1, keepdims=True))
            mixed = jnp.where(head_of == h, mixed * scale + dot_nn(probs.astype(BF), v), mixed)
        return (new_running, new_total, mixed)

    start = (
        [jnp.full((size, 1), -1e30, F32)] * heads,
        [jnp.zeros((size, 1), F32)] * heads,
        jnp.zeros((size, width), F32),
    )
    running, total, mixed = lax.fori_loop(0, block - low_ref[block] + 1, step, start)
    weight = jnp.zeros((size, width), F32)
    for h in range(heads):
        weight = jnp.where(head_of == h, 1.0 / total[h], weight)
    mixed = mixed * weight
    o_ref[...] = mixed.astype(BF).reshape(dealers, rounds, width)
    of_ref[...] = mixed.reshape(dealers, rounds, width)
    lse = [running[h] + jnp.log(total[h]) for h in range(heads)]
    lse_ref[...] = jnp.concatenate(lse, axis=1).reshape(dealers, rounds, heads)


def flash_forward_call(low, q, k, v, col, row):
    dealers, rows, width = q.shape
    rounds = 256 // dealers
    heads = width // HD
    part = lambda w: pl.BlockSpec((dealers, rounds, w), lambda i, low: (0, i, 0))
    whole = lambda shape: pl.BlockSpec(shape, lambda i, low: (0, 0, 0))
    return pl.pallas_call(
        flash_forward,
        name="flash_forward",
        grid_spec=pltpu.PrefetchScalarGridSpec(
            num_scalar_prefetch=1,
            grid=(rows // rounds,),
            in_specs=[part(width), part(2), whole(row.shape), whole(k.shape), whole(v.shape)],
            out_specs=[part(width), part(width), part(heads)],
        ),
        out_shape=[
            jax.ShapeDtypeStruct(q.shape, BF),
            jax.ShapeDtypeStruct(q.shape, F32),
            jax.ShapeDtypeStruct((dealers, rows, heads), F32),
        ],
        compiler_params=pltpu.CompilerParams(vmem_limit_bytes=48 * 2**20),
    )(low, q, col, row, k, v)


def flash_backward(
    low_ref, q_ref, da_ref, of_ref, lse_ref, col_ref, row_ref, k_ref, v_ref, cos_ref, sin_ref,
    d_ref, dk_acc, dv_acc,
):
    block = pl.program_id(0)
    dealers, rounds, width = q_ref.shape
    size = dealers * rounds
    heads = width // HD
    blocks = pl.num_programs(0)

    @pl.when(block == 0)
    def clear():
        dk_acc[...] = jnp.zeros_like(dk_acc)
        dv_acc[...] = jnp.zeros_like(dv_acc)

    q = q_ref[...].reshape(size, width)
    da = da_ref[...].reshape(size, width)
    col = col_ref[...].reshape(size, 2)
    lse = lse_ref[...].reshape(size, heads)
    top, bottom = col[:, 0:1], col[:, 1:2]
    head_of = lax.broadcasted_iota(jnp.int32, (size, width), 1) // HD
    product = da.astype(F32) * of_ref[...].reshape(size, width)
    q_of, da_of, delta = [], [], []
    for h in range(heads):
        q_of.append(jnp.where(head_of == h, q, jnp.zeros_like(q)))
        da_of.append(jnp.where(head_of == h, da, jnp.zeros_like(da)))
        delta.append(jnp.sum(jnp.where(head_of == h, product, 0.0), axis=1, keepdims=True))
    q_turned = q.astype(F32).T.astype(BF)
    da_turned = da.astype(F32).T.astype(BF)

    def step(at, dq):
        window = pl.ds(pl.multiple_of(at * rounds, rounds), rounds)
        k = k_ref[:, window, :].reshape(size, width)
        v = v_ref[:, window, :].reshape(size, width)
        order = row_ref[at]
        allowed = (order <= top) & (order >= bottom)
        for h in range(heads):
            scores = jnp.where(allowed, dot_nt(q_of[h], k), -1e30)
            probs = jnp.exp(scores - lse[:, h : h + 1])
            dprobs = dot_nt(da_of[h], v)
            dscores = (probs * (dprobs - delta[h])).astype(BF)
            own = slice(h * HD, (h + 1) * HD)
            dv_acc[at, own, :] += dot_nn(da_turned[own], probs.astype(BF))
            dk_acc[at, own, :] += dot_nn(q_turned[own], dscores)
            dq = jnp.where(head_of == h, dq + dot_nn(dscores, k), dq)
        return dq

    dq = lax.fori_loop(low_ref[block], block + 1, step, jnp.zeros((size, width), F32))

    def revert(grads, at):
        window = pl.ds(pl.multiple_of(at * rounds, rounds), rounds)
        cosine = wide(cos_ref[:, window, :].reshape(size, LANES), width)
        sine = wide(sin_ref[:, window, :].reshape(size, LANES), width)
        return grads * cosine - partner(grads) * sine

    def put(at, part, grads):
        window = pl.ds(pl.multiple_of(at * rounds, rounds), rounds)
        d_ref[:, window, part * width : (part + 1) * width] = grads.astype(BF).reshape(
            dealers, rounds, width
        )

    put(block, 0, revert(dq * 0.125, block))

    @pl.when(block == blocks - 1)
    def finish():
        def each(at, carry):
            put(at, 1, revert(dk_acc[at].T, at))
            put(at, 2, dv_acc[at].T)
            return carry

        lax.fori_loop(0, blocks, each, 0)


def flash_backward_call(low, q, da, of, lse, col, row, k, v, cosine, sine):
    dealers, rows, width = q.shape
    rounds = 256 // dealers
    heads = width // HD
    part = lambda w: pl.BlockSpec((dealers, rounds, w), lambda i, low: (0, i, 0))
    whole = lambda shape: pl.BlockSpec(shape, lambda i, low: (0, 0, 0))
    blocks = rows // rounds
    return pl.pallas_call(
        flash_backward,
        name="flash_backward",
        grid_spec=pltpu.PrefetchScalarGridSpec(
            num_scalar_prefetch=1,
            grid=(blocks,),
            in_specs=[
                part(width), part(width), part(width), part(heads), part(2), whole(row.shape),
                whole(k.shape), whole(v.shape), whole(cosine.shape), whole(sine.shape),
            ],
            out_specs=whole((dealers, rows, 3 * width)),
            scratch_shapes=[pltpu.VMEM((blocks, width, 256), F32)] * 2,
        ),
        out_shape=jax.ShapeDtypeStruct((dealers, rows, 3 * width), BF),
        compiler_params=pltpu.CompilerParams(vmem_limit_bytes=48 * 2**20),
    )(low, q, da, of, lse, col, row, k, v, cosine, sine)


def body(dealers, shards, *args):
    (
        tokens, cotangent, seq_lengths, token_order, ln_gain, ln_bias, w_qkv, q_bias, k_bias,
        v_bias, w_out, out_bias, w_up, up_bias, w_down, down_bias,
    ) = args
    rows = tokens.shape[1]
    count = dealers * rows
    me = lax.axis_index("ctx")
    shard = lax.axis_index("fsdp")
    width = D // dealers
    spread = HEADS % (dealers * shards) == 0
    head_piece = width // shards if spread else width
    unit_piece = FF // (dealers * shards)

    def over_ctx(value):
        return lax.all_gather(value, "ctx", axis=0, tiled=False)

    def over_fsdp(value):
        return lax.all_gather(value, "fsdp", axis=0, tiled=True)

    x_all = over_ctx(tokens[0])

    order_rows = token_order.reshape(dealers, rows)
    rank = order_rows // dealers
    places = jnp.arange(rows, dtype=jnp.int32)
    order = jnp.sum(
        jnp.where(rank[:, None, :] == places[None, :, None], order_rows[:, None, :], 0), axis=2
    )
    bounds = jnp.cumsum(seq_lengths[0])
    starts = bounds - seq_lengths[0]
    inside = (order[..., None] >= starts) & (order[..., None] < bounds)
    start = jnp.sum(jnp.where(inside, starts, 0), axis=-1)
    position = order - start
    frequency = 10000.0 ** (-jnp.arange(ROT // 2, dtype=F32) * 2.0 / ROT)
    zeros = jnp.zeros((HD - ROT,), F32)
    lane_frequency = jnp.tile(jnp.concatenate([frequency, frequency, zeros]), LANES // HD)
    sign = jnp.concatenate([-jnp.ones((ROT // 2,), F32), jnp.ones((ROT // 2,), F32), zeros])
    angles = position.astype(F32)[..., None] * lane_frequency
    cosine = jnp.cos(angles)
    sine = jnp.sin(angles) * jnp.tile(sign, LANES // HD)
    rounds = 256 // dealers
    blocks = rows // rounds
    row = order.reshape(dealers, blocks, rounds).transpose(1, 0, 2).reshape(blocks, 1, 256)
    col = jnp.stack([order, start], axis=-1)
    low = jnp.min(start.reshape(dealers, blocks, rounds), axis=(0, 2)) // 256

    own_rank = lax.dynamic_index_in_dim(rank, me, 0, keepdims=False)
    pick = (own_rank[None, :] == places[:, None]).astype(BF)
    dy_sorted = dot_nn(pick, cotangent[0]).astype(BF)
    dy_all = over_ctx(dy_sorted).reshape(count, D)

    small = jnp.concatenate(
        [ln_gain, ln_bias, q_bias, k_bias, v_bias, out_bias, up_bias, down_bias]
    )
    small = lax.all_gather(small, "fsdp", axis=0, tiled=False).astype(F32)
    vectors, at = [], 0
    for part in (ln_gain, ln_bias, q_bias, k_bias, v_bias, out_bias, up_bias, down_bias):
        vectors.append(small[:, at : at + part.shape[0]].reshape(shards * part.shape[0]))
        at += part.shape[0]
    gain, shift, qb, kb, vb, ob, ub, db = vectors
    kb = jnp.pad(kb.reshape(HEADS, ROT), ((0, 0), (0, HD - ROT))).reshape(D)

    def own_heads(matrix, axis):
        if not spread:
            return lax.dynamic_slice_in_dim(matrix, me * width, width, axis)
        return jnp.concatenate(
            [
                lax.dynamic_slice_in_dim(
                    matrix, j * (D // shards) + me * head_piece, head_piece, axis
                )
                for j in range(shards)
            ],
            axis=axis,
        )

    def own_units(matrix, axis):
        return jnp.concatenate(
            [
                lax.dynamic_slice_in_dim(
                    matrix, j * (FF // shards) + me * unit_piece, unit_piece, axis
                )
                for j in range(shards)
            ],
            axis=axis,
        )

    qkv_own = jnp.concatenate(
        [own_heads(w_qkv[:, i * D : (i + 1) * D], 1) for i in range(3)], axis=1
    )
    qkv_full = over_fsdp(qkv_own)
    bias_own = jnp.concatenate([own_heads(b, 0) for b in (qb, kb, vb)])
    up_full = over_fsdp(own_units(w_up, 1))
    up_bias_own = own_units(ub, 0)
    down_own = lax.dynamic_slice_in_dim(w_down, me * unit_piece, unit_piece, 0)
    if spread:
        out_own = lax.dynamic_slice_in_dim(w_out, me * head_piece, head_piece, 0)
        both = over_fsdp(jnp.concatenate([out_own, down_own], axis=0))
        both = both.reshape(shards, head_piece + unit_piece, D)
        out_full = both[:, :head_piece].reshape(width, D)
        down_full = both[:, head_piece:].reshape(FF // dealers, D)
    else:
        per = D // shards // width
        mine = lax.dynamic_slice_in_dim(w_out, (me % per) * width, width, 0)
        mine = jnp.where(me // per == shard, mine, jnp.zeros_like(mine))
        out_full = lax.psum(mine, "fsdp")
        down_full = over_fsdp(down_own)

    normed, q, k, v = qkv_call(
        x_all, rank[:, None, :], gain[None], shift[None], qkv_full, bias_own[None], cosine, sine
    )
    normed = normed.reshape(count, D)
    attn, attn_f, lse = flash_forward_call(low, q, k, v, col, row)
    attn = attn.reshape(count, width)
    hidden = dot_nn(normed, up_full) + up_bias_own[None]
    act, gelu_back = jax.vjp(lambda inner: jax.nn.gelu(inner, approximate=True), hidden)
    act = act.astype(BF)
    out_part = (dot_nn(attn, out_full) + dot_nn(act, down_full)).astype(BF)

    d_out = dot_tn(attn, dy_all).astype(BF)
    d_down = dot_tn(act, dy_all).astype(BF)
    scatter = functools.partial(lax.psum_scatter, scatter_dimension=0, tiled=True)
    if spread:
        d_both = jnp.concatenate(
            [d_out.reshape(shards, head_piece, D), d_down.reshape(shards, unit_piece, D)], axis=1
        )
        d_both = over_ctx(scatter(d_both.reshape(shards * (head_piece + unit_piece), D), "fsdp"))
        d_out = d_both[:, :head_piece].astype(F32).reshape(dealers * head_piece, D)
        d_down = d_both[:, head_piece:].astype(F32).reshape(dealers * unit_piece, D)
    else:
        d_out = lax.psum(d_out, "fsdp")
        d_out = jnp.where(me // per == shard, d_out, jnp.zeros_like(d_out))
        spot = jnp.zeros((per * width, D), BF)
        d_out = lax.dynamic_update_slice_in_dim(spot, d_out, (me % per) * width, 0)
        d_out = lax.psum(d_out, "ctx").astype(F32)
        d_down = over_ctx(scatter(d_down, "fsdp")).astype(F32).reshape(dealers * unit_piece, D)
    d_act = dot_nt(dy_all, down_full)
    d_hidden = gelu_back(d_act)[0].astype(BF)
    d_up = over_ctx(scatter(dot_tn(normed, d_hidden).astype(BF), "fsdp"))
    d_up = d_up.reshape(dealers, D // shards, shards, unit_piece).transpose(1, 2, 0, 3)
    d_up = d_up.astype(F32).reshape(D // shards, FF)

    d_attn = dot_nt(dy_all, out_full).astype(BF).reshape(dealers, rows, width)
    d_qkv = flash_backward_call(low, q, d_attn, attn_f, lse, col, row, k, v, cosine, sine)
    d_qkv = d_qkv.reshape(count, 3 * width)
    d_normed = (dot_nt(d_qkv, qkv_full) + dot_nt(d_hidden, up_full)).astype(BF)
    d_w_qkv = over_ctx(scatter(dot_tn(normed, d_qkv).astype(BF), "fsdp"))
    if spread:
        d_w_qkv = d_w_qkv.reshape(dealers, D // shards, 3, shards, head_piece)
        d_w_qkv = d_w_qkv.transpose(1, 2, 3, 0, 4)
    else:
        d_w_qkv = d_w_qkv.reshape(dealers, D // shards, 3, width).transpose(1, 2, 0, 3)
    d_w_qkv = d_w_qkv.astype(F32).reshape(D // shards, 3 * D)

    out_own = dot_tn(pick, scatter(out_part, "ctx"))
    x = tokens[0].astype(F32)
    out_act = (x + out_own + (ob + db)[None]).astype(BF)
    dn = dot_tn(pick, scatter(d_normed, "ctx"))
    mean = jnp.mean(x, axis=-1, keepdims=True)
    centered = x - mean
    variance = jnp.mean(centered * centered, axis=-1, keepdims=True)
    inverse = lax.rsqrt(variance + 1e-05)
    standard = centered * inverse
    grad = dn * gain[None]
    d_tokens = cotangent[0].astype(F32) + inverse * (
        grad
        - jnp.mean(grad, axis=-1, keepdims=True)
        - standard * jnp.mean(grad * standard, axis=-1, keepdims=True)
    )

    def place(vector, pieces):
        piece = vector.shape[0] // pieces
        mine = (jnp.arange(dealers) == me)[None, :, None]
        vector = vector.reshape(pieces, 1, piece)
        return jnp.where(mine, vector, 0.0).reshape(pieces * dealers * piece)

    head_pieces = shards if spread else 1
    sums = jnp.concatenate(
        [
            jnp.sum(dn * standard, axis=0),
            jnp.sum(dn, axis=0),
            jnp.sum(cotangent[0].astype(F32), axis=0),
            place(jnp.sum(d_qkv.astype(F32), axis=0), 3 * head_pieces),
            place(jnp.sum(d_hidden.astype(F32), axis=0), shards),
        ]
    )
    sums = lax.psum(sums, ("ctx", "fsdp"))

    def mine(vector):
        piece = vector.shape[0] // shards
        return lax.dynamic_slice_in_dim(vector, shard * piece, piece, 0)

    gain_sum, shift_sum, dy_sum, qkv_sum, up_sum = (
        sums[:D], sums[D : 2 * D], sums[2 * D : 3 * D], sums[3 * D : 6 * D], sums[6 * D :],
    )
    k_sum = qkv_sum[D : 2 * D].reshape(HEADS, HD)[:, :ROT].reshape(HEADS * ROT)
    return (
        out_act[None], d_tokens[None], mine(gain_sum), mine(shift_sum),
        d_w_qkv, mine(qkv_sum[:D]), mine(k_sum), mine(qkv_sum[2 * D :]),
        d_out, mine(dy_sum), d_up, mine(up_sum), d_down, mine(dy_sum),
    )


def solution(mesh):
    row, vector = P("fsdp", None), P("fsdp")
    split = P("fsdp", "ctx", None)
    in_specs = (
        split, split, row, row, vector, vector, row, vector,
        vector, vector, row, vector, row, vector, row, vector,
    )
    out_specs = (
        split, split, vector, vector, row, vector, vector, vector,
        row, vector, row, vector, row, vector,
    )
    step = functools.partial(body, mesh.shape["ctx"], mesh.shape["fsdp"])
    return jax.shard_map(
        step, mesh=mesh, in_specs=in_specs, out_specs=out_specs, check_vma=False
    )
```

```python
import functools

import jax
import jax.numpy as jnp
import numpy as np
from jax import lax
from jax.experimental import pallas as pl
from jax.experimental.pallas import tpu as pltpu
from jax.sharding import PartitionSpec as P

D = 2048
HEADS = 32
HD = 64
ROT = 32
FF = 8192
LANES = 128
VMEM_BYTES = 56 * 2**20
BF = jnp.bfloat16
F32 = jnp.float32


def dot_nn(a, b):
    return lax.dot_general(a, b, (((1,), (0,)), ((), ())), preferred_element_type=F32)


def dot_nt(a, b):
    return lax.dot_general(a, b, (((1,), (1,)), ((), ())), preferred_element_type=F32)


def dot_tn(a, b):
    return lax.dot_general(a, b, (((0,), (0,)), ((), ())), preferred_element_type=F32)


def wide(table, width):
    return jnp.concatenate([table] * (width // LANES), axis=1)


def partner(values):
    width = values.shape[1]
    lane = lax.broadcasted_iota(jnp.int32, values.shape, 1) % HD
    half = ROT // 2
    return jnp.where(
        lane < half, pltpu.roll(values, width - half, 1), pltpu.roll(values, half, 1)
    )


def sort_norm_project(
    x_ref, rank_ref, gain_ref, shift_ref, w_ref, bias_ref, cos_ref, sin_ref,
    normed_ref, q_ref, k_ref, v_ref,
):
    rows = x_ref.shape[1]
    width = q_ref.shape[2]
    place = lax.broadcasted_iota(jnp.int32, (rows, rows), 0)
    pick = jnp.where(rank_ref[0] == place, 1.0, 0.0).astype(BF)
    x = dot_nn(pick, x_ref[0])
    mean = jnp.mean(x, axis=1, keepdims=True)
    centered = x - mean
    variance = jnp.mean(centered * centered, axis=1, keepdims=True)
    normed = (centered * lax.rsqrt(variance + 1e-05) * gain_ref[...] + shift_ref[...]).astype(BF)
    normed_ref[0] = normed
    projected = dot_nn(normed, w_ref[...]) + bias_ref[...]
    cosine, sine = wide(cos_ref[0], width), wide(sin_ref[0], width)
    q = projected[:, :width]
    k = projected[:, width : 2 * width]
    q = (q * cosine + partner(q) * sine).astype(BF)
    q_ref[0] = (q.astype(F32) * 0.125).astype(BF)
    k_ref[0] = (k * cosine + partner(k) * sine).astype(BF)
    v_ref[0] = projected[:, 2 * width :].astype(BF)


def qkv_call(x_all, rank, gain, shift, weights, bias, cosine, sine):
    dealers, rows, _ = x_all.shape
    width = weights.shape[1] // 3
    whole = lambda *shape: pl.BlockSpec(shape, lambda i: (0,) * len(shape))
    each = lambda *shape: pl.BlockSpec((1,) + shape, lambda i: (i, 0, 0))
    out = lambda w: jax.ShapeDtypeStruct((dealers, rows, w), BF)
    return pl.pallas_call(
        sort_norm_project,
        name="sort_norm_project",
        grid=(dealers,),
        in_specs=[
            each(rows, D), each(1, rows), whole(1, D), whole(1, D),
            whole(D, 3 * width), whole(1, 3 * width), each(rows, LANES), each(rows, LANES),
        ],
        out_specs=[each(rows, D)] + [each(rows, width)] * 3,
        out_shape=[out(D), out(width), out(width), out(width)],
        compiler_params=pltpu.CompilerParams(vmem_limit_bytes=VMEM_BYTES),
    )(x_all, rank, gain, shift, weights, bias, cosine, sine)


def flash_forward(low_ref, q_ref, col_ref, row_ref, k_ref, v_ref, o_ref, of_ref, lse_ref):
    block = pl.program_id(0)
    dealers, rounds, width = q_ref.shape
    size = dealers * rounds
    heads = width // HD
    q = q_ref[...].reshape(size, width)
    col = col_ref[...].reshape(size, 2)
    top, bottom = col[:, 0:1], col[:, 1:2]
    head_of = lax.broadcasted_iota(jnp.int32, (size, width), 1) // HD
    q_of = [jnp.where(head_of == h, q, jnp.zeros_like(q)) for h in range(heads)]

    def step(j, carry):
        at = block - j
        running, total, mixed = carry
        window = pl.ds(pl.multiple_of(at * rounds, rounds), rounds)
        k = k_ref[:, window, :].reshape(size, width)
        v = v_ref[:, window, :].reshape(size, width)
        order = row_ref[at]
        allowed = (order <= top) & (order >= bottom)
        new_running, new_total = [], []
        for h in range(heads):
            scores = jnp.where(allowed, dot_nt(q_of[h], k), -1e30)
            peak = jnp.maximum(running[h], jnp.max(scores, axis=1, keepdims=True))
            probs = jnp.exp(scores - peak)
            scale = jnp.exp(running[h] - peak)
            new_running.append(peak)
            new_total.append(total[h] * scale + jnp.sum(probs, axis=1, keepdims=True))
            mixed = jnp.where(head_of == h, mixed * scale + dot_nn(probs.astype(BF), v), mixed)
        return (new_running, new_total, mixed)

    start = (
        [jnp.full((size, 1), -1e30, F32)] * heads,
        [jnp.zeros((size, 1), F32)] * heads,
        jnp.zeros((size, width), F32),
    )
    running, total, mixed = lax.fori_loop(0, block - low_ref[block] + 1, step, start)
    weight = jnp.zeros((size, width), F32)
    for h in range(heads):
        weight = jnp.where(head_of == h, 1.0 / total[h], weight)
    mixed = mixed * weight
    o_ref[...] = mixed.astype(BF).reshape(dealers, rounds, width)
    of_ref[...] = mixed.reshape(dealers, rounds, width)
    lse = [running[h] + jnp.log(total[h]) for h in range(heads)]
    lse_ref[...] = jnp.concatenate(lse, axis=1).reshape(dealers, rounds, heads)


def flash_forward_call(low, q, k, v, col, row, after=()):
    dealers, rows, width = q.shape
    rounds = 256 // dealers
    heads = width // HD
    part = lambda w: pl.BlockSpec((dealers, rounds, w), lambda i, low: (0, i, 0))
    whole = lambda shape: pl.BlockSpec(shape, lambda i, low: (0, 0, 0))
    return pl.pallas_call(
        behind(flash_forward, len(after), 1),
        name="flash_forward",
        cost_estimate=takes(21),
        grid_spec=pltpu.PrefetchScalarGridSpec(
            num_scalar_prefetch=1,
            grid=(rows // rounds,),
            in_specs=[HBM] * len(after)
            + [part(width), part(2), whole(row.shape), whole(k.shape), whole(v.shape)],
            out_specs=[part(width), part(width), part(heads)],
        ),
        out_shape=[
            jax.ShapeDtypeStruct(q.shape, BF),
            jax.ShapeDtypeStruct(q.shape, F32),
            jax.ShapeDtypeStruct((dealers, rows, heads), F32),
        ],
        compiler_params=pltpu.CompilerParams(vmem_limit_bytes=VMEM_BYTES),
    )(low, *after, q, col, row, k, v)


def flash_backward(
    low_ref, q_ref, da_ref, of_ref, lse_ref, col_ref, row_ref, k_ref, v_ref, cos_ref, sin_ref,
    d_ref, dk_acc, dv_acc,
):
    block = pl.program_id(0)
    dealers, rounds, width = q_ref.shape
    size = dealers * rounds
    heads = width // HD
    blocks = pl.num_programs(0)

    @pl.when(block == 0)
    def clear():
        dk_acc[...] = jnp.zeros_like(dk_acc)
        dv_acc[...] = jnp.zeros_like(dv_acc)

    q = q_ref[...].reshape(size, width)
    da = da_ref[...].reshape(size, width)
    col = col_ref[...].reshape(size, 2)
    lse = lse_ref[...].reshape(size, heads)
    top, bottom = col[:, 0:1], col[:, 1:2]
    head_of = lax.broadcasted_iota(jnp.int32, (size, width), 1) // HD
    product = da.astype(F32) * of_ref[...].reshape(size, width)
    q_of, da_of, delta = [], [], []
    for h in range(heads):
        q_of.append(jnp.where(head_of == h, q, jnp.zeros_like(q)))
        da_of.append(jnp.where(head_of == h, da, jnp.zeros_like(da)))
        delta.append(jnp.sum(jnp.where(head_of == h, product, 0.0), axis=1, keepdims=True))
    q_turned = q.astype(F32).T.astype(BF)
    da_turned = da.astype(F32).T.astype(BF)

    def step(at, dq):
        window = pl.ds(pl.multiple_of(at * rounds, rounds), rounds)
        k = k_ref[:, window, :].reshape(size, width)
        v = v_ref[:, window, :].reshape(size, width)
        order = row_ref[at]
        allowed = (order <= top) & (order >= bottom)
        for h in range(heads):
            scores = jnp.where(allowed, dot_nt(q_of[h], k), -1e30)
            probs = jnp.exp(scores - lse[:, h : h + 1])
            dprobs = dot_nt(da_of[h], v)
            dscores = (probs * (dprobs - delta[h])).astype(BF)
            own = slice(h * HD, (h + 1) * HD)
            dv_acc[at, own, :] += dot_nn(da_turned[own], probs.astype(BF))
            dk_acc[at, own, :] += dot_nn(q_turned[own], dscores)
            dq = jnp.where(head_of == h, dq + dot_nn(dscores, k), dq)
        return dq

    dq = lax.fori_loop(low_ref[block], block + 1, step, jnp.zeros((size, width), F32))

    def revert(grads, at):
        window = pl.ds(pl.multiple_of(at * rounds, rounds), rounds)
        cosine = wide(cos_ref[:, window, :].reshape(size, LANES), width)
        sine = wide(sin_ref[:, window, :].reshape(size, LANES), width)
        return grads * cosine - partner(grads) * sine

    def put(at, part, grads):
        window = pl.ds(pl.multiple_of(at * rounds, rounds), rounds)
        d_ref[:, window, part * width : (part + 1) * width] = grads.astype(BF).reshape(
            dealers, rounds, width
        )

    put(block, 0, revert(dq * 0.125, block))

    @pl.when(block == blocks - 1)
    def finish():
        def each(at, carry):
            put(at, 1, revert(dk_acc[at].T, at))
            put(at, 2, dv_acc[at].T)
            return carry

        lax.fori_loop(0, blocks, each, 0)


class CarriedBackward:
    def __init__(self, operands, d_ref, dk_acc, dv_acc):
        self.q, self.da, self.of, self.lse, self.col, self.row = operands[:6]
        self.k, self.v, self.cos, self.sin = operands[6:]
        self.d_ref, self.dk_acc, self.dv_acc = d_ref, dk_acc, dv_acc
        self.dealers, rows, self.width = self.q.shape
        self.rounds = 256 // self.dealers
        self.blocks = rows // self.rounds
        self.reach = self.dealers * rows // 2 // 256

    def window(self, at):
        return pl.ds(pl.multiple_of(at * self.rounds, self.rounds), self.rounds)

    def load(self, ref, at):
        return ref[:, self.window(at), :].reshape(256, ref.shape[2])

    def put(self, at, part, grads):
        span = slice(part * self.width, (part + 1) * self.width)
        grads = grads.astype(BF).reshape(self.dealers, self.rounds, self.width)
        self.d_ref[:, self.window(at), span] = grads

    def revert(self, grads, at):
        cosine = wide(self.load(self.cos, at), self.width)
        sine = wide(self.load(self.sin, at), self.width)
        return grads * cosine - partner(grads) * sine

    def clear(self):
        self.dk_acc[...] = jnp.zeros_like(self.dk_acc)
        self.dv_acc[...] = jnp.zeros_like(self.dv_acc)

    def block(self, block):
        size, heads = 256, self.width // HD
        q, da = self.load(self.q, block), self.load(self.da, block)
        col, lse = self.load(self.col, block), self.load(self.lse, block)
        top, bottom = col[:, 0:1], col[:, 1:2]
        head_of = lax.broadcasted_iota(jnp.int32, (size, self.width), 1) // HD
        product = da.astype(F32) * self.load(self.of, block)
        q_of, da_of, delta = [], [], []
        for h in range(heads):
            q_of.append(jnp.where(head_of == h, q, jnp.zeros_like(q)))
            da_of.append(jnp.where(head_of == h, da, jnp.zeros_like(da)))
            delta.append(jnp.sum(jnp.where(head_of == h, product, 0.0), axis=1, keepdims=True))
        q_turned = q.astype(F32).T.astype(BF)
        da_turned = da.astype(F32).T.astype(BF)

        def step(at, dq):
            k, v = self.load(self.k, at), self.load(self.v, at)
            order = self.row[at]
            allowed = (order <= top) & (order >= bottom)
            for h in range(heads):
                scores = jnp.where(allowed, dot_nt(q_of[h], k), -1e30)
                probs = jnp.exp(scores - lse[:, h : h + 1])
                dprobs = dot_nt(da_of[h], v)
                dscores = (probs * (dprobs - delta[h])).astype(BF)
                own = slice(h * HD, (h + 1) * HD)
                self.dv_acc[at, own, :] += dot_nn(da_turned[own], probs.astype(BF))
                self.dk_acc[at, own, :] += dot_nn(q_turned[own], dscores)
                dq = jnp.where(head_of == h, dq + dot_nn(dscores, k), dq)
            return dq

        lowest = jnp.maximum(block - self.reach, 0)
        dq = lax.fori_loop(lowest, block + 1, step, jnp.zeros((size, self.width), F32))
        self.put(block, 0, self.revert(dq * 0.125, block))

    def run(self, first, last):
        lax.fori_loop(first, last, lambda at, carry: (self.block(at), carry)[1], 0)

    def finish(self):
        def each(at, carry):
            self.put(at, 1, self.revert(self.dk_acc[at].T, at))
            self.put(at, 2, self.dv_acc[at].T)
            return carry

        lax.fori_loop(0, self.blocks, each, 0)


def flash_backward_call(low, q, da, of, lse, col, row, k, v, cosine, sine, after=()):
    dealers, rows, width = q.shape
    rounds = 256 // dealers
    heads = width // HD
    part = lambda w: pl.BlockSpec((dealers, rounds, w), lambda i, low: (0, i, 0))
    whole = lambda shape: pl.BlockSpec(shape, lambda i, low: (0, 0, 0))
    blocks = rows // rounds
    return pl.pallas_call(
        behind(flash_backward, len(after), 1),
        name="flash_backward",
        cost_estimate=takes(31),
        grid_spec=pltpu.PrefetchScalarGridSpec(
            num_scalar_prefetch=1,
            grid=(blocks,),
            in_specs=[HBM] * len(after)
            + [
                part(width), part(width), part(width), part(heads), part(2), whole(row.shape),
                whole(k.shape), whole(v.shape), whole(cosine.shape), whole(sine.shape),
            ],
            out_specs=whole((dealers, rows, 3 * width)),
            scratch_shapes=[pltpu.VMEM((blocks, width, 256), F32)] * 2,
        ),
        out_shape=jax.ShapeDtypeStruct((dealers, rows, 3 * width), BF),
        compiler_params=pltpu.CompilerParams(vmem_limit_bytes=VMEM_BYTES),
    )(low, *after, q, da, of, lse, col, row, k, v, cosine, sine)


MESH = pl.DeviceIdType.MESH
HBM = pl.BlockSpec(memory_space=pltpu.HBM)


def behind(kernel, waits, scalars=0):
    def run(*refs):
        kernel(*refs[:scalars], *refs[scalars + waits :])

    return run


def tie(value, *waits):
    def nothing(*refs):
        del refs

    return pl.pallas_call(
        nothing,
        name="tie",
        in_specs=[HBM] * (1 + len(waits)),
        out_specs=HBM,
        out_shape=jax.ShapeDtypeStruct(value.shape, value.dtype),
        input_output_aliases={0: 0},
    )(value, *waits)


def takes(microseconds):
    return pl.CostEstimate(
        flops=0, bytes_accessed=int(microseconds * 3.69e3), transcendentals=0
    )


def plane_neighbours(shard):
    return shard + 1 - 2 * (shard % 2), (shard + 2) % 4, 3 - shard


class PlaneGather:
    def __init__(self, out_ref, send_sem, recv_sem, base):
        self.out, self.send_sem, self.recv_sem, self.base = out_ref, send_sem, recv_sem, base
        self.shard = lax.axis_index("fsdp")
        self.half = out_ref.shape[1] // 2

    def copy(self, k, src, dst):
        x, y, _ = plane_neighbours(self.shard)
        return pltpu.make_async_remote_copy(
            src_ref=src,
            dst_ref=dst,
            send_sem=self.send_sem.at[self.base + k],
            recv_sem=self.recv_sem.at[self.base + k],
            device_id={"fsdp": x if k % 2 == 0 else y},
            device_id_type=MESH,
        )

    def part(self, slot, k):
        return self.out.at[slot, pl.ds((k % 2) * self.half, self.half)]

    def first(self, src):
        for k in range(2):
            self.copy(k, src, self.out.at[self.shard]).start()

    def forward(self):
        x, y, _ = plane_neighbours(self.shard)
        for k in range(2):
            self.copy(k, self.out.at[x], self.out.at[(x, y)[k]]).wait_recv()
        for k in range(2):
            piece = self.part((y, x)[k], k)
            self.copy(2 + k, piece, piece).start()

    def finish(self, src):
        x, y, across = plane_neighbours(self.shard)
        for k in range(2):
            self.copy(k, src, self.out.at[self.shard]).wait_send()
            piece = self.part((y, x)[k], k)
            self.copy(2 + k, piece, piece).wait_send()
            self.copy(2 + k, piece, self.part(across, k)).wait_recv()


def rows_of_orders(col_ref, row_ref):
    rounds = 256 // col_ref.shape[0]
    for at in range(row_ref.shape[0]):
        order = col_ref[:, at * rounds : (at + 1) * rounds, :].reshape(256, 2)[:, 0:1]
        order = jnp.broadcast_to(order.astype(F32), (256, LANES)).T[0:1]
        row_ref[at] = order.astype(jnp.int32)


class CarriedForward:
    def __init__(self, q_ref, k_ref, v_ref, col_ref, row_ref, o_ref, of_ref, lse_ref):
        self.q, self.k, self.v, self.col, self.row = q_ref, k_ref, v_ref, col_ref, row_ref
        self.o, self.of, self.lse = o_ref, of_ref, lse_ref
        self.dealers, rows, self.width = q_ref.shape
        self.rounds = 256 // self.dealers
        self.blocks = rows // self.rounds
        self.reach = self.dealers * rows // 2 // 256

    def window(self, at):
        return pl.ds(pl.multiple_of(at * self.rounds, self.rounds), self.rounds)

    def load(self, ref, at):
        return ref[:, self.window(at), :].reshape(256, ref.shape[2])

    def save(self, ref, at, value):
        ref[:, self.window(at), :] = value.reshape(self.dealers, self.rounds, ref.shape[2])

    def block(self, block):
        size, heads = 256, self.width // HD
        q, col = self.load(self.q, block), self.load(self.col, block)
        top, bottom = col[:, 0:1], col[:, 1:2]
        head_of = lax.broadcasted_iota(jnp.int32, (size, self.width), 1) // HD
        q_of = [jnp.where(head_of == h, q, jnp.zeros_like(q)) for h in range(heads)]

        def step(j, carry):
            at = block - j
            running, total, mixed = carry
            k, v = self.load(self.k, at), self.load(self.v, at)
            order = self.row[at]
            allowed = (order <= top) & (order >= bottom)
            new_running, new_total = [], []
            for h in range(heads):
                scores = jnp.where(allowed, dot_nt(q_of[h], k), -1e30)
                peak = jnp.maximum(running[h], jnp.max(scores, axis=1, keepdims=True))
                probs = jnp.exp(scores - peak)
                scale = jnp.exp(running[h] - peak)
                new_running.append(peak)
                new_total.append(total[h] * scale + jnp.sum(probs, axis=1, keepdims=True))
                mixed = jnp.where(head_of == h, mixed * scale + dot_nn(probs.astype(BF), v), mixed)
            return (new_running, new_total, mixed)

        start = (
            [jnp.full((size, 1), -1e30, F32)] * heads,
            [jnp.zeros((size, 1), F32)] * heads,
            jnp.zeros((size, self.width), F32),
        )
        steps = jnp.minimum(block, self.reach) + 1
        running, total, mixed = lax.fori_loop(0, steps, step, start)
        weight = jnp.zeros((size, self.width), F32)
        for h in range(heads):
            weight = jnp.where(head_of == h, 1.0 / total[h], weight)
        mixed = mixed * weight
        self.save(self.o, block, mixed.astype(BF))
        self.save(self.of, block, mixed)
        lse = [running[h] + jnp.log(total[h]) for h in range(heads)]
        self.save(self.lse, block, jnp.concatenate(lse, axis=1))

    def run(self, first, last):
        lax.fori_loop(first, last, lambda at, carry: (self.block(at), carry)[1], 0)


class LineSum:
    def __init__(self, turned, operands, out_ref, buffers):
        self.turned, self.out_ref = turned, out_ref
        self.a, self.b, self.wa, self.wb = operands
        self.mine, self.both, self.arrived, self.passing = buffers[:4]
        self.pair_send, self.pair_recv, self.line_send, self.line_recv = buffers[4:]
        self.me = lax.axis_index("ctx")
        self.chips, self.rows = self.mine.shape[:2]
        self.chip, self.core = self.me // 2, self.me % 2
        self.side = (2 * self.chip) // self.chips
        self.first = 0

    def goal(self, j):
        return (1 - self.side) * (self.chips - 1 - j) + self.side * j

    def products(self, j):
        goal, rows, tile = self.goal(j), self.rows, 1024
        pair = pl.ds(2 * goal, 2)
        a = self.a[pair].reshape(2 * rows, self.a.shape[2])
        b = self.b[pair].reshape(2 * rows, self.b.shape[2])

        def one(t, carry):
            span = pl.ds(pl.multiple_of(t * tile, tile), tile)
            if self.turned:
                value = dot_nt(a, self.wa[span, :]) + dot_nt(b, self.wb[span, :])
            else:
                value = dot_nn(a, self.wa[:, span]) + dot_nn(b, self.wb[:, span])
            self.both[j % 2, :, :, span] = value.astype(BF).reshape(2, rows, tile)
            return carry

        lax.fori_loop(0, D // tile, one, 0)

    def to_pair(self, j):
        return pltpu.make_async_remote_copy(
            src_ref=self.both.at[j % 2, 1 - self.core], dst_ref=self.arrived.at[self.goal(j)],
            send_sem=self.pair_send.at[j], recv_sem=self.pair_recv.at[j],
            device_id={"ctx": self.me + 1 - 2 * self.core}, device_id_type=MESH,
        )

    def add(self, goal, base, extra):
        def one(t, carry):
            span = pl.ds(pl.multiple_of(t * 16, 16), 16)
            value = base[span, :].astype(F32) + extra[span, :].astype(F32)
            self.mine[goal, span, :] = value.astype(BF)
            return carry

        lax.fori_loop(0, self.rows // 16, one, 0)

    def pairwise(self, j):
        if not isinstance(j, int):
            pl.when(j >= self.first + 2)(lambda: self.to_pair(j - 2).wait_send())
        self.products(j)
        self.to_pair(j).start()
        self.to_pair(j).wait_recv()
        goal = self.goal(j)
        self.add(goal, self.both.at[j % 2, self.core], self.arrived.at[goal])

    def way(self, way, s):
        last = self.chips - 1
        place = self.chip if way == 0 else last - self.chip
        goal = last - s + self.chip if way == 0 else s - (last - self.chip)
        copy = pltpu.make_async_remote_copy(
            src_ref=self.mine.at[goal], dst_ref=self.passing.at[way, s],
            send_sem=self.line_send.at[way, s], recv_sem=self.line_recv.at[way, s],
            device_id={"ctx": self.me + 2 if way == 0 else self.me - 2}, device_id_type=MESH,
        )
        return place, goal, copy

    def coming(self, way, s):
        return pltpu.make_async_remote_copy(
            src_ref=self.mine.at[self.chip], dst_ref=self.passing.at[way, s],
            send_sem=self.line_send.at[way, s], recv_sem=self.line_recv.at[way, s],
            device_id={"ctx": self.me - 2 if way == 0 else self.me + 2}, device_id_type=MESH,
        )

    def start(self, s):
        for way in range(2):
            place, _, copy = self.way(way, s)
            pl.when(place == 0)(copy.start)

    def relay(self, s):
        for way in range(2):
            place, goal, copy = self.way(way, s)

            @pl.when((place > 0) & (place <= s))
            def later(way=way, goal=goal, copy=copy):
                self.coming(way, s - 1).wait_recv()
                self.add(goal, self.mine.at[goal], self.passing.at[way, s - 1])
                copy.start()

    def last(self):
        for way in range(2):
            place = self.chip if way == 0 else self.chips - 1 - self.chip
            copy = self.coming(way, self.chips - 2)
            pl.when(place > 0)(copy.wait_recv)

        def one(t, carry):
            span = pl.ds(pl.multiple_of(t * 16, 16), 16)
            self.out_ref[span, :] = self.mine[self.chip, span, :].astype(F32)
            for way in range(2):
                place = self.chip if way == 0 else self.chips - 1 - self.chip

                @pl.when(place > 0)
                def more(way=way):
                    value = self.passing[way, self.chips - 2, span, :]
                    self.out_ref[span, :] += value.astype(F32)

            return carry

        lax.fori_loop(0, self.rows // 16, one, 0)

    def drain(self):
        for j in range(self.chips - 2, self.chips):
            self.to_pair(j).wait_send()
        for s in range(self.chips - 1):
            for way in range(2):
                place, _, copy = self.way(way, s)
                pl.when(place <= s)(copy.wait_send)


class LineGather:
    def __init__(self, own_ref, out_ref, line_send, line_recv, pair_send, pair_recv, keep_sem):
        self.own_ref, self.out_ref = own_ref, out_ref
        self.line_send, self.line_recv = line_send, line_recv
        self.pair_send, self.pair_recv, self.keep_sem = pair_send, pair_recv, keep_sem
        self.me = lax.axis_index("ctx")
        self.chips = out_ref.shape[0] // 2
        self.chip, self.core = self.me // 2, self.me % 2

    def place(self, way):
        return self.chip if way == 0 else self.chips - 1 - self.chip

    def slot(self, way, h):
        return self.me - 2 * h if way == 0 else self.me + 2 * h

    def on(self, way, h):
        slot = self.slot(way, h)
        src = self.own_ref if h == 0 else self.out_ref.at[slot]
        return pltpu.make_async_remote_copy(
            src_ref=src, dst_ref=self.out_ref.at[slot],
            send_sem=self.line_send.at[way, h], recv_sem=self.line_recv.at[way, h],
            device_id={"ctx": self.me + 2 if way == 0 else self.me - 2}, device_id_type=MESH,
        )

    def arriving(self, way, h):
        slot = self.slot(way, h)
        return pltpu.make_async_remote_copy(
            src_ref=self.own_ref, dst_ref=self.out_ref.at[slot],
            send_sem=self.line_send.at[way, h - 1], recv_sem=self.line_recv.at[way, h - 1],
            device_id={"ctx": self.me - 2 if way == 0 else self.me + 2}, device_id_type=MESH,
        )

    def across(self, chip, slot, src):
        return pltpu.make_async_remote_copy(
            src_ref=src, dst_ref=self.out_ref.at[slot],
            send_sem=self.pair_send.at[chip], recv_sem=self.pair_recv.at[chip],
            device_id={"ctx": self.me + 1 - 2 * self.core}, device_id_type=MESH,
        )

    def keep(self):
        return pltpu.make_async_copy(self.own_ref, self.out_ref.at[self.me], self.keep_sem)

    def start(self):
        for place in range(self.chips - 1):
            self.launch(place)
        self.stay()

    def launch(self, place):
        for way in range(2):
            pl.when(self.place(way) == place)(self.on(way, 0).start)

    def stay(self):
        self.across(self.chip, self.me, self.own_ref).start()
        self.keep().start()

    def step(self, h):
        for way in range(2):

            @pl.when(self.place(way) >= h)
            def come(way=way):
                self.arriving(way, h).wait_recv()
                pl.when(self.place(way) < self.chips - 1)(self.on(way, h).start)
                slot = self.slot(way, h)
                self.across(slot // 2, slot, self.out_ref.at[slot]).start()

    def come(self, chip):
        slot = 2 * chip + 1 - self.core
        self.across(chip, slot, self.out_ref.at[slot]).wait_recv()

    def finish(self, came=False):
        for h in range(self.chips - 1):
            for way in range(2):
                pl.when((self.place(way) < self.chips - 1) & (self.place(way) >= h))(
                    self.on(way, h).wait_send
                )
        for chip in range(self.chips):
            slot = 2 * chip + self.core
            self.across(chip, slot, self.out_ref.at[slot]).wait_send()
            if not came:
                self.come(chip)
        if not came:
            self.keep().wait()


def greet_all(across=False):
    me = lax.axis_index("ctx")
    chips = lax.axis_size("ctx") // 2
    chip = me // 2
    barrier = pltpu.get_barrier_semaphore()
    x, y, far = plane_neighbours(lax.axis_index("fsdp"))
    greet = lambda axis, who: pl.semaphore_signal(
        barrier, inc=1, device_id={axis: who}, device_id_type=MESH
    )
    greet("fsdp", x)
    greet("fsdp", y)
    if across:
        greet("fsdp", far)
    greet("ctx", me + 1 - 2 * (me % 2))
    pl.when(chip > 0)(lambda: greet("ctx", me - 2))
    pl.when(chip < chips - 1)(lambda: greet("ctx", me + 2))
    plane = 3 if across else 2
    line = 1 + (chip + chips - 1) // chips + (2 * chips - 2 - chip) // chips
    pl.semaphore_wait(barrier, plane + line)


def greet_line():
    me = lax.axis_index("ctx")
    chips = lax.axis_size("ctx") // 2
    chip = me // 2
    barrier = pltpu.get_barrier_semaphore()
    greet = lambda who: pl.semaphore_signal(
        barrier, inc=1, device_id={"ctx": who}, device_id_type=MESH
    )
    greet(me + 1 - 2 * (me % 2))
    pl.when(chip > 0)(lambda: greet(me - 2))
    pl.when(chip < chips - 1)(lambda: greet(me + 2))
    pl.semaphore_wait(barrier, 1 + (chip + chips - 1) // chips + (2 * chips - 2 - chip) // chips)


class Staged:
    def __init__(self, hbm_refs, vmem_refs, sem):
        self.copies = [
            pltpu.make_async_copy(src, dst, sem.at[i])
            for i, (src, dst) in enumerate(zip(hbm_refs, vmem_refs))
        ]

    def start(self):
        for copy in self.copies:
            copy.start()

    def wait(self, first, last):
        for copy in self.copies[first:last]:
            copy.wait()


class PlaneSum:
    def __init__(self, sent, come, send_sem, recv_sem):
        self.sent, self.come, self.send_sem, self.recv_sem = sent, come, send_sem, recv_sem
        self.shard, self.half = lax.axis_index("fsdp"), sent.shape[1] // 2

    def owner(self, r):
        across_x = (self.shard % 2 + r % 2) % 2
        across_y = (self.shard // 2 + r // 2) % 2
        return 2 * across_y + across_x

    def part(self, ref, slot, lower):
        return ref.at[slot, pl.ds(lower * self.half, self.half)]

    def copy(self, i):
        block, slot, lower, along = (
            (1, 0, 0, 0), (3, 1, 0, 0), (2, 0, 1, 1), (3, 1, 1, 1), (2, 2, 0, 1), (1, 2, 1, 0),
        )[i]
        x, y, _ = plane_neighbours(self.shard)
        return pltpu.make_async_remote_copy(
            src_ref=self.part(self.sent, block, lower), dst_ref=self.part(self.come, slot, lower),
            send_sem=self.send_sem.at[i], recv_sem=self.recv_sem.at[i],
            device_id={"fsdp": y if along else x}, device_id_type=MESH,
        )

    def fill(self, block):
        def one(r, carry):
            self.sent[r] = block(self.owner(r))
            return carry

        lax.fori_loop(0, self.sent.shape[0], one, 0)

    def start(self):
        for i in range(4):
            self.copy(i).start()

    def add(self, block, slot, lower):
        def one(t, carry):
            span = pl.ds(pl.multiple_of(lower * self.half + t * 16, 16), 16)
            value = self.sent[block, span, :].astype(F32) + self.come[slot, span, :].astype(F32)
            self.sent[block, span, :] = value.astype(BF)
            return carry

        lax.fori_loop(0, self.half // 16, one, 0)

    def relay(self):
        for lower, passed in ((0, 2), (1, 1)):
            self.copy(2 * lower + 1).wait_recv()
            self.add(passed, 1, lower)
            self.copy(4 + lower).start()
            self.copy(2 * lower).wait_recv()
            self.add(0, 0, lower)

    def total(self, target):
        for i in (4, 5):
            self.copy(i).wait_recv()

        def add(t, carry):
            span = pl.ds(pl.multiple_of(t * 16, 16), 16)
            value = self.sent[0, span, :].astype(F32) + self.come[2, span, :].astype(F32)
            target[span, :] = value.astype(BF)
            return carry

        lax.fori_loop(0, 2 * self.half // 16, add, 0)

    def drain(self):
        for i in range(6):
            self.copy(i).wait_send()


def plane_scratch(shards, rows, columns):
    sem = pltpu.SemaphoreType.DMA((6,))
    return [
        pltpu.VMEM((shards, rows, columns), BF), pltpu.VMEM((3, rows, columns), BF), sem, sem,
    ]


def line_scratch(chips, rows):
    return [
        pltpu.VMEM((chips, rows, D), BF),
        pltpu.VMEM((2, 2, rows, D), BF),
        pltpu.VMEM((chips, rows, D), BF),
        pltpu.VMEM((2, chips - 1, rows, D), BF),
        pltpu.SemaphoreType.DMA((chips,)),
        pltpu.SemaphoreType.DMA((chips,)),
        pltpu.SemaphoreType.DMA((2, chips - 1)),
        pltpu.SemaphoreType.DMA((2, chips - 1)),
    ]


def gather_scratch(chips):
    line = pltpu.SemaphoreType.DMA((2, chips - 1))
    pair = pltpu.SemaphoreType.DMA((chips,))
    return [line, line, pair, pair, pltpu.SemaphoreType.DMA]


def taker(refs):
    refs = list(refs)

    def take(count):
        taken = refs[:count]
        del refs[:count]
        return taken

    return take


def sum_out(own_ref, *refs):
    take = taker(refs)
    (far,), given = take(1), take(14)
    out_ref, all_ref, d_ref = take(3)
    line, gathering, held, (stage_sem, far_sem), accs = take(8), take(5), take(14), take(2), take(2)
    staged = Staged(given, held, stage_sem)
    job = LineSum(False, held[:4], out_ref, line)
    job.first = 1
    ready = pltpu.make_async_copy(far, job.mine.at[job.goal(0)], far_sem)
    gather = LineGather(own_ref, all_ref, *gathering)
    back = CarriedBackward(held[4:], d_ref, *accs)
    chips = job.chips
    ready.start()
    staged.start()
    greet_line()
    gather.start()
    ready.wait()
    job.start(0)
    staged.wait(0, 4)
    lax.fori_loop(1, chips, lambda j, carry: (job.pairwise(j), carry)[1], 0)
    for s in range(1, chips - 1):
        job.start(s)
    staged.wait(4, 14)
    back.clear()
    steps = []
    for s in range(1, chips):
        steps.append(functools.partial(gather.step, s))
        if s < chips - 1:
            steps.append(functools.partial(job.relay, s))
    at = 0
    for i, step in enumerate(steps):
        step()
        upto = back.blocks // 2 + i if i < len(steps) - 1 else back.blocks
        upto = min(upto, back.blocks)
        back.run(at, upto)
        at = upto
    back.finish()
    job.last()
    job.drain()
    gather.finish()


def sum_out_call(own, far, operands, carried):
    dealers, rows, _ = operands[0].shape
    chips, width = dealers // 2, carried[0].shape[2]
    vmem = pl.BlockSpec(memory_space=pltpu.VMEM)
    given = (*operands, *carried)
    return pl.pallas_call(
        sum_out,
        name="sum_out",
        in_specs=[HBM] * (2 + len(given)),
        out_specs=[vmem, HBM, vmem],
        out_shape=[
            jax.ShapeDtypeStruct((rows, D), F32),
            jax.ShapeDtypeStruct((dealers,) + own.shape, own.dtype),
            jax.ShapeDtypeStruct((dealers, rows, 3 * width), BF),
        ],
        scratch_shapes=line_scratch(chips, rows)
        + gather_scratch(chips)
        + [pltpu.VMEM(value.shape, value.dtype) for value in given]
        + [pltpu.SemaphoreType.DMA((len(given),)), pltpu.SemaphoreType.DMA]
        + [pltpu.VMEM((dealers * rows // 256, width, 256), F32)] * 2,
        compiler_params=pltpu.CompilerParams(
            collective_id=2, has_side_effects=True, vmem_limit_bytes=VMEM_BYTES
        ),
    )(own, far, *given)


def sum_back(own_ref, *refs):
    take = taker(refs)
    given = take(5)
    out_ref, all_ref, qkv_ref = take(3)
    line, gathering, held, (stage_sem,), plane = take(8), take(5), take(5), take(1), take(4)
    staged = Staged(given, held, stage_sem)
    job = LineSum(True, held[:4], out_ref, line)
    gather = LineGather(own_ref, all_ref, *gathering)
    weights = PlaneSum(*plane)
    chips = job.chips
    d_qkv, normed = held[0], held[4]
    staged.start()
    greet_all()
    gather.start()
    staged.wait(0, 4)
    job.pairwise(0)
    job.start(0)
    lax.fori_loop(1, chips, lambda j, carry: (job.pairwise(j), carry)[1], 0)
    for s in range(1, chips - 1):
        job.start(s)
    staged.wait(4, 5)
    lines = qkv_ref.shape[0]
    grads = d_qkv[...].reshape(normed.shape[0], d_qkv.shape[2])

    def block(owner):
        span = pl.ds(pl.multiple_of(owner * lines, lines), lines)
        return dot_tn(normed[:, span], grads).astype(BF)

    gather.step(1)
    weights.fill(block)
    weights.start()
    for s in range(1, chips):
        if s > 1:
            gather.step(s)
        if s < chips - 1:
            job.relay(s)
        if s == 1:
            weights.relay()
    weights.total(qkv_ref)
    job.last()
    job.drain()
    gather.finish()
    weights.drain()


def sum_back_call(shards, own, operands, normed, after=()):
    dealers, rows, width = operands[0].shape
    chips = dealers // 2
    vmem = pl.BlockSpec(memory_space=pltpu.VMEM)
    given = (*operands, normed)
    return pl.pallas_call(
        behind(sum_back, len(after)),
        name="sum_back",
        in_specs=[HBM] * (len(after) + 1 + len(given)),
        out_specs=[vmem, HBM, vmem],
        out_shape=[
            jax.ShapeDtypeStruct((rows, D), F32),
            jax.ShapeDtypeStruct((dealers,) + own.shape, own.dtype),
            jax.ShapeDtypeStruct((D // shards, width), BF),
        ],
        scratch_shapes=line_scratch(chips, rows)
        + gather_scratch(chips)
        + [pltpu.VMEM(value.shape, value.dtype) for value in given]
        + [pltpu.SemaphoreType.DMA((len(given),))]
        + plane_scratch(shards, D // shards, width),
        compiler_params=pltpu.CompilerParams(
            collective_id=3, has_side_effects=True, vmem_limit_bytes=VMEM_BYTES
        ),
    )(*after, own, *given)


class Rows:
    def __init__(self, src_ref, dst_ref, sem):
        self.src, self.dst, self.sem = src_ref, dst_ref, sem

    def copy(self, chip):
        span = pl.ds(2 * chip, 2)
        return pltpu.make_async_copy(self.src.at[span], self.dst.at[span], self.sem.at[chip])

    def finish(self):
        for chip in range(self.src.shape[0] // 2):
            self.copy(chip).wait()


def paired(left, right, odd):
    lane = lax.broadcasted_iota(jnp.int32, left.shape, 1)
    left = jnp.where(odd, pltpu.roll(left, HD, 1), left)
    right = jnp.where(odd, right, pltpu.roll(right, HD, 1))
    return jnp.where(lane < HD, left, right)


def phase_one(*refs):
    take = taker(refs)
    lengths, order_ref, turn_ref = take(3)
    vectors = take(8)
    x_hbm, dy_hbm, w_qkv, w_up, w_out, w_down = take(6)
    small, col_ref, row_ref, attn_ref, attn_f_ref, lse_ref = take(6)
    q_out, k_out, v_out, cos_out, sin_out = take(5)
    normed_out, act_out, slope_out, dy_out, qkv_out, up_out, wo_out, wd_out = take(8)
    q_ref, k_ref, v_ref, cos_ref, sin_ref = take(5)
    x_all, normed, act, slope, qkv, up, raw, dy_raw, dy_own, small_own = take(10)
    tile_sem, up_sem, own_sem, send_sem, recv_sem, keep_sem = take(6)
    normed_sem, act_sem, slope_sem, q_sem, k_sem, v_sem = take(6)
    x_sems, dy_sems = take(5), take(5)
    me, shard = lax.axis_index("ctx"), lax.axis_index("fsdp")
    dealers, rows, width = q_ref.shape
    chips, shards, units = dealers // 2, qkv.shape[0], act.shape[2]
    unit, heads, lines = units // shards, wo_out.shape[1], wd_out.shape[1]
    odd = me % 2 == 1

    tiles = []
    for i in range(3 * shards):
        column = (i // shards) * D + (i % shards) * (D // shards) + (me // 2) * LANES
        tiles.append(
            pltpu.make_async_copy(
                w_qkv.at[:, pl.ds(pl.multiple_of(column, LANES), LANES)],
                raw.at[:, pl.ds(i * LANES, LANES)],
                tile_sem.at[i],
            )
        )
    slices = []
    for j in range(shards):
        column = pl.multiple_of(j * (FF // shards) + me * unit, LANES)
        slices.append(
            pltpu.make_async_copy(
                w_up.at[:, pl.ds(column, unit)],
                up.at[shard, :, pl.ds(j * unit, unit)],
                up_sem.at[j],
            )
        )
    load_dy = pltpu.make_async_copy(dy_hbm, dy_raw, own_sem.at[0])
    wo_own = w_out.at[pl.ds(me * heads, heads)]
    wd_own = w_down.at[pl.ds(me * lines, lines)]
    owns = [
        pltpu.make_async_copy(wo_own, wo_out.at[shard], own_sem.at[1]),
        pltpu.make_async_copy(wd_own, wd_out.at[shard], own_sem.at[2]),
    ]
    for copy in (*tiles, *slices, load_dy):
        copy.start()
    x = LineGather(x_hbm, x_all, *x_sems)
    dy = LineGather(dy_own, dy_out, *dy_sems)
    gathers = [
        PlaneGather(out, send_sem, recv_sem, 4 * i)
        for i, out in enumerate((small, qkv, up, wd_out, wo_out))
    ]
    small_gather, qkv_gather, up_gather, wd_gather, wo_gather = gathers
    greet_all()
    x.start()

    at, starts = 0, []
    for vector in vectors:
        starts.append(at)
        small_own[at : at + vector.shape[0], :] = vector[...].astype(F32)
        at += vector.shape[0]
    small_own[at:, :] = jnp.zeros((small_own.shape[0] - at, LANES), F32)
    small[shard] = small_own[...]
    small_gather.first(small_own)
    for tile in tiles:
        tile.wait()
    for i in range(3 * shards // 2):
        left = raw[:, 2 * i * LANES : (2 * i + 1) * LANES].astype(F32)
        right = raw[:, (2 * i + 1) * LANES : (2 * i + 2) * LANES].astype(F32)
        qkv[shard, :, i * LANES : (i + 1) * LANES] = paired(left, right, odd).astype(BF)
    qkv_gather.first(qkv.at[shard])
    for own in owns:
        own.start()

    place = lax.broadcasted_iota(jnp.int32, (rows, rows), 0)
    load_dy.wait()
    pick = jnp.where(order_ref[me] // dealers == place, 1.0, 0.0).astype(BF)
    dy_own[...] = dot_nn(pick, dy_raw[...]).astype(BF)

    def tables(dealer, carry):
        order_row = order_ref[dealer]
        chosen = order_row // dealers == place
        order = jnp.sum(jnp.where(chosen, order_row.astype(F32), 0.0), axis=1, keepdims=True)
        order = order.astype(jnp.int32)
        start = jnp.zeros_like(order)
        bound = 0
        for i in range(lengths.shape[1]):
            start = jnp.where(order >= bound, bound, start)
            bound = bound + lengths[0, i]
        col_ref[dealer] = jnp.concatenate([order, start], axis=1)
        angles = (order - start).astype(F32) * turn_ref[0:1]
        cos_ref[dealer] = jnp.cos(angles)
        sin_ref[dealer] = jnp.sin(angles) * turn_ref[1:2]
        return carry

    small_gather.forward()
    lax.fori_loop(0, dealers, tables, 0)
    rows_of_orders(col_ref, row_ref)
    turned = [
        pltpu.make_async_copy(cos_ref, cos_out, keep_sem.at[2]),
        pltpu.make_async_copy(sin_ref, sin_out, keep_sem.at[3]),
    ]
    for copy in turned:
        copy.start()
    small_gather.finish(small_own)

    def line(base, count):
        return jnp.concatenate(
            [small[j, base + i : base + i + 1, :] for j in range(shards) for i in range(count)], axis=1
        )

    def heads_of(base):
        row = pl.ds(base + me // 2, 1)
        return [paired(small[j, row, :], small[j + 1, row, :], odd) for j in range(0, shards, 2)]

    def turned_heads(base):
        lane = lax.broadcasted_iota(jnp.int32, (1, LANES), 1)
        found = []
        for j in range(shards):
            value = small[j, pl.ds(base + me * ROT // LANES, 1), :]
            moved = jnp.zeros_like(value)
            for i in range(LANES // ROT):
                here = me % (LANES // ROT) == i
                moved = jnp.where(here, pltpu.roll(value, (LANES - i * ROT) % LANES, 1), moved)
            moved = jnp.where(lane < ROT, moved, 0.0)
            found.append(pltpu.roll(moved, HD, 1) if j % 2 else moved)
        return [found[j] + found[j + 1] for j in range(0, shards, 2)]

    gain, shift = line(starts[0], 4), line(starts[1], 4)
    bias = jnp.concatenate(heads_of(starts[2]) + turned_heads(starts[3]) + heads_of(starts[4]), axis=1)
    up_bias = jnp.concatenate(
        [
            small[j, pl.ds(starts[6] + me * (unit // LANES) + i, 1), :]
            for j in range(shards)
            for i in range(unit // LANES)
        ],
        axis=1,
    )

    chip = me // 2
    side = (2 * chip) // chips
    near = (1 - side) * chip + side * (chips - 1 - chip)

    def nth(j):
        zigzag = near + j // 2 if j % 2 == 0 else near - (j + 1) // 2
        close = (2 * near - j + 2 * chips) // (2 * chips)
        found = close * zigzag + (1 - close) * j
        return (1 - side) * found + side * (chips - 1 - found)

    qkv_w = qkv.reshape(D, 3 * width)
    up_w = up.reshape(D, units)
    normed_rows = Rows(normed, normed_out, normed_sem)
    act_rows, slope_rows = Rows(act, act_out, act_sem), Rows(slope, slope_out, slope_sem)
    projected_rows = [
        Rows(q_ref, q_out, q_sem), Rows(k_ref, k_out, k_sem), Rows(v_ref, v_out, v_sem),
    ]

    def project(j):
        def one(core, carry):
            dealer = 2 * nth(j) + core
            chosen = order_ref[dealer] // dealers == place
            value = dot_nn(jnp.where(chosen, 1.0, 0.0).astype(BF), x_all[dealer])
            mean = jnp.mean(value, axis=1, keepdims=True)
            centered = value - mean
            variance = jnp.mean(centered * centered, axis=1, keepdims=True)
            value = centered * lax.rsqrt(variance + 1e-05) * gain + shift
            normed[dealer] = value.astype(BF)
            projected = dot_nn(normed[dealer], qkv_w[...]) + bias
            cosine, sine = wide(cos_ref[dealer], width), wide(sin_ref[dealer], width)
            q = projected[:, :width]
            k = projected[:, width : 2 * width]
            q = (q * cosine + partner(q) * sine).astype(BF)
            q_ref[dealer] = (q.astype(F32) * 0.125).astype(BF)
            k_ref[dealer] = (k * cosine + partner(k) * sine).astype(BF)
            v_ref[dealer] = projected[:, 2 * width :].astype(BF)
            return carry

        if j == 0:
            x.keep().wait()
        x.come(nth(j))
        lax.fori_loop(0, 2, one, 0)
        for kept in (normed_rows, *projected_rows):
            kept.copy(nth(j)).start()

    def expand(at, carry):
        pair = pl.ds(2 * at, 2)
        hidden = dot_nn(normed[pair].reshape(2 * rows, D), up_w[...]) + up_bias
        square = hidden * hidden
        factor = 0.7978845608028654
        bent = jnp.tanh(factor * (hidden + 0.044715 * (hidden * square)))
        half = 0.5 * (1.0 + bent)
        act[pair] = (hidden * half).astype(BF).reshape(2, rows, units)
        grad = half + 0.5 * hidden * (1.0 - bent * bent) * (
            factor * (1.0 + 3.0 * 0.044715 * square)
        )
        slope[pair] = grad.astype(BF).reshape(2, rows, units)
        act_rows.copy(at).start()
        slope_rows.copy(at).start()
        return carry

    for copy in slices:
        copy.wait()
    x.step(1)
    dy.stay()
    dy.launch(0)
    qkv_gather.forward()
    up_gather.first(up.at[shard])
    qkv_gather.finish(qkv.at[shard])
    project(0)
    if chips > 2:
        x.step(2)
        dy.launch(1)
    for j in range(1, chips - 1):
        project(j)
    up_gather.forward()
    wd_gather.first(wd_own)
    wo_gather.first(wo_own)
    for h in range(3, chips):
        x.step(h)
        dy.launch(h - 1)
    project(chips - 1)
    x.finish(True)
    up_gather.finish(up.at[shard])
    keeps = [
        pltpu.make_async_copy(qkv, qkv_out, keep_sem.at[0]),
        pltpu.make_async_copy(up, up_out, keep_sem.at[1]),
    ]
    for keep in keeps:
        keep.start()
    flash = CarriedForward(q_ref, k_ref, v_ref, col_ref, row_ref, attn_ref, attn_f_ref, lse_ref)
    cut = flash.blocks // 2
    lax.fori_loop(0, chips // 2, expand, 0)
    dy.step(1)
    lax.fori_loop(chips // 2, chips, expand, 0)
    flash.run(0, cut)
    for h in range(2, chips - 1):
        dy.step(h)
    wd_gather.forward()
    wo_gather.forward()
    flash.run(cut, flash.blocks - 1)
    dy.step(chips - 1)
    flash.run(flash.blocks - 1, flash.blocks)
    dy.finish()
    wd_gather.finish(wd_own)
    wo_gather.finish(wo_own)
    for copy in (*owns, *keeps, *turned):
        copy.wait()
    for kept in (normed_rows, act_rows, slope_rows, *projected_rows):
        kept.finish()


def phase_one_call(shards, lengths, order, turn, vectors, x, dy, w_qkv, w_up, w_out, w_down):
    dealers, _, rows = order.shape
    chips, blocks = dealers // 2, dealers * rows // 256
    width, units, lines = D // dealers, FF // dealers, D // shards
    vmem = pl.BlockSpec(memory_space=pltpu.VMEM)
    out = lambda kind, *shape: jax.ShapeDtypeStruct(shape, kind)
    small = sum(vector.shape[0] for vector in vectors)
    small += -small % 16
    per_row = lambda kind, w: out(kind, dealers, rows, w)
    dma = lambda *shape: pltpu.SemaphoreType.DMA(shape)
    return pl.pallas_call(
        phase_one,
        name="phase_one",
        in_specs=[pl.BlockSpec(memory_space=pltpu.SMEM)] + [vmem] * 10 + [HBM] * 6,
        out_specs=[vmem] * 6 + [HBM] * 13,
        out_shape=[
            out(F32, shards, small, LANES), per_row(jnp.int32, 2), out(jnp.int32, blocks, 1, 256),
            per_row(BF, width), per_row(F32, width), per_row(F32, width // HD),
            per_row(BF, width), per_row(BF, width), per_row(BF, width),
            per_row(F32, LANES), per_row(F32, LANES),
            per_row(BF, D), per_row(BF, units), per_row(BF, units), per_row(BF, D),
            out(BF, shards, lines, 3 * width), out(BF, shards, lines, units),
            out(BF, shards, width // shards, D), out(BF, shards, units // shards, D),
        ],
        scratch_shapes=[pltpu.VMEM((dealers, rows, width), BF)] * 3
        + [pltpu.VMEM((dealers, rows, LANES), F32)] * 2
        + [
            pltpu.VMEM((dealers, rows, D), BF), pltpu.VMEM((dealers, rows, D), BF),
            pltpu.VMEM((dealers, rows, units), BF), pltpu.VMEM((dealers, rows, units), BF),
            pltpu.VMEM((shards, lines, 3 * width), BF), pltpu.VMEM((shards, lines, units), BF),
            pltpu.VMEM((lines, 3 * shards * LANES), BF),
            pltpu.VMEM((rows, D), BF), pltpu.VMEM((rows, D), BF), pltpu.VMEM((small, LANES), F32),
            dma(3 * shards), dma(shards), dma(3), dma(20), dma(20), dma(4),
        ]
        + [dma(chips)] * 6
        + gather_scratch(chips)
        + gather_scratch(chips),
        compiler_params=pltpu.CompilerParams(
            collective_id=0, has_side_effects=True, vmem_limit_bytes=VMEM_BYTES
        ),
    )(lengths, order, turn, *vectors, x, dy, w_qkv, w_up, w_out, w_down)


def hidden_grads(*refs):
    take = taker(refs)
    given = take(7)
    d_attn_ref, second_ref, d_up_out, d_hidden_out, far_out, first_all, out_all = take(7)
    d_up_ref, d_hidden_ref = take(2)
    held, (stage_sem, up_sem, keep_sem) = take(7), take(3)
    *parts, out_sum = [PlaneSum(*take(4)) for _ in range(3)]
    first_ref, out_own, d_out = take(3)
    far, (far_send, far_recv) = take(3), take(2)
    dy, attn, act, wo, wd, slope, normed = held
    units, half = first_ref.shape
    count, shards = dy.shape[0], parts[0].sent.shape[0]
    staged = Staged(given, held, stage_sem)
    gather = LineGather(first_ref, first_all, *take(5))
    out_gather = LineGather(out_own, out_all, *take(5))
    chips = gather.chips
    width, dealers = attn.shape[1], 2 * chips
    rows = count // dealers
    job = LineSum(
        False,
        (attn.reshape(dealers, rows, width), act.reshape(dealers, rows, act.shape[1]), wo, wd),
        None,
        (*far, None, far_send, far_recv, None, None),
    )
    staged.start()
    greet_all()
    staged.wait(0, 2)

    def down_block(part):
        columns = slice(0, half) if part == 0 else slice(half, D)

        def block(owner):
            span = pl.ds(pl.multiple_of(owner * units, units), units)
            return dot_tn(act[:, span], dy[:, columns]).astype(BF)

        return block

    some = count // chips

    def attn_rows(t, carry):
        span = pl.ds(pl.multiple_of(t * some, some), some)
        d_attn_ref[span, :] = dot_nt(dy[span, :], wo[...]).astype(BF)
        return carry

    def hidden_rows(t, carry):
        span = pl.ds(pl.multiple_of(t * some, some), some)
        value = dot_nt(dy[span, :], wd[...]) * slope[span, :].astype(F32)
        d_hidden_ref[span, :] = value.astype(BF)
        return carry

    lines = normed.shape[1] // shards

    def up_rows(t, carry):
        span = pl.ds(pl.multiple_of(t * lines, lines), lines)
        value = dot_tn(normed[:, span], d_hidden_ref[...])
        d_up_ref[t] = value.astype(BF)
        leave_up(t).start()
        return carry

    def leave_up(t):
        return pltpu.make_async_copy(d_up_ref.at[t], d_up_out.at[t], up_sem.at[t])

    piece = attn.shape[1] // shards

    def out_block(owner):
        return d_out[pl.ds(pl.multiple_of(owner * piece, piece), piece), :]

    d_out[...] = dot_tn(attn[...], dy[...]).astype(BF)
    out_sum.fill(out_block)
    out_sum.start()
    staged.wait(2, 3)
    parts[0].fill(down_block(0))
    out_sum.relay()
    parts[0].start()
    parts[1].fill(down_block(1))
    out_sum.total(out_own)
    out_gather.start()
    staged.wait(3, 4)
    lax.fori_loop(0, chips, attn_rows, 0)
    parts[0].relay()
    parts[1].start()
    staged.wait(4, 6)
    out_gather.step(1)
    lax.fori_loop(0, chips // 2, hidden_rows, 0)
    parts[0].total(first_ref)
    gather.start()
    lax.fori_loop(chips // 2, chips, hidden_rows, 0)
    leave_hidden = pltpu.make_async_copy(d_hidden_ref, d_hidden_out, keep_sem.at[0])
    leave_hidden.start()
    for h in range(2, chips - 1):
        out_gather.step(h)
    job.pairwise(0)
    leave_far = pltpu.make_async_copy(job.mine.at[job.goal(0)], far_out, keep_sem.at[1])
    leave_far.start()
    parts[1].relay()
    staged.wait(6, 7)
    lax.fori_loop(0, shards // 2, up_rows, 0)
    out_gather.step(chips - 1)
    gather.step(1)
    lax.fori_loop(shards // 2, shards, up_rows, 0)
    for h in range(2, chips - 1):
        gather.step(h)
    parts[1].total(second_ref)
    gather.step(chips - 1)
    out_sum.drain()
    out_gather.finish()
    job.to_pair(0).wait_send()
    for copy in (leave_hidden, leave_far, *(leave_up(t) for t in range(shards))):
        copy.wait()
    for part in parts:
        part.drain()
    gather.finish()


def hidden_grads_call(shards, dy, attn, act, wo, wd, slope, normed):
    count, units = act.shape
    width = wo.shape[0]
    dealers = FF // units
    chips, rows, unit, first = dealers // 2, count // dealers, units // shards, D // 4
    vmem = pl.BlockSpec(memory_space=pltpu.VMEM)
    out = lambda *shape: jax.ShapeDtypeStruct(shape, BF)
    given = (dy, attn, act, wo, wd, slope, normed)
    piece = width // shards
    return pl.pallas_call(
        hidden_grads,
        name="hidden_grads",
        in_specs=[HBM] * len(given),
        out_specs=[vmem] * 2 + [HBM] * 5,
        out_shape=[
            out(count, width), out(unit, D - first), out(shards, D // shards, units),
            out(count, units), out(rows, D), out(dealers, unit, first), out(dealers, piece, D),
        ],
        scratch_shapes=[
            pltpu.VMEM((shards, D // shards, units), BF), pltpu.VMEM((count, units), BF),
        ]
        + [pltpu.VMEM(value.shape, value.dtype) for value in given]
        + [pltpu.SemaphoreType.DMA((count,)) for count in (len(given), shards, 2)]
        + plane_scratch(shards, unit, first)
        + plane_scratch(shards, unit, D - first)
        + plane_scratch(shards, piece, D)
        + [pltpu.VMEM((unit, first), BF), pltpu.VMEM((piece, D), BF), pltpu.VMEM((width, D), BF)]
        + [
            pltpu.VMEM((chips, rows, D), BF), pltpu.VMEM((2, 2, rows, D), BF),
            pltpu.VMEM((chips, rows, D), BF),
            pltpu.SemaphoreType.DMA((chips,)), pltpu.SemaphoreType.DMA((chips,)),
        ]
        + gather_scratch(chips)
        + gather_scratch(chips),
        compiler_params=pltpu.CompilerParams(
            collective_id=5, has_side_effects=True, vmem_limit_bytes=VMEM_BYTES
        ),
    )(*given)


def small_sum(in_ref, out_ref, from_plane, total, from_line, send_sem, recv_sem):
    me, shard = lax.axis_index("ctx"), lax.axis_index("fsdp")
    shards, dealers = from_plane.shape[0], from_line.shape[0]
    barrier = pltpu.get_barrier_semaphore()
    others = [("fsdp", i, lax.rem(shard + i, shards)) for i in range(1, shards)]
    others += [("ctx", i, lax.rem(me + i, dealers)) for i in range(1, dealers)]
    for axis, _, who in others:
        pl.semaphore_signal(barrier, inc=1, device_id={axis: who}, device_id_type=MESH)
    pl.semaphore_wait(barrier, len(others))

    def copy(axis, i, who):
        plane = axis == "fsdp"
        k = i - 1 if plane else shards - 2 + i
        return pltpu.make_async_remote_copy(
            src_ref=in_ref.at[who] if plane else total,
            dst_ref=(from_plane if plane else from_line).at[i],
            send_sem=send_sem.at[k],
            recv_sem=recv_sem.at[k],
            device_id={axis: who},
            device_id_type=MESH,
        )

    copies = [copy(*other) for other in others]
    for one in copies[: shards - 1]:
        one.start()
    for one in copies[: shards - 1]:
        one.wait()
    value = in_ref[shard]
    for i in range(1, shards):
        value = value + from_plane[i]
    total[...] = value
    for one in copies[shards - 1 :]:
        one.start()
    for one in copies[shards - 1 :]:
        one.wait()
    for i in range(1, dealers):
        value = value + from_line[i]
    out_ref[...] = value


def small_sum_call(dealers, value):
    shards, rows, _ = value.shape
    vmem = pl.BlockSpec(memory_space=pltpu.VMEM)
    return pl.pallas_call(
        small_sum,
        name="small_sum",
        in_specs=[vmem],
        out_specs=vmem,
        out_shape=jax.ShapeDtypeStruct((rows, LANES), F32),
        scratch_shapes=[
            pltpu.VMEM((shards, rows, LANES), F32),
            pltpu.VMEM((rows, LANES), F32),
            pltpu.VMEM((dealers, rows, LANES), F32),
            pltpu.SemaphoreType.DMA((shards + dealers - 2,)),
            pltpu.SemaphoreType.DMA((shards + dealers - 2,)),
        ],
        compiler_params=pltpu.CompilerParams(collective_id=4, has_side_effects=True),
    )(value)


def place_up(in_ref, out_ref):
    unit = in_ref.shape[2]
    for i in range(in_ref.shape[0]):
        out_ref[:, i * unit : (i + 1) * unit] = in_ref[i].astype(F32)


def place_up_call(shards, grads, after=()):
    dealers, _, units = grads.shape
    rows, unit = D // shards, units // shards
    return pl.pallas_call(
        behind(place_up, len(after)),
        name="place_up",
        cost_estimate=takes(8),
        grid=(shards,),
        in_specs=[HBM] * len(after) + [pl.BlockSpec((dealers, rows, unit), lambda j: (0, 0, j))],
        out_specs=pl.BlockSpec((rows, dealers * unit), lambda j: (0, j)),
        out_shape=jax.ShapeDtypeStruct((rows, FF), F32),
        compiler_params=pltpu.CompilerParams(vmem_limit_bytes=VMEM_BYTES),
    )(*after, grads)


def place_parts(*refs):
    at, out_ref = 0, refs[-1]
    for ref in refs[:-1]:
        out_ref[:, at : at + ref.shape[2]] = ref[0].astype(F32)
        at += ref.shape[2]


def place_parts_call(*parts, after=()):
    dealers, rows, _ = parts[0].shape
    return pl.pallas_call(
        behind(place_parts, len(after)),
        name="place_parts",
        grid=(dealers,),
        in_specs=[HBM] * len(after)
        + [pl.BlockSpec((1, rows, part.shape[2]), lambda i: (i, 0, 0)) for part in parts],
        out_specs=pl.BlockSpec((rows, D), lambda i: (i, 0)),
        out_shape=jax.ShapeDtypeStruct((dealers * rows, D), F32),
        compiler_params=pltpu.CompilerParams(vmem_limit_bytes=VMEM_BYTES),
    )(*after, *parts)


def place_qkv(shards, in_ref, out_ref):
    dealers, rows, _ = in_ref.shape
    lane = lax.broadcasted_iota(jnp.int32, (rows, LANES), 1)
    for i in range(3 * shards):
        tile = slice((i // 2) * LANES, (i // 2 + 1) * LANES)
        at = (i // shards) * D + (i % shards) * (D // shards)
        for t in range(dealers // 2):
            left = in_ref[2 * t, :, tile].astype(F32)
            right = in_ref[2 * t + 1, :, tile].astype(F32)
            if i % 2 == 0:
                right = pltpu.roll(right, HD, 1)
            else:
                left = pltpu.roll(left, HD, 1)
            out_ref[:, at + t * LANES : at + (t + 1) * LANES] = jnp.where(lane < HD, left, right)


def place_qkv_call(shards, grads, after=()):
    dealers, rows, width = grads.shape
    some = rows // 4
    return pl.pallas_call(
        behind(functools.partial(place_qkv, shards), len(after)),
        name="place_qkv",
        cost_estimate=takes(9),
        grid=(rows // some,),
        in_specs=[HBM] * len(after) + [pl.BlockSpec((dealers, some, width), lambda i: (0, i, 0))],
        out_specs=pl.BlockSpec((some, 3 * D), lambda i: (i, 0)),
        out_shape=jax.ShapeDtypeStruct((rows, 3 * D), F32),
        compiler_params=pltpu.CompilerParams(vmem_limit_bytes=VMEM_BYTES),
    )(*after, grads)


def body(dealers, shards, *args):
    (
        tokens, cotangent, seq_lengths, token_order, ln_gain, ln_bias, w_qkv, q_bias, k_bias,
        v_bias, w_out, out_bias, w_up, up_bias, w_down, down_bias,
    ) = args
    rows = tokens.shape[1]
    count = dealers * rows
    me = lax.axis_index("ctx")
    shard = lax.axis_index("fsdp")
    width, units = D // dealers, FF // dealers
    head_piece, unit_piece = width // shards, units // shards

    def over_ctx(value):
        return lax.all_gather(value, "ctx", axis=0, tiled=False)

    scatter = functools.partial(
        lax.psum_scatter, axis_name="fsdp", scatter_dimension=0, tiled=True
    )
    order_rows = token_order.reshape(dealers, 1, rows)
    frequency = 10000.0 ** (-np.arange(ROT // 2) * 2.0 / ROT)
    zeros = np.zeros(HD - ROT)
    sign = np.concatenate([-np.ones(ROT // 2), np.ones(ROT // 2), zeros])
    turn = np.stack([np.concatenate([frequency, frequency, zeros]), sign]).astype(np.float32)
    turn = jnp.asarray(np.tile(turn, (1, LANES // HD)))
    parts = (ln_gain, ln_bias, q_bias, k_bias, v_bias, out_bias, up_bias, down_bias)
    parts = [part.reshape(-1, LANES) for part in parts]
    (
        small, col, row, attn, attn_f, lse, q, k, v, cosine, sine,
        normed, act, slope, dy_all, qkv_full, up_full, out_full, down_full,
    ) = phase_one_call(
        shards, seq_lengths, order_rows, turn, parts, tokens[0], cotangent[0],
        w_qkv, w_up, w_out, w_down,
    )
    qkv_full = qkv_full.reshape(D, 3 * width)
    up_full = up_full.reshape(D, units)
    vectors, at = [], 0
    for part in parts:
        vectors.append(small[:, at : at + part.shape[0]].reshape(-1))
        at += part.shape[0]
    gain, ob, db = vectors[0], vectors[5], vectors[7]
    flat = lambda value: value.reshape(count, value.shape[2])
    normed_flat = flat(normed)
    dy_all = flat(dy_all)
    out_full = out_full.reshape(width, D)
    down_full = down_full.reshape(units, D)
    rank = lax.dynamic_index_in_dim(order_rows, me, 0).reshape(rows) // dealers
    pick = (rank[None, :] == jnp.arange(rows, dtype=jnp.int32)[:, None]).astype(BF)

    d_attn, second_own, d_up, d_hidden, out_far, first_all, out_all = hidden_grads_call(
        shards, dy_all, flat(attn), flat(act), out_full, down_full, flat(slope), normed_flat
    )
    up_own = scatter(d_up.reshape(-1, units))
    out_own, second_all, d_qkv = sum_out_call(
        second_own, out_far, (attn, act, out_full, down_full),
        (q, d_attn.reshape(q.shape), attn_f, lse, col, row, k, v, cosine, sine),
    )
    dn, up_all, qkv_own = sum_back_call(
        shards, up_own, (d_qkv, d_hidden.reshape(act.shape), qkv_full, up_full), normed_flat,
        after=(out_own,),
    )
    qkv_all = over_ctx(qkv_own)
    d_w_down = place_parts_call(first_all, second_all, after=(qkv_own,))
    d_w_up = place_up_call(shards, up_all)
    d_w_out = place_parts_call(out_all, after=(qkv_own,))
    d_w_qkv = place_qkv_call(shards, qkv_all, after=(d_w_up, d_w_out, d_w_down))
    x = tokens[0].astype(F32)
    out_own = dot_tn(pick, out_own.astype(BF))
    out_act = (x + out_own + (ob + db)[None]).astype(BF)
    dn = dot_tn(pick, dn.astype(BF))
    mean = jnp.mean(x, axis=-1, keepdims=True)
    centered = x - mean
    variance = jnp.mean(centered * centered, axis=-1, keepdims=True)
    inverse = lax.rsqrt(variance + 1e-05)
    standard = centered * inverse
    grad = dn * gain[None]
    d_tokens = cotangent[0].astype(F32) + inverse * (
        grad
        - jnp.mean(grad, axis=-1, keepdims=True)
        - standard * jnp.mean(grad * standard, axis=-1, keepdims=True)
    )

    def place(vector, count):
        mine = (jnp.arange(dealers) == me)[None, :, None]
        vector = jnp.where(mine, vector.reshape(count, 1, -1), 0.0)
        return vector.reshape(count // shards, shards, -1)

    d_qkv_sum = place(jnp.sum(flat(d_qkv).astype(F32), axis=0), 3 * shards)
    d_up_sum = place(jnp.sum(d_hidden.astype(F32), axis=0), shards)
    own = lambda vector: vector.reshape(shards, -1)
    sums = jnp.concatenate(
        [
            own(jnp.sum(dn * standard, axis=0)),
            own(jnp.sum(dn, axis=0)),
            d_qkv_sum[0], d_qkv_sum[1], d_qkv_sum[2], d_up_sum[0],
            own(jnp.sum(cotangent[0].astype(F32), axis=0)),
        ],
        axis=1,
    )
    size = sums.shape[1]
    sums = sums.reshape(shards, -1, LANES)
    sums = jnp.pad(sums, ((0, 0), (0, -sums.shape[1] % 8), (0, 0)))
    sums = small_sum_call(dealers, sums).reshape(-1)[:size]
    piece = D // shards
    gain_sum, shift_sum, q_sum, k_sum, v_sum = (
        sums[i * piece : (i + 1) * piece] for i in range(5)
    )
    up_sum, dy_sum = sums[5 * piece : -piece], sums[-piece:]
    k_sum = k_sum.reshape(-1, HD)[:, :ROT].reshape(-1)
    return (
        out_act[None], d_tokens[None], gain_sum, shift_sum, d_w_qkv, q_sum, k_sum, v_sum,
        d_w_out, dy_sum, d_w_up, up_sum, d_w_down, dy_sum,
    )


def general_body(dealers, shards, *args):
    (
        tokens, cotangent, seq_lengths, token_order, ln_gain, ln_bias, w_qkv, q_bias, k_bias,
        v_bias, w_out, out_bias, w_up, up_bias, w_down, down_bias,
    ) = args
    rows = tokens.shape[1]
    count = dealers * rows
    me = lax.axis_index("ctx")
    shard = lax.axis_index("fsdp")
    width = D // dealers
    spread = HEADS % (dealers * shards) == 0
    head_piece = width // shards if spread else width
    unit_piece = FF // (dealers * shards)

    def over_ctx(value):
        return lax.all_gather(value, "ctx", axis=0, tiled=False)

    def over_fsdp(value):
        return lax.all_gather(value, "fsdp", axis=0, tiled=True)

    x_all = over_ctx(tokens[0])

    order_rows = token_order.reshape(dealers, rows)
    rank = order_rows // dealers
    places = jnp.arange(rows, dtype=jnp.int32)
    order = jnp.sum(
        jnp.where(rank[:, None, :] == places[None, :, None], order_rows[:, None, :], 0), axis=2
    )
    bounds = jnp.cumsum(seq_lengths[0])
    starts = bounds - seq_lengths[0]
    inside = (order[..., None] >= starts) & (order[..., None] < bounds)
    start = jnp.sum(jnp.where(inside, starts, 0), axis=-1)
    position = order - start
    frequency = 10000.0 ** (-jnp.arange(ROT // 2, dtype=F32) * 2.0 / ROT)
    zeros = jnp.zeros((HD - ROT,), F32)
    lane_frequency = jnp.tile(jnp.concatenate([frequency, frequency, zeros]), LANES // HD)
    sign = jnp.concatenate([-jnp.ones((ROT // 2,), F32), jnp.ones((ROT // 2,), F32), zeros])
    angles = position.astype(F32)[..., None] * lane_frequency
    cosine = jnp.cos(angles)
    sine = jnp.sin(angles) * jnp.tile(sign, LANES // HD)
    rounds = 256 // dealers
    blocks = rows // rounds
    row = order.reshape(dealers, blocks, rounds).transpose(1, 0, 2).reshape(blocks, 1, 256)
    col = jnp.stack([order, start], axis=-1)
    low = jnp.min(start.reshape(dealers, blocks, rounds), axis=(0, 2)) // 256

    own_rank = lax.dynamic_index_in_dim(rank, me, 0, keepdims=False)
    pick = (own_rank[None, :] == places[:, None]).astype(BF)
    dy_sorted = dot_nn(pick, cotangent[0]).astype(BF)
    dy_all = over_ctx(dy_sorted).reshape(count, D)

    small = jnp.concatenate(
        [ln_gain, ln_bias, q_bias, k_bias, v_bias, out_bias, up_bias, down_bias]
    )
    small = lax.all_gather(small, "fsdp", axis=0, tiled=False).astype(F32)
    vectors, at = [], 0
    for part in (ln_gain, ln_bias, q_bias, k_bias, v_bias, out_bias, up_bias, down_bias):
        vectors.append(small[:, at : at + part.shape[0]].reshape(shards * part.shape[0]))
        at += part.shape[0]
    gain, shift, qb, kb, vb, ob, ub, db = vectors
    kb = jnp.pad(kb.reshape(HEADS, ROT), ((0, 0), (0, HD - ROT))).reshape(D)

    def own_heads(matrix, axis):
        if not spread:
            return lax.dynamic_slice_in_dim(matrix, me * width, width, axis)
        return jnp.concatenate(
            [
                lax.dynamic_slice_in_dim(
                    matrix, j * (D // shards) + me * head_piece, head_piece, axis
                )
                for j in range(shards)
            ],
            axis=axis,
        )

    def own_units(matrix, axis):
        return jnp.concatenate(
            [
                lax.dynamic_slice_in_dim(
                    matrix, j * (FF // shards) + me * unit_piece, unit_piece, axis
                )
                for j in range(shards)
            ],
            axis=axis,
        )

    qkv_own = jnp.concatenate(
        [own_heads(w_qkv[:, i * D : (i + 1) * D], 1) for i in range(3)], axis=1
    )
    qkv_full = over_fsdp(qkv_own)
    bias_own = jnp.concatenate([own_heads(b, 0) for b in (qb, kb, vb)])
    up_full = over_fsdp(own_units(w_up, 1))
    up_bias_own = own_units(ub, 0)
    down_own = lax.dynamic_slice_in_dim(w_down, me * unit_piece, unit_piece, 0)
    if spread:
        out_own = lax.dynamic_slice_in_dim(w_out, me * head_piece, head_piece, 0)
        both = over_fsdp(jnp.concatenate([out_own, down_own], axis=0))
        both = both.reshape(shards, head_piece + unit_piece, D)
        out_full = both[:, :head_piece].reshape(width, D)
        down_full = both[:, head_piece:].reshape(FF // dealers, D)
    else:
        per = D // shards // width
        mine = lax.dynamic_slice_in_dim(w_out, (me % per) * width, width, 0)
        mine = jnp.where(me // per == shard, mine, jnp.zeros_like(mine))
        out_full = lax.psum(mine, "fsdp")
        down_full = over_fsdp(down_own)

    normed, q, k, v = qkv_call(
        x_all, rank[:, None, :], gain[None], shift[None], qkv_full, bias_own[None], cosine, sine
    )
    normed = normed.reshape(count, D)
    attn, attn_f, lse = flash_forward_call(low, q, k, v, col, row)
    attn = attn.reshape(count, width)
    hidden = dot_nn(normed, up_full) + up_bias_own[None]
    act, gelu_back = jax.vjp(lambda inner: jax.nn.gelu(inner, approximate=True), hidden)
    act = act.astype(BF)
    out_part = (dot_nn(attn, out_full) + dot_nn(act, down_full)).astype(BF)

    d_out = dot_tn(attn, dy_all).astype(BF)
    d_down = dot_tn(act, dy_all).astype(BF)
    scatter = functools.partial(lax.psum_scatter, scatter_dimension=0, tiled=True)
    if spread:
        d_both = jnp.concatenate(
            [d_out.reshape(shards, head_piece, D), d_down.reshape(shards, unit_piece, D)], axis=1
        )
        d_both = over_ctx(scatter(d_both.reshape(shards * (head_piece + unit_piece), D), "fsdp"))
        d_out = d_both[:, :head_piece].astype(F32).reshape(dealers * head_piece, D)
        d_down = d_both[:, head_piece:].astype(F32).reshape(dealers * unit_piece, D)
    else:
        d_out = lax.psum(d_out, "fsdp")
        d_out = jnp.where(me // per == shard, d_out, jnp.zeros_like(d_out))
        spot = jnp.zeros((per * width, D), BF)
        d_out = lax.dynamic_update_slice_in_dim(spot, d_out, (me % per) * width, 0)
        d_out = lax.psum(d_out, "ctx").astype(F32)
        d_down = over_ctx(scatter(d_down, "fsdp")).astype(F32).reshape(dealers * unit_piece, D)
    d_act = dot_nt(dy_all, down_full)
    d_hidden = gelu_back(d_act)[0].astype(BF)
    d_up = over_ctx(scatter(dot_tn(normed, d_hidden).astype(BF), "fsdp"))
    d_up = d_up.reshape(dealers, D // shards, shards, unit_piece).transpose(1, 2, 0, 3)
    d_up = d_up.astype(F32).reshape(D // shards, FF)

    d_attn = dot_nt(dy_all, out_full).astype(BF).reshape(dealers, rows, width)
    d_qkv = flash_backward_call(low, q, d_attn, attn_f, lse, col, row, k, v, cosine, sine)
    d_qkv = d_qkv.reshape(count, 3 * width)
    d_normed = (dot_nt(d_qkv, qkv_full) + dot_nt(d_hidden, up_full)).astype(BF)
    d_w_qkv = over_ctx(scatter(dot_tn(normed, d_qkv).astype(BF), "fsdp"))
    if spread:
        d_w_qkv = d_w_qkv.reshape(dealers, D // shards, 3, shards, head_piece)
        d_w_qkv = d_w_qkv.transpose(1, 2, 3, 0, 4)
    else:
        d_w_qkv = d_w_qkv.reshape(dealers, D // shards, 3, width).transpose(1, 2, 0, 3)
    d_w_qkv = d_w_qkv.astype(F32).reshape(D // shards, 3 * D)

    out_own = dot_tn(pick, scatter(out_part, "ctx"))
    x = tokens[0].astype(F32)
    out_act = (x + out_own + (ob + db)[None]).astype(BF)
    dn = dot_tn(pick, scatter(d_normed, "ctx"))
    mean = jnp.mean(x, axis=-1, keepdims=True)
    centered = x - mean
    variance = jnp.mean(centered * centered, axis=-1, keepdims=True)
    inverse = lax.rsqrt(variance + 1e-05)
    standard = centered * inverse
    grad = dn * gain[None]
    d_tokens = cotangent[0].astype(F32) + inverse * (
        grad
        - jnp.mean(grad, axis=-1, keepdims=True)
        - standard * jnp.mean(grad * standard, axis=-1, keepdims=True)
    )

    def place(vector, pieces):
        piece = vector.shape[0] // pieces
        mine = (jnp.arange(dealers) == me)[None, :, None]
        vector = vector.reshape(pieces, 1, piece)
        return jnp.where(mine, vector, 0.0).reshape(pieces * dealers * piece)

    head_pieces = shards if spread else 1
    sums = jnp.concatenate(
        [
            jnp.sum(dn * standard, axis=0),
            jnp.sum(dn, axis=0),
            jnp.sum(cotangent[0].astype(F32), axis=0),
            place(jnp.sum(d_qkv.astype(F32), axis=0), 3 * head_pieces),
            place(jnp.sum(d_hidden.astype(F32), axis=0), shards),
        ]
    )
    sums = lax.psum(sums, ("ctx", "fsdp"))

    def mine(vector):
        piece = vector.shape[0] // shards
        return lax.dynamic_slice_in_dim(vector, shard * piece, piece, 0)

    gain_sum, shift_sum, dy_sum, qkv_sum, up_sum = (
        sums[:D], sums[D : 2 * D], sums[2 * D : 3 * D], sums[3 * D : 6 * D], sums[6 * D :],
    )
    k_sum = qkv_sum[D : 2 * D].reshape(HEADS, HD)[:, :ROT].reshape(HEADS * ROT)
    return (
        out_act[None], d_tokens[None], mine(gain_sum), mine(shift_sum),
        d_w_qkv, mine(qkv_sum[:D]), mine(k_sum), mine(qkv_sum[2 * D :]),
        d_out, mine(dy_sum), d_up, mine(up_sum), d_down, mine(dy_sum),
    )


def solution(mesh):
    row, vector = P("fsdp", None), P("fsdp")
    split = P("fsdp", "ctx", None)
    in_specs = (
        split, split, row, row, vector, vector, row, vector,
        vector, vector, row, vector, row, vector, row, vector,
    )
    out_specs = (
        split, split, vector, vector, row, vector, vector, vector,
        row, vector, row, vector, row, vector,
    )
    dealers, shards = mesh.shape["ctx"], mesh.shape["fsdp"]
    fast = shards == 4 and dealers % 2 == 0 and D // (dealers * shards) == HD
    step = functools.partial(body if fast else general_body, dealers, shards)
    return jax.shard_map(
        step, mesh=mesh, in_specs=in_specs, out_specs=out_specs, check_vma=False
    )
```

```python
import functools

import jax
import jax.numpy as jnp
import numpy as np
from jax import lax
from jax.experimental import pallas as pl
from jax.experimental.pallas import tpu as pltpu
from jax.sharding import PartitionSpec as P

D = 2048
HEADS = 32
HD = 64
ROT = 32
FF = 8192
LANES = 128
VMEM_BYTES = 56 * 2**20
BF = jnp.bfloat16
F32 = jnp.float32


def dot_nn(a, b):
    return lax.dot_general(a, b, (((1,), (0,)), ((), ())), preferred_element_type=F32)


def dot_nt(a, b):
    return lax.dot_general(a, b, (((1,), (1,)), ((), ())), preferred_element_type=F32)


def dot_tn(a, b):
    return lax.dot_general(a, b, (((0,), (0,)), ((), ())), preferred_element_type=F32)


def wide(table, width):
    return jnp.concatenate([table] * (width // LANES), axis=1)


def partner(values):
    width = values.shape[1]
    lane = lax.broadcasted_iota(jnp.int32, values.shape, 1) % HD
    half = ROT // 2
    return jnp.where(
        lane < half, pltpu.roll(values, width - half, 1), pltpu.roll(values, half, 1)
    )


def sort_norm_project(
    x_ref, rank_ref, gain_ref, shift_ref, w_ref, bias_ref, cos_ref, sin_ref,
    normed_ref, q_ref, k_ref, v_ref,
):
    rows = x_ref.shape[1]
    width = q_ref.shape[2]
    place = lax.broadcasted_iota(jnp.int32, (rows, rows), 0)
    pick = jnp.where(rank_ref[0] == place, 1.0, 0.0).astype(BF)
    x = dot_nn(pick, x_ref[0])
    mean = jnp.mean(x, axis=1, keepdims=True)
    centered = x - mean
    variance = jnp.mean(centered * centered, axis=1, keepdims=True)
    normed = (centered * lax.rsqrt(variance + 1e-05) * gain_ref[...] + shift_ref[...]).astype(BF)
    normed_ref[0] = normed
    projected = dot_nn(normed, w_ref[...]) + bias_ref[...]
    cosine, sine = wide(cos_ref[0], width), wide(sin_ref[0], width)
    q = projected[:, :width]
    k = projected[:, width : 2 * width]
    q = (q * cosine + partner(q) * sine).astype(BF)
    q_ref[0] = (q.astype(F32) * 0.125).astype(BF)
    k_ref[0] = (k * cosine + partner(k) * sine).astype(BF)
    v_ref[0] = projected[:, 2 * width :].astype(BF)


def qkv_call(x_all, rank, gain, shift, weights, bias, cosine, sine):
    dealers, rows, _ = x_all.shape
    width = weights.shape[1] // 3
    whole = lambda *shape: pl.BlockSpec(shape, lambda i: (0,) * len(shape))
    each = lambda *shape: pl.BlockSpec((1,) + shape, lambda i: (i, 0, 0))
    out = lambda w: jax.ShapeDtypeStruct((dealers, rows, w), BF)
    return pl.pallas_call(
        sort_norm_project,
        name="sort_norm_project",
        grid=(dealers,),
        in_specs=[
            each(rows, D), each(1, rows), whole(1, D), whole(1, D),
            whole(D, 3 * width), whole(1, 3 * width), each(rows, LANES), each(rows, LANES),
        ],
        out_specs=[each(rows, D)] + [each(rows, width)] * 3,
        out_shape=[out(D), out(width), out(width), out(width)],
        compiler_params=pltpu.CompilerParams(vmem_limit_bytes=VMEM_BYTES),
    )(x_all, rank, gain, shift, weights, bias, cosine, sine)


def flash_forward(low_ref, q_ref, col_ref, row_ref, k_ref, v_ref, o_ref, of_ref, lse_ref):
    block = pl.program_id(0)
    dealers, rounds, width = q_ref.shape
    size = dealers * rounds
    heads = width // HD
    q = q_ref[...].reshape(size, width)
    col = col_ref[...].reshape(size, 2)
    top, bottom = col[:, 0:1], col[:, 1:2]
    head_of = lax.broadcasted_iota(jnp.int32, (size, width), 1) // HD
    q_of = [jnp.where(head_of == h, q, jnp.zeros_like(q)) for h in range(heads)]

    def step(j, carry):
        at = block - j
        running, total, mixed = carry
        window = pl.ds(pl.multiple_of(at * rounds, rounds), rounds)
        k = k_ref[:, window, :].reshape(size, width)
        v = v_ref[:, window, :].reshape(size, width)
        order = row_ref[at]
        allowed = (order <= top) & (order >= bottom)
        new_running, new_total = [], []
        for h in range(heads):
            scores = jnp.where(allowed, dot_nt(q_of[h], k), -1e30)
            peak = jnp.maximum(running[h], jnp.max(scores, axis=1, keepdims=True))
            probs = jnp.exp(scores - peak)
            scale = jnp.exp(running[h] - peak)
            new_running.append(peak)
            new_total.append(total[h] * scale + jnp.sum(probs, axis=1, keepdims=True))
            mixed = jnp.where(head_of == h, mixed * scale + dot_nn(probs.astype(BF), v), mixed)
        return (new_running, new_total, mixed)

    start = (
        [jnp.full((size, 1), -1e30, F32)] * heads,
        [jnp.zeros((size, 1), F32)] * heads,
        jnp.zeros((size, width), F32),
    )
    running, total, mixed = lax.fori_loop(0, block - low_ref[block] + 1, step, start)
    weight = jnp.zeros((size, width), F32)
    for h in range(heads):
        weight = jnp.where(head_of == h, 1.0 / total[h], weight)
    mixed = mixed * weight
    o_ref[...] = mixed.astype(BF).reshape(dealers, rounds, width)
    of_ref[...] = mixed.reshape(dealers, rounds, width)
    lse = [running[h] + jnp.log(total[h]) for h in range(heads)]
    lse_ref[...] = jnp.concatenate(lse, axis=1).reshape(dealers, rounds, heads)


def flash_forward_call(low, q, k, v, col, row, after=()):
    dealers, rows, width = q.shape
    rounds = 256 // dealers
    heads = width // HD
    part = lambda w: pl.BlockSpec((dealers, rounds, w), lambda i, low: (0, i, 0))
    whole = lambda shape: pl.BlockSpec(shape, lambda i, low: (0, 0, 0))
    return pl.pallas_call(
        behind(flash_forward, len(after), 1),
        name="flash_forward",
        cost_estimate=takes(21),
        grid_spec=pltpu.PrefetchScalarGridSpec(
            num_scalar_prefetch=1,
            grid=(rows // rounds,),
            in_specs=[HBM] * len(after)
            + [part(width), part(2), whole(row.shape), whole(k.shape), whole(v.shape)],
            out_specs=[part(width), part(width), part(heads)],
        ),
        out_shape=[
            jax.ShapeDtypeStruct(q.shape, BF),
            jax.ShapeDtypeStruct(q.shape, F32),
            jax.ShapeDtypeStruct((dealers, rows, heads), F32),
        ],
        compiler_params=pltpu.CompilerParams(vmem_limit_bytes=VMEM_BYTES),
    )(low, *after, q, col, row, k, v)


def flash_backward(
    low_ref, q_ref, da_ref, of_ref, lse_ref, col_ref, row_ref, k_ref, v_ref, cos_ref, sin_ref,
    d_ref, dk_acc, dv_acc,
):
    block = pl.program_id(0)
    dealers, rounds, width = q_ref.shape
    size = dealers * rounds
    heads = width // HD
    blocks = pl.num_programs(0)

    @pl.when(block == 0)
    def clear():
        dk_acc[...] = jnp.zeros_like(dk_acc)
        dv_acc[...] = jnp.zeros_like(dv_acc)

    q = q_ref[...].reshape(size, width)
    da = da_ref[...].reshape(size, width)
    col = col_ref[...].reshape(size, 2)
    lse = lse_ref[...].reshape(size, heads)
    top, bottom = col[:, 0:1], col[:, 1:2]
    head_of = lax.broadcasted_iota(jnp.int32, (size, width), 1) // HD
    product = da.astype(F32) * of_ref[...].reshape(size, width)
    q_of, da_of, delta = [], [], []
    for h in range(heads):
        q_of.append(jnp.where(head_of == h, q, jnp.zeros_like(q)))
        da_of.append(jnp.where(head_of == h, da, jnp.zeros_like(da)))
        delta.append(jnp.sum(jnp.where(head_of == h, product, 0.0), axis=1, keepdims=True))
    q_turned = q.astype(F32).T.astype(BF)
    da_turned = da.astype(F32).T.astype(BF)

    def step(at, dq):
        window = pl.ds(pl.multiple_of(at * rounds, rounds), rounds)
        k = k_ref[:, window, :].reshape(size, width)
        v = v_ref[:, window, :].reshape(size, width)
        order = row_ref[at]
        allowed = (order <= top) & (order >= bottom)
        for h in range(heads):
            scores = jnp.where(allowed, dot_nt(q_of[h], k), -1e30)
            probs = jnp.exp(scores - lse[:, h : h + 1])
            dprobs = dot_nt(da_of[h], v)
            dscores = (probs * (dprobs - delta[h])).astype(BF)
            own = slice(h * HD, (h + 1) * HD)
            dv_acc[at, own, :] += dot_nn(da_turned[own], probs.astype(BF))
            dk_acc[at, own, :] += dot_nn(q_turned[own], dscores)
            dq = jnp.where(head_of == h, dq + dot_nn(dscores, k), dq)
        return dq

    dq = lax.fori_loop(low_ref[block], block + 1, step, jnp.zeros((size, width), F32))

    def revert(grads, at):
        window = pl.ds(pl.multiple_of(at * rounds, rounds), rounds)
        cosine = wide(cos_ref[:, window, :].reshape(size, LANES), width)
        sine = wide(sin_ref[:, window, :].reshape(size, LANES), width)
        return grads * cosine - partner(grads) * sine

    def put(at, part, grads):
        window = pl.ds(pl.multiple_of(at * rounds, rounds), rounds)
        d_ref[:, window, part * width : (part + 1) * width] = grads.astype(BF).reshape(
            dealers, rounds, width
        )

    put(block, 0, revert(dq * 0.125, block))

    @pl.when(block == blocks - 1)
    def finish():
        def each(at, carry):
            put(at, 1, revert(dk_acc[at].T, at))
            put(at, 2, dv_acc[at].T)
            return carry

        lax.fori_loop(0, blocks, each, 0)


class CarriedBackward:
    def __init__(self, operands, d_ref, dk_acc, dv_acc):
        self.q, self.da, self.of, self.lse, self.col, self.row = operands[:6]
        self.k, self.v, self.cos, self.sin = operands[6:]
        self.d_ref, self.dk_acc, self.dv_acc = d_ref, dk_acc, dv_acc
        self.dealers, rows, self.width = self.q.shape
        self.rounds = 256 // self.dealers
        self.blocks = rows // self.rounds
        self.reach = self.dealers * rows // 2 // 256

    def window(self, at):
        return pl.ds(pl.multiple_of(at * self.rounds, self.rounds), self.rounds)

    def load(self, ref, at):
        return ref[:, self.window(at), :].reshape(256, ref.shape[2])

    def put(self, at, part, grads):
        span = slice(part * self.width, (part + 1) * self.width)
        grads = grads.astype(BF).reshape(self.dealers, self.rounds, self.width)
        self.d_ref[:, self.window(at), span] = grads

    def revert(self, grads, at):
        cosine = wide(self.load(self.cos, at), self.width)
        sine = wide(self.load(self.sin, at), self.width)
        return grads * cosine - partner(grads) * sine

    def clear(self):
        self.dk_acc[...] = jnp.zeros_like(self.dk_acc)
        self.dv_acc[...] = jnp.zeros_like(self.dv_acc)

    def block(self, block):
        size, heads = 256, self.width // HD
        q, da = self.load(self.q, block), self.load(self.da, block)
        col, lse = self.load(self.col, block), self.load(self.lse, block)
        top, bottom = col[:, 0:1], col[:, 1:2]
        head_of = lax.broadcasted_iota(jnp.int32, (size, self.width), 1) // HD
        product = da.astype(F32) * self.load(self.of, block)
        q_of, da_of, delta = [], [], []
        for h in range(heads):
            q_of.append(jnp.where(head_of == h, q, jnp.zeros_like(q)))
            da_of.append(jnp.where(head_of == h, da, jnp.zeros_like(da)))
            delta.append(jnp.sum(jnp.where(head_of == h, product, 0.0), axis=1, keepdims=True))
        q_turned = q.astype(F32).T.astype(BF)
        da_turned = da.astype(F32).T.astype(BF)

        def step(at, dq):
            k, v = self.load(self.k, at), self.load(self.v, at)
            order = self.row[at]
            allowed = (order <= top) & (order >= bottom)
            for h in range(heads):
                scores = jnp.where(allowed, dot_nt(q_of[h], k), -1e30)
                probs = jnp.exp(scores - lse[:, h : h + 1])
                dprobs = dot_nt(da_of[h], v)
                dscores = (probs * (dprobs - delta[h])).astype(BF)
                own = slice(h * HD, (h + 1) * HD)
                self.dv_acc[at, own, :] += dot_nn(da_turned[own], probs.astype(BF))
                self.dk_acc[at, own, :] += dot_nn(q_turned[own], dscores)
                dq = jnp.where(head_of == h, dq + dot_nn(dscores, k), dq)
            return dq

        lowest = jnp.maximum(block - self.reach, 0)
        dq = lax.fori_loop(lowest, block + 1, step, jnp.zeros((size, self.width), F32))
        self.put(block, 0, self.revert(dq * 0.125, block))

    def run(self, first, last):
        lax.fori_loop(first, last, lambda at, carry: (self.block(at), carry)[1], 0)

    def finish(self):
        def each(at, carry):
            self.put(at, 1, self.revert(self.dk_acc[at].T, at))
            self.put(at, 2, self.dv_acc[at].T)
            return carry

        lax.fori_loop(0, self.blocks, each, 0)


def flash_backward_call(low, q, da, of, lse, col, row, k, v, cosine, sine, after=()):
    dealers, rows, width = q.shape
    rounds = 256 // dealers
    heads = width // HD
    part = lambda w: pl.BlockSpec((dealers, rounds, w), lambda i, low: (0, i, 0))
    whole = lambda shape: pl.BlockSpec(shape, lambda i, low: (0, 0, 0))
    blocks = rows // rounds
    return pl.pallas_call(
        behind(flash_backward, len(after), 1),
        name="flash_backward",
        cost_estimate=takes(31),
        grid_spec=pltpu.PrefetchScalarGridSpec(
            num_scalar_prefetch=1,
            grid=(blocks,),
            in_specs=[HBM] * len(after)
            + [
                part(width), part(width), part(width), part(heads), part(2), whole(row.shape),
                whole(k.shape), whole(v.shape), whole(cosine.shape), whole(sine.shape),
            ],
            out_specs=whole((dealers, rows, 3 * width)),
            scratch_shapes=[pltpu.VMEM((blocks, width, 256), F32)] * 2,
        ),
        out_shape=jax.ShapeDtypeStruct((dealers, rows, 3 * width), BF),
        compiler_params=pltpu.CompilerParams(vmem_limit_bytes=VMEM_BYTES),
    )(low, *after, q, da, of, lse, col, row, k, v, cosine, sine)


MESH = pl.DeviceIdType.MESH
HBM = pl.BlockSpec(memory_space=pltpu.HBM)


def behind(kernel, waits, scalars=0):
    def run(*refs):
        kernel(*refs[:scalars], *refs[scalars + waits :])

    return run


def tie(value, *waits):
    def nothing(*refs):
        del refs

    return pl.pallas_call(
        nothing,
        name="tie",
        in_specs=[HBM] * (1 + len(waits)),
        out_specs=HBM,
        out_shape=jax.ShapeDtypeStruct(value.shape, value.dtype),
        input_output_aliases={0: 0},
    )(value, *waits)


def takes(microseconds):
    return pl.CostEstimate(
        flops=0, bytes_accessed=int(microseconds * 3.69e3), transcendentals=0
    )


def plane_neighbours(shard):
    return shard + 1 - 2 * (shard % 2), (shard + 2) % 4, 3 - shard


class PlaneGather:
    def __init__(self, out_ref, send_sem, recv_sem, base):
        self.out, self.send_sem, self.recv_sem, self.base = out_ref, send_sem, recv_sem, base
        self.shard = lax.axis_index("fsdp")
        self.half = out_ref.shape[1] // 2

    def copy(self, k, src, dst):
        x, y, _ = plane_neighbours(self.shard)
        return pltpu.make_async_remote_copy(
            src_ref=src,
            dst_ref=dst,
            send_sem=self.send_sem.at[self.base + k],
            recv_sem=self.recv_sem.at[self.base + k],
            device_id={"fsdp": x if k % 2 == 0 else y},
            device_id_type=MESH,
        )

    def part(self, slot, k):
        return self.out.at[slot, pl.ds((k % 2) * self.half, self.half)]

    def first(self, src):
        for k in range(2):
            self.copy(k, src, self.out.at[self.shard]).start()

    def forward(self):
        x, y, _ = plane_neighbours(self.shard)
        for k in range(2):
            self.copy(k, self.out.at[x], self.out.at[(x, y)[k]]).wait_recv()
        for k in range(2):
            piece = self.part((y, x)[k], k)
            self.copy(2 + k, piece, piece).start()

    def finish(self, src):
        x, y, across = plane_neighbours(self.shard)
        for k in range(2):
            self.copy(k, src, self.out.at[self.shard]).wait_send()
            piece = self.part((y, x)[k], k)
            self.copy(2 + k, piece, piece).wait_send()
            self.copy(2 + k, piece, self.part(across, k)).wait_recv()


def rows_of_orders(col_ref, row_ref):
    rounds = 256 // col_ref.shape[0]
    for at in range(row_ref.shape[0]):
        order = col_ref[:, at * rounds : (at + 1) * rounds, :].reshape(256, 2)[:, 0:1]
        order = jnp.broadcast_to(order.astype(F32), (256, LANES)).T[0:1]
        row_ref[at] = order.astype(jnp.int32)


class CarriedForward:
    def __init__(self, q_ref, k_ref, v_ref, col_ref, row_ref, o_ref, of_ref, lse_ref):
        self.q, self.k, self.v, self.col, self.row = q_ref, k_ref, v_ref, col_ref, row_ref
        self.o, self.of, self.lse = o_ref, of_ref, lse_ref
        self.dealers, rows, self.width = q_ref.shape
        self.rounds = 256 // self.dealers
        self.blocks = rows // self.rounds
        self.reach = self.dealers * rows // 2 // 256

    def window(self, at):
        return pl.ds(pl.multiple_of(at * self.rounds, self.rounds), self.rounds)

    def load(self, ref, at):
        return ref[:, self.window(at), :].reshape(256, ref.shape[2])

    def save(self, ref, at, value):
        ref[:, self.window(at), :] = value.reshape(self.dealers, self.rounds, ref.shape[2])

    def block(self, block):
        size, heads = 256, self.width // HD
        q, col = self.load(self.q, block), self.load(self.col, block)
        top, bottom = col[:, 0:1], col[:, 1:2]
        head_of = lax.broadcasted_iota(jnp.int32, (size, self.width), 1) // HD
        q_of = [jnp.where(head_of == h, q, jnp.zeros_like(q)) for h in range(heads)]

        def step(j, carry):
            at = block - j
            running, total, mixed = carry
            k, v = self.load(self.k, at), self.load(self.v, at)
            order = self.row[at]
            allowed = (order <= top) & (order >= bottom)
            new_running, new_total = [], []
            for h in range(heads):
                scores = jnp.where(allowed, dot_nt(q_of[h], k), -1e30)
                peak = jnp.maximum(running[h], jnp.max(scores, axis=1, keepdims=True))
                probs = jnp.exp(scores - peak)
                scale = jnp.exp(running[h] - peak)
                new_running.append(peak)
                new_total.append(total[h] * scale + jnp.sum(probs, axis=1, keepdims=True))
                mixed = jnp.where(head_of == h, mixed * scale + dot_nn(probs.astype(BF), v), mixed)
            return (new_running, new_total, mixed)

        start = (
            [jnp.full((size, 1), -1e30, F32)] * heads,
            [jnp.zeros((size, 1), F32)] * heads,
            jnp.zeros((size, self.width), F32),
        )
        steps = jnp.minimum(block, self.reach) + 1
        running, total, mixed = lax.fori_loop(0, steps, step, start)
        weight = jnp.zeros((size, self.width), F32)
        for h in range(heads):
            weight = jnp.where(head_of == h, 1.0 / total[h], weight)
        mixed = mixed * weight
        self.save(self.o, block, mixed.astype(BF))
        self.save(self.of, block, mixed)
        lse = [running[h] + jnp.log(total[h]) for h in range(heads)]
        self.save(self.lse, block, jnp.concatenate(lse, axis=1))

    def run(self, first, last):
        lax.fori_loop(first, last, lambda at, carry: (self.block(at), carry)[1], 0)


class LineSum:
    def __init__(self, turned, operands, out_ref, buffers):
        self.turned, self.out_ref = turned, out_ref
        self.a, self.b, self.wa, self.wb = operands
        self.mine, self.both, self.arrived, self.passing = buffers[:4]
        self.pair_send, self.pair_recv, self.line_send, self.line_recv = buffers[4:]
        self.me = lax.axis_index("ctx")
        self.chips, self.rows = self.mine.shape[:2]
        self.chip, self.core = self.me // 2, self.me % 2
        self.side = (2 * self.chip) // self.chips
        self.first = 0

    def goal(self, j):
        return (1 - self.side) * (self.chips - 1 - j) + self.side * j

    def products(self, j):
        goal, rows, tile = self.goal(j), self.rows, 1024
        pair = pl.ds(2 * goal, 2)
        a = self.a[pair].reshape(2 * rows, self.a.shape[2])
        b = self.b[pair].reshape(2 * rows, self.b.shape[2])

        def one(t, carry):
            span = pl.ds(pl.multiple_of(t * tile, tile), tile)
            if self.turned:
                value = dot_nt(a, self.wa[span, :]) + dot_nt(b, self.wb[span, :])
            else:
                value = dot_nn(a, self.wa[:, span]) + dot_nn(b, self.wb[:, span])
            self.both[j % 2, :, :, span] = value.astype(BF).reshape(2, rows, tile)
            return carry

        lax.fori_loop(0, D // tile, one, 0)

    def to_pair(self, j):
        return pltpu.make_async_remote_copy(
            src_ref=self.both.at[j % 2, 1 - self.core], dst_ref=self.arrived.at[self.goal(j)],
            send_sem=self.pair_send.at[j], recv_sem=self.pair_recv.at[j],
            device_id={"ctx": self.me + 1 - 2 * self.core}, device_id_type=MESH,
        )

    def add(self, goal, base, extra):
        def one(t, carry):
            span = pl.ds(pl.multiple_of(t * 16, 16), 16)
            value = base[span, :].astype(F32) + extra[span, :].astype(F32)
            self.mine[goal, span, :] = value.astype(BF)
            return carry

        lax.fori_loop(0, self.rows // 16, one, 0)

    def pairwise(self, j):
        if not isinstance(j, int):
            pl.when(j >= self.first + 2)(lambda: self.to_pair(j - 2).wait_send())
        self.products(j)
        self.to_pair(j).start()
        self.to_pair(j).wait_recv()
        goal = self.goal(j)
        self.add(goal, self.both.at[j % 2, self.core], self.arrived.at[goal])

    def way(self, way, s):
        last = self.chips - 1
        place = self.chip if way == 0 else last - self.chip
        goal = last - s + self.chip if way == 0 else s - (last - self.chip)
        copy = pltpu.make_async_remote_copy(
            src_ref=self.mine.at[goal], dst_ref=self.passing.at[way, s],
            send_sem=self.line_send.at[way, s], recv_sem=self.line_recv.at[way, s],
            device_id={"ctx": self.me + 2 if way == 0 else self.me - 2}, device_id_type=MESH,
        )
        return place, goal, copy

    def coming(self, way, s):
        return pltpu.make_async_remote_copy(
            src_ref=self.mine.at[self.chip], dst_ref=self.passing.at[way, s],
            send_sem=self.line_send.at[way, s], recv_sem=self.line_recv.at[way, s],
            device_id={"ctx": self.me - 2 if way == 0 else self.me + 2}, device_id_type=MESH,
        )

    def start(self, s):
        for way in range(2):
            place, _, copy = self.way(way, s)
            pl.when(place == 0)(copy.start)

    def relay(self, s):
        for way in range(2):
            place, goal, copy = self.way(way, s)

            @pl.when((place > 0) & (place <= s))
            def later(way=way, goal=goal, copy=copy):
                self.coming(way, s - 1).wait_recv()
                self.add(goal, self.mine.at[goal], self.passing.at[way, s - 1])
                copy.start()

    def last(self):
        for way in range(2):
            place = self.chip if way == 0 else self.chips - 1 - self.chip
            copy = self.coming(way, self.chips - 2)
            pl.when(place > 0)(copy.wait_recv)

        def one(t, carry):
            span = pl.ds(pl.multiple_of(t * 16, 16), 16)
            self.out_ref[span, :] = self.mine[self.chip, span, :].astype(F32)
            for way in range(2):
                place = self.chip if way == 0 else self.chips - 1 - self.chip

                @pl.when(place > 0)
                def more(way=way):
                    value = self.passing[way, self.chips - 2, span, :]
                    self.out_ref[span, :] += value.astype(F32)

            return carry

        lax.fori_loop(0, self.rows // 16, one, 0)

    def drain(self):
        for j in range(self.chips - 2, self.chips):
            self.to_pair(j).wait_send()
        for s in range(self.chips - 1):
            for way in range(2):
                place, _, copy = self.way(way, s)
                pl.when(place <= s)(copy.wait_send)


class LineGather:
    def __init__(self, own_ref, out_ref, line_send, line_recv, pair_send, pair_recv, keep_sem):
        self.own_ref, self.out_ref = own_ref, out_ref
        self.line_send, self.line_recv = line_send, line_recv
        self.pair_send, self.pair_recv, self.keep_sem = pair_send, pair_recv, keep_sem
        self.me = lax.axis_index("ctx")
        self.chips = out_ref.shape[0] // 2
        self.chip, self.core = self.me // 2, self.me % 2

    def place(self, way):
        return self.chip if way == 0 else self.chips - 1 - self.chip

    def slot(self, way, h):
        return self.me - 2 * h if way == 0 else self.me + 2 * h

    def on(self, way, h):
        slot = self.slot(way, h)
        src = self.own_ref if h == 0 else self.out_ref.at[slot]
        return pltpu.make_async_remote_copy(
            src_ref=src, dst_ref=self.out_ref.at[slot],
            send_sem=self.line_send.at[way, h], recv_sem=self.line_recv.at[way, h],
            device_id={"ctx": self.me + 2 if way == 0 else self.me - 2}, device_id_type=MESH,
        )

    def arriving(self, way, h):
        slot = self.slot(way, h)
        return pltpu.make_async_remote_copy(
            src_ref=self.own_ref, dst_ref=self.out_ref.at[slot],
            send_sem=self.line_send.at[way, h - 1], recv_sem=self.line_recv.at[way, h - 1],
            device_id={"ctx": self.me - 2 if way == 0 else self.me + 2}, device_id_type=MESH,
        )

    def across(self, chip, slot, src):
        return pltpu.make_async_remote_copy(
            src_ref=src, dst_ref=self.out_ref.at[slot],
            send_sem=self.pair_send.at[chip], recv_sem=self.pair_recv.at[chip],
            device_id={"ctx": self.me + 1 - 2 * self.core}, device_id_type=MESH,
        )

    def keep(self):
        return pltpu.make_async_copy(self.own_ref, self.out_ref.at[self.me], self.keep_sem)

    def start(self):
        for place in range(self.chips - 1):
            self.launch(place)
        self.stay()

    def launch(self, place):
        for way in range(2):
            pl.when(self.place(way) == place)(self.on(way, 0).start)

    def stay(self):
        self.across(self.chip, self.me, self.own_ref).start()
        self.keep().start()

    def step(self, h):
        for way in range(2):

            @pl.when(self.place(way) >= h)
            def come(way=way):
                self.arriving(way, h).wait_recv()
                pl.when(self.place(way) < self.chips - 1)(self.on(way, h).start)
                slot = self.slot(way, h)
                self.across(slot // 2, slot, self.out_ref.at[slot]).start()

    def come(self, chip):
        slot = 2 * chip + 1 - self.core
        self.across(chip, slot, self.out_ref.at[slot]).wait_recv()

    def finish(self, came=False):
        for h in range(self.chips - 1):
            for way in range(2):
                pl.when((self.place(way) < self.chips - 1) & (self.place(way) >= h))(
                    self.on(way, h).wait_send
                )
        for chip in range(self.chips):
            slot = 2 * chip + self.core
            self.across(chip, slot, self.out_ref.at[slot]).wait_send()
            if not came:
                self.come(chip)
        if not came:
            self.keep().wait()


def greet_all(across=False):
    me = lax.axis_index("ctx")
    chips = lax.axis_size("ctx") // 2
    chip = me // 2
    barrier = pltpu.get_barrier_semaphore()
    x, y, far = plane_neighbours(lax.axis_index("fsdp"))
    greet = lambda axis, who: pl.semaphore_signal(
        barrier, inc=1, device_id={axis: who}, device_id_type=MESH
    )
    greet("fsdp", x)
    greet("fsdp", y)
    if across:
        greet("fsdp", far)
    greet("ctx", me + 1 - 2 * (me % 2))
    pl.when(chip > 0)(lambda: greet("ctx", me - 2))
    pl.when(chip < chips - 1)(lambda: greet("ctx", me + 2))
    plane = 3 if across else 2
    line = 1 + (chip + chips - 1) // chips + (2 * chips - 2 - chip) // chips
    pl.semaphore_wait(barrier, plane + line)


def greet_line():
    me = lax.axis_index("ctx")
    chips = lax.axis_size("ctx") // 2
    chip = me // 2
    barrier = pltpu.get_barrier_semaphore()
    greet = lambda who: pl.semaphore_signal(
        barrier, inc=1, device_id={"ctx": who}, device_id_type=MESH
    )
    greet(me + 1 - 2 * (me % 2))
    pl.when(chip > 0)(lambda: greet(me - 2))
    pl.when(chip < chips - 1)(lambda: greet(me + 2))
    pl.semaphore_wait(barrier, 1 + (chip + chips - 1) // chips + (2 * chips - 2 - chip) // chips)


class Staged:
    def __init__(self, hbm_refs, vmem_refs, sem):
        self.copies = [
            pltpu.make_async_copy(src, dst, sem.at[i])
            for i, (src, dst) in enumerate(zip(hbm_refs, vmem_refs))
        ]

    def start(self):
        for copy in self.copies:
            copy.start()

    def wait(self, first, last):
        for copy in self.copies[first:last]:
            copy.wait()


class PlaneSum:
    def __init__(self, sent, come, send_sem, recv_sem):
        self.sent, self.come, self.send_sem, self.recv_sem = sent, come, send_sem, recv_sem
        self.shard, self.half = lax.axis_index("fsdp"), sent.shape[1] // 2

    def owner(self, r):
        across_x = (self.shard % 2 + r % 2) % 2
        across_y = (self.shard // 2 + r // 2) % 2
        return 2 * across_y + across_x

    def part(self, ref, slot, lower):
        return ref.at[slot, pl.ds(lower * self.half, self.half)]

    def copy(self, i):
        block, slot, lower, along = (
            (1, 0, 0, 0), (3, 1, 0, 0), (2, 0, 1, 1), (3, 1, 1, 1), (2, 2, 0, 1), (1, 2, 1, 0),
        )[i]
        x, y, _ = plane_neighbours(self.shard)
        return pltpu.make_async_remote_copy(
            src_ref=self.part(self.sent, block, lower), dst_ref=self.part(self.come, slot, lower),
            send_sem=self.send_sem.at[i], recv_sem=self.recv_sem.at[i],
            device_id={"fsdp": y if along else x}, device_id_type=MESH,
        )

    def fill(self, block):
        def one(r, carry):
            self.sent[r] = block(self.owner(r))
            return carry

        lax.fori_loop(0, self.sent.shape[0], one, 0)

    def start(self):
        for i in range(4):
            self.copy(i).start()

    def add(self, block, slot, lower):
        def one(t, carry):
            span = pl.ds(pl.multiple_of(lower * self.half + t * 16, 16), 16)
            value = self.sent[block, span, :].astype(F32) + self.come[slot, span, :].astype(F32)
            self.sent[block, span, :] = value.astype(BF)
            return carry

        lax.fori_loop(0, self.half // 16, one, 0)

    def relay(self):
        for lower, passed in ((0, 2), (1, 1)):
            self.copy(2 * lower + 1).wait_recv()
            self.add(passed, 1, lower)
            self.copy(4 + lower).start()
            self.copy(2 * lower).wait_recv()
            self.add(0, 0, lower)

    def total(self, target):
        for i in (4, 5):
            self.copy(i).wait_recv()

        def add(t, carry):
            span = pl.ds(pl.multiple_of(t * 16, 16), 16)
            value = self.sent[0, span, :].astype(F32) + self.come[2, span, :].astype(F32)
            target[span, :] = value.astype(BF)
            return carry

        lax.fori_loop(0, 2 * self.half // 16, add, 0)

    def drain(self):
        for i in range(6):
            self.copy(i).wait_send()


def plane_scratch(shards, rows, columns):
    sem = pltpu.SemaphoreType.DMA((6,))
    return [
        pltpu.VMEM((shards, rows, columns), BF), pltpu.VMEM((3, rows, columns), BF), sem, sem,
    ]


def line_scratch(chips, rows):
    return [
        pltpu.VMEM((chips, rows, D), BF),
        pltpu.VMEM((2, 2, rows, D), BF),
        pltpu.VMEM((chips, rows, D), BF),
        pltpu.VMEM((2, chips - 1, rows, D), BF),
        pltpu.SemaphoreType.DMA((chips,)),
        pltpu.SemaphoreType.DMA((chips,)),
        pltpu.SemaphoreType.DMA((2, chips - 1)),
        pltpu.SemaphoreType.DMA((2, chips - 1)),
    ]


def gather_scratch(chips):
    line = pltpu.SemaphoreType.DMA((2, chips - 1))
    pair = pltpu.SemaphoreType.DMA((chips,))
    return [line, line, pair, pair, pltpu.SemaphoreType.DMA]


def taker(refs):
    refs = list(refs)

    def take(count):
        taken = refs[:count]
        del refs[:count]
        return taken

    return take


def sum_out(own_ref, *refs):
    take = taker(refs)
    (far,), given = take(1), take(14)
    out_ref, all_ref, d_ref = take(3)
    line, gathering, held, (stage_sem, far_sem), accs = take(8), take(5), take(14), take(2), take(2)
    staged = Staged(given, held, stage_sem)
    job = LineSum(False, held[:4], out_ref, line)
    job.first = 1
    ready = pltpu.make_async_copy(far, job.mine.at[job.goal(0)], far_sem)
    gather = LineGather(own_ref, all_ref, *gathering)
    back = CarriedBackward(held[4:], d_ref, *accs)
    chips = job.chips
    ready.start()
    staged.start()
    greet_line()
    gather.start()
    ready.wait()
    job.start(0)
    staged.wait(0, 4)
    lax.fori_loop(1, chips, lambda j, carry: (job.pairwise(j), carry)[1], 0)
    for s in range(1, chips - 1):
        job.start(s)
    staged.wait(4, 14)
    back.clear()
    half, late = back.blocks // 2, back.blocks - 1
    gather.step(1)
    back.run(0, half)
    for s in range(1, chips - 2):
        job.relay(s)
        gather.step(s + 1)
    back.run(half, late)
    if chips > 2:
        job.relay(chips - 2)
    back.run(late, back.blocks)
    if chips > 2:
        gather.step(chips - 1)
    back.finish()
    job.last()
    job.drain()
    gather.finish()


def sum_out_call(own, far, operands, carried):
    dealers, rows, _ = operands[0].shape
    chips, width = dealers // 2, carried[0].shape[2]
    vmem = pl.BlockSpec(memory_space=pltpu.VMEM)
    given = (*operands, *carried)
    return pl.pallas_call(
        sum_out,
        name="sum_out",
        in_specs=[HBM] * (2 + len(given)),
        out_specs=[vmem, HBM, vmem],
        out_shape=[
            jax.ShapeDtypeStruct((rows, D), F32),
            jax.ShapeDtypeStruct((dealers,) + own.shape, own.dtype),
            jax.ShapeDtypeStruct((dealers, rows, 3 * width), BF),
        ],
        scratch_shapes=line_scratch(chips, rows)
        + gather_scratch(chips)
        + [pltpu.VMEM(value.shape, value.dtype) for value in given]
        + [pltpu.SemaphoreType.DMA((len(given),)), pltpu.SemaphoreType.DMA]
        + [pltpu.VMEM((dealers * rows // 256, width, 256), F32)] * 2,
        compiler_params=pltpu.CompilerParams(
            collective_id=2, has_side_effects=True, vmem_limit_bytes=VMEM_BYTES
        ),
    )(own, far, *given)


def sum_back(own_ref, *refs):
    take = taker(refs)
    given = take(5)
    out_ref, all_ref, qkv_ref = take(3)
    line, gathering, held, (stage_sem,), plane = take(8), take(5), take(5), take(1), take(4)
    staged = Staged(given, held, stage_sem)
    job = LineSum(True, held[:4], out_ref, line)
    gather = LineGather(own_ref, all_ref, *gathering)
    weights = PlaneSum(*plane)
    chips = job.chips
    d_qkv, normed = held[0], held[4]
    staged.start()
    greet_all()
    gather.start()
    staged.wait(0, 4)
    job.pairwise(0)
    job.start(0)
    lax.fori_loop(1, chips, lambda j, carry: (job.pairwise(j), carry)[1], 0)
    for s in range(1, chips - 1):
        job.start(s)
    staged.wait(4, 5)
    lines = qkv_ref.shape[0]
    grads = d_qkv[...].reshape(normed.shape[0], d_qkv.shape[2])

    def block(owner):
        span = pl.ds(pl.multiple_of(owner * lines, lines), lines)
        return dot_tn(normed[:, span], grads).astype(BF)

    gather.step(1)
    if chips > 2:
        job.relay(1)
    weights.fill(block)
    weights.start()
    for s in range(2, chips):
        gather.step(s)
        if s == 2:
            weights.relay()
        if s < chips - 1:
            job.relay(s)
    weights.total(qkv_ref)
    job.last()
    job.drain()
    gather.finish()
    weights.drain()


def sum_back_call(shards, own, operands, normed, after=()):
    dealers, rows, width = operands[0].shape
    chips = dealers // 2
    vmem = pl.BlockSpec(memory_space=pltpu.VMEM)
    given = (*operands, normed)
    return pl.pallas_call(
        behind(sum_back, len(after)),
        name="sum_back",
        in_specs=[HBM] * (len(after) + 1 + len(given)),
        out_specs=[vmem, HBM, vmem],
        out_shape=[
            jax.ShapeDtypeStruct((rows, D), F32),
            jax.ShapeDtypeStruct((dealers,) + own.shape, own.dtype),
            jax.ShapeDtypeStruct((D // shards, width), BF),
        ],
        scratch_shapes=line_scratch(chips, rows)
        + gather_scratch(chips)
        + [pltpu.VMEM(value.shape, value.dtype) for value in given]
        + [pltpu.SemaphoreType.DMA((len(given),))]
        + plane_scratch(shards, D // shards, width),
        compiler_params=pltpu.CompilerParams(
            collective_id=3, has_side_effects=True, vmem_limit_bytes=VMEM_BYTES
        ),
    )(*after, own, *given)


class Rows:
    def __init__(self, src_ref, dst_ref, sem):
        self.src, self.dst, self.sem = src_ref, dst_ref, sem

    def copy(self, chip):
        span = pl.ds(2 * chip, 2)
        return pltpu.make_async_copy(self.src.at[span], self.dst.at[span], self.sem.at[chip])

    def finish(self):
        for chip in range(self.src.shape[0] // 2):
            self.copy(chip).wait()


def paired(left, right, odd):
    lane = lax.broadcasted_iota(jnp.int32, left.shape, 1)
    left = jnp.where(odd, pltpu.roll(left, HD, 1), left)
    right = jnp.where(odd, right, pltpu.roll(right, HD, 1))
    return jnp.where(lane < HD, left, right)


def phase_one(*refs):
    take = taker(refs)
    lengths, order_ref, turn_ref = take(3)
    vectors = take(8)
    x_hbm, dy_hbm, w_qkv, w_up, w_out, w_down = take(6)
    small, col_ref, row_ref, attn_ref, attn_f_ref, lse_ref = take(6)
    q_out, k_out, v_out, cos_out, sin_out = take(5)
    normed_out, act_out, slope_out, dy_out, qkv_out, up_out, wo_out, wd_out = take(8)
    q_ref, k_ref, v_ref, cos_ref, sin_ref = take(5)
    x_all, normed, act, slope, qkv, up, raw, dy_raw, dy_own, small_own = take(10)
    tile_sem, up_sem, own_sem, send_sem, recv_sem, keep_sem = take(6)
    normed_sem, act_sem, slope_sem, q_sem, k_sem, v_sem = take(6)
    x_sems, dy_sems = take(5), take(5)
    me, shard = lax.axis_index("ctx"), lax.axis_index("fsdp")
    dealers, rows, width = q_ref.shape
    chips, shards, units = dealers // 2, qkv.shape[0], act.shape[2]
    unit, heads, lines = units // shards, wo_out.shape[1], wd_out.shape[1]
    odd = me % 2 == 1

    tiles = []
    for i in range(3 * shards):
        column = (i // shards) * D + (i % shards) * (D // shards) + (me // 2) * LANES
        tiles.append(
            pltpu.make_async_copy(
                w_qkv.at[:, pl.ds(pl.multiple_of(column, LANES), LANES)],
                raw.at[:, pl.ds(i * LANES, LANES)],
                tile_sem.at[i],
            )
        )
    slices = []
    for j in range(shards):
        column = pl.multiple_of(j * (FF // shards) + me * unit, LANES)
        slices.append(
            pltpu.make_async_copy(
                w_up.at[:, pl.ds(column, unit)],
                up.at[shard, :, pl.ds(j * unit, unit)],
                up_sem.at[j],
            )
        )
    load_dy = pltpu.make_async_copy(dy_hbm, dy_raw, own_sem.at[0])
    wo_own = w_out.at[pl.ds(me * heads, heads)]
    wd_own = w_down.at[pl.ds(me * lines, lines)]
    owns = [
        pltpu.make_async_copy(wo_own, wo_out.at[shard], own_sem.at[1]),
        pltpu.make_async_copy(wd_own, wd_out.at[shard], own_sem.at[2]),
    ]
    for copy in (*tiles, *slices, load_dy):
        copy.start()
    x = LineGather(x_hbm, x_all, *x_sems)
    dy = LineGather(dy_own, dy_out, *dy_sems)
    gathers = [
        PlaneGather(out, send_sem, recv_sem, 4 * i)
        for i, out in enumerate((small, qkv, up, wd_out, wo_out))
    ]
    small_gather, qkv_gather, up_gather, wd_gather, wo_gather = gathers
    greet_all()
    x.start()

    at, starts = 0, []
    for vector in vectors:
        starts.append(at)
        small_own[at : at + vector.shape[0], :] = vector[...].astype(F32)
        at += vector.shape[0]
    small_own[at:, :] = jnp.zeros((small_own.shape[0] - at, LANES), F32)
    small[shard] = small_own[...]
    small_gather.first(small_own)
    for tile in tiles:
        tile.wait()
    for i in range(3 * shards // 2):
        left = raw[:, 2 * i * LANES : (2 * i + 1) * LANES].astype(F32)
        right = raw[:, (2 * i + 1) * LANES : (2 * i + 2) * LANES].astype(F32)
        qkv[shard, :, i * LANES : (i + 1) * LANES] = paired(left, right, odd).astype(BF)
    qkv_gather.first(qkv.at[shard])
    for own in owns:
        own.start()

    place = lax.broadcasted_iota(jnp.int32, (rows, rows), 0)
    load_dy.wait()
    pick = jnp.where(order_ref[me] // dealers == place, 1.0, 0.0).astype(BF)
    dy_own[...] = dot_nn(pick, dy_raw[...]).astype(BF)

    def tables(dealer, carry):
        order_row = order_ref[dealer]
        chosen = order_row // dealers == place
        order = jnp.sum(jnp.where(chosen, order_row.astype(F32), 0.0), axis=1, keepdims=True)
        order = order.astype(jnp.int32)
        start = jnp.zeros_like(order)
        bound = 0
        for i in range(lengths.shape[1]):
            start = jnp.where(order >= bound, bound, start)
            bound = bound + lengths[0, i]
        col_ref[dealer] = jnp.concatenate([order, start], axis=1)
        angles = (order - start).astype(F32) * turn_ref[0:1]
        cos_ref[dealer] = jnp.cos(angles)
        sin_ref[dealer] = jnp.sin(angles) * turn_ref[1:2]
        return carry

    small_gather.forward()
    lax.fori_loop(0, dealers, tables, 0)
    rows_of_orders(col_ref, row_ref)
    turned = [
        pltpu.make_async_copy(cos_ref, cos_out, keep_sem.at[2]),
        pltpu.make_async_copy(sin_ref, sin_out, keep_sem.at[3]),
    ]
    for copy in turned:
        copy.start()
    small_gather.finish(small_own)

    def line(base, count):
        return jnp.concatenate(
            [small[j, base + i : base + i + 1, :] for j in range(shards) for i in range(count)], axis=1
        )

    def heads_of(base):
        row = pl.ds(base + me // 2, 1)
        return [paired(small[j, row, :], small[j + 1, row, :], odd) for j in range(0, shards, 2)]

    def turned_heads(base):
        lane = lax.broadcasted_iota(jnp.int32, (1, LANES), 1)
        found = []
        for j in range(shards):
            value = small[j, pl.ds(base + me * ROT // LANES, 1), :]
            moved = jnp.zeros_like(value)
            for i in range(LANES // ROT):
                here = me % (LANES // ROT) == i
                moved = jnp.where(here, pltpu.roll(value, (LANES - i * ROT) % LANES, 1), moved)
            moved = jnp.where(lane < ROT, moved, 0.0)
            found.append(pltpu.roll(moved, HD, 1) if j % 2 else moved)
        return [found[j] + found[j + 1] for j in range(0, shards, 2)]

    gain, shift = line(starts[0], 4), line(starts[1], 4)
    bias = jnp.concatenate(heads_of(starts[2]) + turned_heads(starts[3]) + heads_of(starts[4]), axis=1)
    up_bias = jnp.concatenate(
        [
            small[j, pl.ds(starts[6] + me * (unit // LANES) + i, 1), :]
            for j in range(shards)
            for i in range(unit // LANES)
        ],
        axis=1,
    )

    chip = me // 2
    side = (2 * chip) // chips
    near = (1 - side) * chip + side * (chips - 1 - chip)

    def nth(j):
        zigzag = near + j // 2 if j % 2 == 0 else near - (j + 1) // 2
        close = (2 * near - j + 2 * chips) // (2 * chips)
        found = close * zigzag + (1 - close) * j
        return (1 - side) * found + side * (chips - 1 - found)

    qkv_w = qkv.reshape(D, 3 * width)
    up_w = up.reshape(D, units)
    normed_rows = Rows(normed, normed_out, normed_sem)
    act_rows, slope_rows = Rows(act, act_out, act_sem), Rows(slope, slope_out, slope_sem)
    projected_rows = [
        Rows(q_ref, q_out, q_sem), Rows(k_ref, k_out, k_sem), Rows(v_ref, v_out, v_sem),
    ]

    def project(j):
        def one(core, carry):
            dealer = 2 * nth(j) + core
            chosen = order_ref[dealer] // dealers == place
            value = dot_nn(jnp.where(chosen, 1.0, 0.0).astype(BF), x_all[dealer])
            mean = jnp.mean(value, axis=1, keepdims=True)
            centered = value - mean
            variance = jnp.mean(centered * centered, axis=1, keepdims=True)
            value = centered * lax.rsqrt(variance + 1e-05) * gain + shift
            normed[dealer] = value.astype(BF)
            projected = dot_nn(normed[dealer], qkv_w[...]) + bias
            cosine, sine = wide(cos_ref[dealer], width), wide(sin_ref[dealer], width)
            q = projected[:, :width]
            k = projected[:, width : 2 * width]
            q = (q * cosine + partner(q) * sine).astype(BF)
            q_ref[dealer] = (q.astype(F32) * 0.125).astype(BF)
            k_ref[dealer] = (k * cosine + partner(k) * sine).astype(BF)
            v_ref[dealer] = projected[:, 2 * width :].astype(BF)
            return carry

        if j == 0:
            x.keep().wait()
        x.come(nth(j))
        lax.fori_loop(0, 2, one, 0)
        for kept in (normed_rows, *projected_rows):
            kept.copy(nth(j)).start()

    def expand(at, carry):
        pair = pl.ds(2 * at, 2)
        hidden = dot_nn(normed[pair].reshape(2 * rows, D), up_w[...]) + up_bias
        square = hidden * hidden
        factor = 0.7978845608028654
        bent = jnp.tanh(factor * (hidden + 0.044715 * (hidden * square)))
        half = 0.5 * (1.0 + bent)
        act[pair] = (hidden * half).astype(BF).reshape(2, rows, units)
        grad = half + 0.5 * hidden * (1.0 - bent * bent) * (
            factor * (1.0 + 3.0 * 0.044715 * square)
        )
        slope[pair] = grad.astype(BF).reshape(2, rows, units)
        act_rows.copy(at).start()
        slope_rows.copy(at).start()
        return carry

    for copy in slices:
        copy.wait()
    x.step(1)
    dy.stay()
    dy.launch(0)
    qkv_gather.forward()
    up_gather.first(up.at[shard])
    qkv_gather.finish(qkv.at[shard])
    project(0)
    if chips > 2:
        x.step(2)
        dy.launch(1)
    for j in range(1, chips - 1):
        project(j)
    up_gather.forward()
    wd_gather.first(wd_own)
    wo_gather.first(wo_own)
    for h in range(3, chips):
        x.step(h)
        dy.launch(h - 1)
    project(chips - 1)
    x.finish(True)
    up_gather.finish(up.at[shard])
    keeps = [
        pltpu.make_async_copy(qkv, qkv_out, keep_sem.at[0]),
        pltpu.make_async_copy(up, up_out, keep_sem.at[1]),
    ]
    for keep in keeps:
        keep.start()
    flash = CarriedForward(q_ref, k_ref, v_ref, col_ref, row_ref, attn_ref, attn_f_ref, lse_ref)
    cut = flash.blocks // 2
    lax.fori_loop(0, chips // 2, expand, 0)
    dy.step(1)
    lax.fori_loop(chips // 2, chips, expand, 0)
    flash.run(0, cut)
    for h in range(2, chips - 1):
        dy.step(h)
    wd_gather.forward()
    wo_gather.forward()
    flash.run(cut, flash.blocks - 1)
    dy.step(chips - 1)
    flash.run(flash.blocks - 1, flash.blocks)
    dy.finish()
    wd_gather.finish(wd_own)
    wo_gather.finish(wo_own)
    for copy in (*owns, *keeps, *turned):
        copy.wait()
    for kept in (normed_rows, act_rows, slope_rows, *projected_rows):
        kept.finish()


def phase_one_call(shards, lengths, order, turn, vectors, x, dy, w_qkv, w_up, w_out, w_down):
    dealers, _, rows = order.shape
    chips, blocks = dealers // 2, dealers * rows // 256
    width, units, lines = D // dealers, FF // dealers, D // shards
    vmem = pl.BlockSpec(memory_space=pltpu.VMEM)
    out = lambda kind, *shape: jax.ShapeDtypeStruct(shape, kind)
    small = sum(vector.shape[0] for vector in vectors)
    small += -small % 16
    per_row = lambda kind, w: out(kind, dealers, rows, w)
    dma = lambda *shape: pltpu.SemaphoreType.DMA(shape)
    return pl.pallas_call(
        phase_one,
        name="phase_one",
        in_specs=[pl.BlockSpec(memory_space=pltpu.SMEM)] + [vmem] * 10 + [HBM] * 6,
        out_specs=[vmem] * 6 + [HBM] * 13,
        out_shape=[
            out(F32, shards, small, LANES), per_row(jnp.int32, 2), out(jnp.int32, blocks, 1, 256),
            per_row(BF, width), per_row(F32, width), per_row(F32, width // HD),
            per_row(BF, width), per_row(BF, width), per_row(BF, width),
            per_row(F32, LANES), per_row(F32, LANES),
            per_row(BF, D), per_row(BF, units), per_row(BF, units), per_row(BF, D),
            out(BF, shards, lines, 3 * width), out(BF, shards, lines, units),
            out(BF, shards, width // shards, D), out(BF, shards, units // shards, D),
        ],
        scratch_shapes=[pltpu.VMEM((dealers, rows, width), BF)] * 3
        + [pltpu.VMEM((dealers, rows, LANES), F32)] * 2
        + [
            pltpu.VMEM((dealers, rows, D), BF), pltpu.VMEM((dealers, rows, D), BF),
            pltpu.VMEM((dealers, rows, units), BF), pltpu.VMEM((dealers, rows, units), BF),
            pltpu.VMEM((shards, lines, 3 * width), BF), pltpu.VMEM((shards, lines, units), BF),
            pltpu.VMEM((lines, 3 * shards * LANES), BF),
            pltpu.VMEM((rows, D), BF), pltpu.VMEM((rows, D), BF), pltpu.VMEM((small, LANES), F32),
            dma(3 * shards), dma(shards), dma(3), dma(20), dma(20), dma(4),
        ]
        + [dma(chips)] * 6
        + gather_scratch(chips)
        + gather_scratch(chips),
        compiler_params=pltpu.CompilerParams(
            collective_id=0, has_side_effects=True, vmem_limit_bytes=VMEM_BYTES
        ),
    )(lengths, order, turn, *vectors, x, dy, w_qkv, w_up, w_out, w_down)


def hidden_grads(*refs):
    take = taker(refs)
    given = take(7)
    d_attn_ref, second_ref, d_up_out, d_hidden_out, far_out, first_all, out_all = take(7)
    d_up_ref, d_hidden_ref = take(2)
    held, (stage_sem, up_sem, keep_sem) = take(7), take(3)
    *parts, out_sum = [PlaneSum(*take(4)) for _ in range(3)]
    first_ref, out_own, d_out = take(3)
    far, (far_send, far_recv) = take(3), take(2)
    dy, attn, act, wo, wd, slope, normed = held
    units, half = first_ref.shape
    count, shards = dy.shape[0], parts[0].sent.shape[0]
    staged = Staged(given, held, stage_sem)
    gather = LineGather(first_ref, first_all, *take(5))
    out_gather = LineGather(out_own, out_all, *take(5))
    chips = gather.chips
    width, dealers = attn.shape[1], 2 * chips
    rows = count // dealers
    job = LineSum(
        False,
        (attn.reshape(dealers, rows, width), act.reshape(dealers, rows, act.shape[1]), wo, wd),
        None,
        (*far, None, far_send, far_recv, None, None),
    )
    staged.start()
    greet_all()
    staged.wait(0, 2)

    def down_block(part):
        columns = slice(0, half) if part == 0 else slice(half, D)

        def block(owner):
            span = pl.ds(pl.multiple_of(owner * units, units), units)
            return dot_tn(act[:, span], dy[:, columns]).astype(BF)

        return block

    some = count // chips

    def attn_rows(t, carry):
        span = pl.ds(pl.multiple_of(t * some, some), some)
        d_attn_ref[span, :] = dot_nt(dy[span, :], wo[...]).astype(BF)
        return carry

    def hidden_rows(t, carry):
        span = pl.ds(pl.multiple_of(t * some, some), some)
        value = dot_nt(dy[span, :], wd[...]) * slope[span, :].astype(F32)
        d_hidden_ref[span, :] = value.astype(BF)
        return carry

    lines = normed.shape[1] // shards

    def up_rows(t, carry):
        span = pl.ds(pl.multiple_of(t * lines, lines), lines)
        value = dot_tn(normed[:, span], d_hidden_ref[...])
        d_up_ref[t] = value.astype(BF)
        leave_up(t).start()
        return carry

    def leave_up(t):
        return pltpu.make_async_copy(d_up_ref.at[t], d_up_out.at[t], up_sem.at[t])

    piece = attn.shape[1] // shards

    def out_block(owner):
        return d_out[pl.ds(pl.multiple_of(owner * piece, piece), piece), :]

    d_out[...] = dot_tn(attn[...], dy[...]).astype(BF)
    out_sum.fill(out_block)
    out_sum.start()
    staged.wait(2, 3)
    parts[0].fill(down_block(0))
    out_sum.relay()
    parts[0].start()
    parts[1].fill(down_block(1))
    out_sum.total(out_own)
    out_gather.start()
    staged.wait(3, 4)
    lax.fori_loop(0, chips, attn_rows, 0)
    parts[0].relay()
    parts[1].start()
    staged.wait(4, 6)
    out_gather.step(1)
    lax.fori_loop(0, chips // 2, hidden_rows, 0)
    parts[0].total(first_ref)
    gather.start()
    lax.fori_loop(chips // 2, chips, hidden_rows, 0)
    leave_hidden = pltpu.make_async_copy(d_hidden_ref, d_hidden_out, keep_sem.at[0])
    leave_hidden.start()
    for h in range(2, chips - 1):
        out_gather.step(h)
    job.pairwise(0)
    leave_far = pltpu.make_async_copy(job.mine.at[job.goal(0)], far_out, keep_sem.at[1])
    leave_far.start()
    parts[1].relay()
    staged.wait(6, 7)
    lax.fori_loop(0, shards // 2, up_rows, 0)
    out_gather.step(chips - 1)
    gather.step(1)
    lax.fori_loop(shards // 2, shards, up_rows, 0)
    for h in range(2, chips - 1):
        gather.step(h)
    parts[1].total(second_ref)
    gather.step(chips - 1)
    out_sum.drain()
    out_gather.finish()
    job.to_pair(0).wait_send()
    for copy in (leave_hidden, leave_far, *(leave_up(t) for t in range(shards))):
        copy.wait()
    for part in parts:
        part.drain()
    gather.finish()


def hidden_grads_call(shards, dy, attn, act, wo, wd, slope, normed):
    count, units = act.shape
    width = wo.shape[0]
    dealers = FF // units
    chips, rows, unit, first = dealers // 2, count // dealers, units // shards, D // 4
    vmem = pl.BlockSpec(memory_space=pltpu.VMEM)
    out = lambda *shape: jax.ShapeDtypeStruct(shape, BF)
    given = (dy, attn, act, wo, wd, slope, normed)
    piece = width // shards
    return pl.pallas_call(
        hidden_grads,
        name="hidden_grads",
        in_specs=[HBM] * len(given),
        out_specs=[vmem] * 2 + [HBM] * 5,
        out_shape=[
            out(count, width), out(unit, D - first), out(shards, D // shards, units),
            out(count, units), out(rows, D), out(dealers, unit, first), out(dealers, piece, D),
        ],
        scratch_shapes=[
            pltpu.VMEM((shards, D // shards, units), BF), pltpu.VMEM((count, units), BF),
        ]
        + [pltpu.VMEM(value.shape, value.dtype) for value in given]
        + [pltpu.SemaphoreType.DMA((count,)) for count in (len(given), shards, 2)]
        + plane_scratch(shards, unit, first)
        + plane_scratch(shards, unit, D - first)
        + plane_scratch(shards, piece, D)
        + [pltpu.VMEM((unit, first), BF), pltpu.VMEM((piece, D), BF), pltpu.VMEM((width, D), BF)]
        + [
            pltpu.VMEM((chips, rows, D), BF), pltpu.VMEM((2, 2, rows, D), BF),
            pltpu.VMEM((chips, rows, D), BF),
            pltpu.SemaphoreType.DMA((chips,)), pltpu.SemaphoreType.DMA((chips,)),
        ]
        + gather_scratch(chips)
        + gather_scratch(chips),
        compiler_params=pltpu.CompilerParams(
            collective_id=5, has_side_effects=True, vmem_limit_bytes=VMEM_BYTES
        ),
    )(*given)


def small_sum(in_ref, out_ref, from_plane, total, from_line, send_sem, recv_sem):
    me, shard = lax.axis_index("ctx"), lax.axis_index("fsdp")
    shards, dealers = from_plane.shape[0], from_line.shape[0]
    barrier = pltpu.get_barrier_semaphore()
    others = [("fsdp", i, lax.rem(shard + i, shards)) for i in range(1, shards)]
    others += [("ctx", i, lax.rem(me + i, dealers)) for i in range(1, dealers)]
    for axis, _, who in others:
        pl.semaphore_signal(barrier, inc=1, device_id={axis: who}, device_id_type=MESH)
    pl.semaphore_wait(barrier, len(others))

    def copy(axis, i, who):
        plane = axis == "fsdp"
        k = i - 1 if plane else shards - 2 + i
        return pltpu.make_async_remote_copy(
            src_ref=in_ref.at[who] if plane else total,
            dst_ref=(from_plane if plane else from_line).at[i],
            send_sem=send_sem.at[k],
            recv_sem=recv_sem.at[k],
            device_id={axis: who},
            device_id_type=MESH,
        )

    copies = [copy(*other) for other in others]
    for one in copies[: shards - 1]:
        one.start()
    for one in copies[: shards - 1]:
        one.wait()
    value = in_ref[shard]
    for i in range(1, shards):
        value = value + from_plane[i]
    total[...] = value
    for one in copies[shards - 1 :]:
        one.start()
    for one in copies[shards - 1 :]:
        one.wait()
    for i in range(1, dealers):
        value = value + from_line[i]
    out_ref[...] = value


def small_sum_call(dealers, value):
    shards, rows, _ = value.shape
    vmem = pl.BlockSpec(memory_space=pltpu.VMEM)
    return pl.pallas_call(
        small_sum,
        name="small_sum",
        in_specs=[vmem],
        out_specs=vmem,
        out_shape=jax.ShapeDtypeStruct((rows, LANES), F32),
        scratch_shapes=[
            pltpu.VMEM((shards, rows, LANES), F32),
            pltpu.VMEM((rows, LANES), F32),
            pltpu.VMEM((dealers, rows, LANES), F32),
            pltpu.SemaphoreType.DMA((shards + dealers - 2,)),
            pltpu.SemaphoreType.DMA((shards + dealers - 2,)),
        ],
        compiler_params=pltpu.CompilerParams(collective_id=4, has_side_effects=True),
    )(value)


def place_up(in_ref, out_ref):
    unit = in_ref.shape[2]
    for i in range(in_ref.shape[0]):
        out_ref[:, i * unit : (i + 1) * unit] = in_ref[i].astype(F32)


def place_up_call(shards, grads, after=()):
    dealers, _, units = grads.shape
    rows, unit = D // shards, units // shards
    return pl.pallas_call(
        behind(place_up, len(after)),
        name="place_up",
        cost_estimate=takes(8),
        grid=(shards,),
        in_specs=[HBM] * len(after) + [pl.BlockSpec((dealers, rows, unit), lambda j: (0, 0, j))],
        out_specs=pl.BlockSpec((rows, dealers * unit), lambda j: (0, j)),
        out_shape=jax.ShapeDtypeStruct((rows, FF), F32),
        compiler_params=pltpu.CompilerParams(vmem_limit_bytes=VMEM_BYTES),
    )(*after, grads)


def place_parts(*refs):
    at, out_ref = 0, refs[-1]
    for ref in refs[:-1]:
        out_ref[:, at : at + ref.shape[2]] = ref[0].astype(F32)
        at += ref.shape[2]


def place_parts_call(*parts, after=()):
    dealers, rows, _ = parts[0].shape
    return pl.pallas_call(
        behind(place_parts, len(after)),
        name="place_parts",
        grid=(dealers,),
        in_specs=[HBM] * len(after)
        + [pl.BlockSpec((1, rows, part.shape[2]), lambda i: (i, 0, 0)) for part in parts],
        out_specs=pl.BlockSpec((rows, D), lambda i: (i, 0)),
        out_shape=jax.ShapeDtypeStruct((dealers * rows, D), F32),
        compiler_params=pltpu.CompilerParams(vmem_limit_bytes=VMEM_BYTES),
    )(*after, *parts)


def place_qkv(shards, in_ref, out_ref):
    dealers, rows, _ = in_ref.shape
    lane = lax.broadcasted_iota(jnp.int32, (rows, LANES), 1)
    for i in range(3 * shards):
        tile = slice((i // 2) * LANES, (i // 2 + 1) * LANES)
        at = (i // shards) * D + (i % shards) * (D // shards)
        for t in range(dealers // 2):
            left = in_ref[2 * t, :, tile].astype(F32)
            right = in_ref[2 * t + 1, :, tile].astype(F32)
            if i % 2 == 0:
                right = pltpu.roll(right, HD, 1)
            else:
                left = pltpu.roll(left, HD, 1)
            out_ref[:, at + t * LANES : at + (t + 1) * LANES] = jnp.where(lane < HD, left, right)


def place_qkv_call(shards, grads, after=()):
    dealers, rows, width = grads.shape
    some = rows // 4
    return pl.pallas_call(
        behind(functools.partial(place_qkv, shards), len(after)),
        name="place_qkv",
        cost_estimate=takes(9),
        grid=(rows // some,),
        in_specs=[HBM] * len(after) + [pl.BlockSpec((dealers, some, width), lambda i: (0, i, 0))],
        out_specs=pl.BlockSpec((some, 3 * D), lambda i: (i, 0)),
        out_shape=jax.ShapeDtypeStruct((rows, 3 * D), F32),
        compiler_params=pltpu.CompilerParams(vmem_limit_bytes=VMEM_BYTES),
    )(*after, grads)


def body(dealers, shards, *args):
    (
        tokens, cotangent, seq_lengths, token_order, ln_gain, ln_bias, w_qkv, q_bias, k_bias,
        v_bias, w_out, out_bias, w_up, up_bias, w_down, down_bias,
    ) = args
    rows = tokens.shape[1]
    count = dealers * rows
    me = lax.axis_index("ctx")
    shard = lax.axis_index("fsdp")
    width, units = D // dealers, FF // dealers
    head_piece, unit_piece = width // shards, units // shards

    def over_ctx(value):
        return lax.all_gather(value, "ctx", axis=0, tiled=False)

    scatter = functools.partial(
        lax.psum_scatter, axis_name="fsdp", scatter_dimension=0, tiled=True
    )
    order_rows = token_order.reshape(dealers, 1, rows)
    frequency = 10000.0 ** (-np.arange(ROT // 2) * 2.0 / ROT)
    zeros = np.zeros(HD - ROT)
    sign = np.concatenate([-np.ones(ROT // 2), np.ones(ROT // 2), zeros])
    turn = np.stack([np.concatenate([frequency, frequency, zeros]), sign]).astype(np.float32)
    turn = jnp.asarray(np.tile(turn, (1, LANES // HD)))
    parts = (ln_gain, ln_bias, q_bias, k_bias, v_bias, out_bias, up_bias, down_bias)
    parts = [part.reshape(-1, LANES) for part in parts]
    (
        small, col, row, attn, attn_f, lse, q, k, v, cosine, sine,
        normed, act, slope, dy_all, qkv_full, up_full, out_full, down_full,
    ) = phase_one_call(
        shards, seq_lengths, order_rows, turn, parts, tokens[0], cotangent[0],
        w_qkv, w_up, w_out, w_down,
    )
    qkv_full = qkv_full.reshape(D, 3 * width)
    up_full = up_full.reshape(D, units)
    vectors, at = [], 0
    for part in parts:
        vectors.append(small[:, at : at + part.shape[0]].reshape(-1))
        at += part.shape[0]
    gain, ob, db = vectors[0], vectors[5], vectors[7]
    flat = lambda value: value.reshape(count, value.shape[2])
    normed_flat = flat(normed)
    dy_all = flat(dy_all)
    out_full = out_full.reshape(width, D)
    down_full = down_full.reshape(units, D)
    rank = lax.dynamic_index_in_dim(order_rows, me, 0).reshape(rows) // dealers
    pick = (rank[None, :] == jnp.arange(rows, dtype=jnp.int32)[:, None]).astype(BF)

    d_attn, second_own, d_up, d_hidden, out_far, first_all, out_all = hidden_grads_call(
        shards, dy_all, flat(attn), flat(act), out_full, down_full, flat(slope), normed_flat
    )
    up_own = scatter(d_up.reshape(-1, units))
    out_own, second_all, d_qkv = sum_out_call(
        second_own, out_far, (attn, act, out_full, down_full),
        (q, d_attn.reshape(q.shape), attn_f, lse, col, row, k, v, cosine, sine),
    )
    dn, up_all, qkv_own = sum_back_call(
        shards, up_own, (d_qkv, d_hidden.reshape(act.shape), qkv_full, up_full), normed_flat,
        after=(out_own,),
    )
    qkv_all = over_ctx(qkv_own)
    d_w_down = place_parts_call(first_all, second_all, after=(qkv_own,))
    d_w_up = place_up_call(shards, up_all)
    d_w_out = place_parts_call(out_all, after=(qkv_own,))
    d_w_qkv = place_qkv_call(shards, qkv_all, after=(d_w_up, d_w_out, d_w_down))
    x = tokens[0].astype(F32)
    out_own = dot_tn(pick, out_own.astype(BF))
    out_act = (x + out_own + (ob + db)[None]).astype(BF)
    dn = dot_tn(pick, dn.astype(BF))
    mean = jnp.mean(x, axis=-1, keepdims=True)
    centered = x - mean
    variance = jnp.mean(centered * centered, axis=-1, keepdims=True)
    inverse = lax.rsqrt(variance + 1e-05)
    standard = centered * inverse
    grad = dn * gain[None]
    d_tokens = cotangent[0].astype(F32) + inverse * (
        grad
        - jnp.mean(grad, axis=-1, keepdims=True)
        - standard * jnp.mean(grad * standard, axis=-1, keepdims=True)
    )

    def place(vector, count):
        mine = (jnp.arange(dealers) == me)[None, :, None]
        vector = jnp.where(mine, vector.reshape(count, 1, -1), 0.0)
        return vector.reshape(count // shards, shards, -1)

    d_qkv_sum = place(jnp.sum(flat(d_qkv).astype(F32), axis=0), 3 * shards)
    d_up_sum = place(jnp.sum(d_hidden.astype(F32), axis=0), shards)
    own = lambda vector: vector.reshape(shards, -1)
    sums = jnp.concatenate(
        [
            own(jnp.sum(dn * standard, axis=0)),
            own(jnp.sum(dn, axis=0)),
            d_qkv_sum[0], d_qkv_sum[1], d_qkv_sum[2], d_up_sum[0],
            own(jnp.sum(cotangent[0].astype(F32), axis=0)),
        ],
        axis=1,
    )
    size = sums.shape[1]
    sums = sums.reshape(shards, -1, LANES)
    sums = jnp.pad(sums, ((0, 0), (0, -sums.shape[1] % 8), (0, 0)))
    sums = small_sum_call(dealers, sums).reshape(-1)[:size]
    piece = D // shards
    gain_sum, shift_sum, q_sum, k_sum, v_sum = (
        sums[i * piece : (i + 1) * piece] for i in range(5)
    )
    up_sum, dy_sum = sums[5 * piece : -piece], sums[-piece:]
    k_sum = k_sum.reshape(-1, HD)[:, :ROT].reshape(-1)
    return (
        out_act[None], d_tokens[None], gain_sum, shift_sum, d_w_qkv, q_sum, k_sum, v_sum,
        d_w_out, dy_sum, d_w_up, up_sum, d_w_down, dy_sum,
    )


def general_body(dealers, shards, *args):
    (
        tokens, cotangent, seq_lengths, token_order, ln_gain, ln_bias, w_qkv, q_bias, k_bias,
        v_bias, w_out, out_bias, w_up, up_bias, w_down, down_bias,
    ) = args
    rows = tokens.shape[1]
    count = dealers * rows
    me = lax.axis_index("ctx")
    shard = lax.axis_index("fsdp")
    width = D // dealers
    spread = HEADS % (dealers * shards) == 0
    head_piece = width // shards if spread else width
    unit_piece = FF // (dealers * shards)

    def over_ctx(value):
        return lax.all_gather(value, "ctx", axis=0, tiled=False)

    def over_fsdp(value):
        return lax.all_gather(value, "fsdp", axis=0, tiled=True)

    x_all = over_ctx(tokens[0])

    order_rows = token_order.reshape(dealers, rows)
    rank = order_rows // dealers
    places = jnp.arange(rows, dtype=jnp.int32)
    order = jnp.sum(
        jnp.where(rank[:, None, :] == places[None, :, None], order_rows[:, None, :], 0), axis=2
    )
    bounds = jnp.cumsum(seq_lengths[0])
    starts = bounds - seq_lengths[0]
    inside = (order[..., None] >= starts) & (order[..., None] < bounds)
    start = jnp.sum(jnp.where(inside, starts, 0), axis=-1)
    position = order - start
    frequency = 10000.0 ** (-jnp.arange(ROT // 2, dtype=F32) * 2.0 / ROT)
    zeros = jnp.zeros((HD - ROT,), F32)
    lane_frequency = jnp.tile(jnp.concatenate([frequency, frequency, zeros]), LANES // HD)
    sign = jnp.concatenate([-jnp.ones((ROT // 2,), F32), jnp.ones((ROT // 2,), F32), zeros])
    angles = position.astype(F32)[..., None] * lane_frequency
    cosine = jnp.cos(angles)
    sine = jnp.sin(angles) * jnp.tile(sign, LANES // HD)
    rounds = 256 // dealers
    blocks = rows // rounds
    row = order.reshape(dealers, blocks, rounds).transpose(1, 0, 2).reshape(blocks, 1, 256)
    col = jnp.stack([order, start], axis=-1)
    low = jnp.min(start.reshape(dealers, blocks, rounds), axis=(0, 2)) // 256

    own_rank = lax.dynamic_index_in_dim(rank, me, 0, keepdims=False)
    pick = (own_rank[None, :] == places[:, None]).astype(BF)
    dy_sorted = dot_nn(pick, cotangent[0]).astype(BF)
    dy_all = over_ctx(dy_sorted).reshape(count, D)

    small = jnp.concatenate(
        [ln_gain, ln_bias, q_bias, k_bias, v_bias, out_bias, up_bias, down_bias]
    )
    small = lax.all_gather(small, "fsdp", axis=0, tiled=False).astype(F32)
    vectors, at = [], 0
    for part in (ln_gain, ln_bias, q_bias, k_bias, v_bias, out_bias, up_bias, down_bias):
        vectors.append(small[:, at : at + part.shape[0]].reshape(shards * part.shape[0]))
        at += part.shape[0]
    gain, shift, qb, kb, vb, ob, ub, db = vectors
    kb = jnp.pad(kb.reshape(HEADS, ROT), ((0, 0), (0, HD - ROT))).reshape(D)

    def own_heads(matrix, axis):
        if not spread:
            return lax.dynamic_slice_in_dim(matrix, me * width, width, axis)
        return jnp.concatenate(
            [
                lax.dynamic_slice_in_dim(
                    matrix, j * (D // shards) + me * head_piece, head_piece, axis
                )
                for j in range(shards)
            ],
            axis=axis,
        )

    def own_units(matrix, axis):
        return jnp.concatenate(
            [
                lax.dynamic_slice_in_dim(
                    matrix, j * (FF // shards) + me * unit_piece, unit_piece, axis
                )
                for j in range(shards)
            ],
            axis=axis,
        )

    qkv_own = jnp.concatenate(
        [own_heads(w_qkv[:, i * D : (i + 1) * D], 1) for i in range(3)], axis=1
    )
    qkv_full = over_fsdp(qkv_own)
    bias_own = jnp.concatenate([own_heads(b, 0) for b in (qb, kb, vb)])
    up_full = over_fsdp(own_units(w_up, 1))
    up_bias_own = own_units(ub, 0)
    down_own = lax.dynamic_slice_in_dim(w_down, me * unit_piece, unit_piece, 0)
    if spread:
        out_own = lax.dynamic_slice_in_dim(w_out, me * head_piece, head_piece, 0)
        both = over_fsdp(jnp.concatenate([out_own, down_own], axis=0))
        both = both.reshape(shards, head_piece + unit_piece, D)
        out_full = both[:, :head_piece].reshape(width, D)
        down_full = both[:, head_piece:].reshape(FF // dealers, D)
    else:
        per = D // shards // width
        mine = lax.dynamic_slice_in_dim(w_out, (me % per) * width, width, 0)
        mine = jnp.where(me // per == shard, mine, jnp.zeros_like(mine))
        out_full = lax.psum(mine, "fsdp")
        down_full = over_fsdp(down_own)

    normed, q, k, v = qkv_call(
        x_all, rank[:, None, :], gain[None], shift[None], qkv_full, bias_own[None], cosine, sine
    )
    normed = normed.reshape(count, D)
    attn, attn_f, lse = flash_forward_call(low, q, k, v, col, row)
    attn = attn.reshape(count, width)
    hidden = dot_nn(normed, up_full) + up_bias_own[None]
    act, gelu_back = jax.vjp(lambda inner: jax.nn.gelu(inner, approximate=True), hidden)
    act = act.astype(BF)
    out_part = (dot_nn(attn, out_full) + dot_nn(act, down_full)).astype(BF)

    d_out = dot_tn(attn, dy_all).astype(BF)
    d_down = dot_tn(act, dy_all).astype(BF)
    scatter = functools.partial(lax.psum_scatter, scatter_dimension=0, tiled=True)
    if spread:
        d_both = jnp.concatenate(
            [d_out.reshape(shards, head_piece, D), d_down.reshape(shards, unit_piece, D)], axis=1
        )
        d_both = over_ctx(scatter(d_both.reshape(shards * (head_piece + unit_piece), D), "fsdp"))
        d_out = d_both[:, :head_piece].astype(F32).reshape(dealers * head_piece, D)
        d_down = d_both[:, head_piece:].astype(F32).reshape(dealers * unit_piece, D)
    else:
        d_out = lax.psum(d_out, "fsdp")
        d_out = jnp.where(me // per == shard, d_out, jnp.zeros_like(d_out))
        spot = jnp.zeros((per * width, D), BF)
        d_out = lax.dynamic_update_slice_in_dim(spot, d_out, (me % per) * width, 0)
        d_out = lax.psum(d_out, "ctx").astype(F32)
        d_down = over_ctx(scatter(d_down, "fsdp")).astype(F32).reshape(dealers * unit_piece, D)
    d_act = dot_nt(dy_all, down_full)
    d_hidden = gelu_back(d_act)[0].astype(BF)
    d_up = over_ctx(scatter(dot_tn(normed, d_hidden).astype(BF), "fsdp"))
    d_up = d_up.reshape(dealers, D // shards, shards, unit_piece).transpose(1, 2, 0, 3)
    d_up = d_up.astype(F32).reshape(D // shards, FF)

    d_attn = dot_nt(dy_all, out_full).astype(BF).reshape(dealers, rows, width)
    d_qkv = flash_backward_call(low, q, d_attn, attn_f, lse, col, row, k, v, cosine, sine)
    d_qkv = d_qkv.reshape(count, 3 * width)
    d_normed = (dot_nt(d_qkv, qkv_full) + dot_nt(d_hidden, up_full)).astype(BF)
    d_w_qkv = over_ctx(scatter(dot_tn(normed, d_qkv).astype(BF), "fsdp"))
    if spread:
        d_w_qkv = d_w_qkv.reshape(dealers, D // shards, 3, shards, head_piece)
        d_w_qkv = d_w_qkv.transpose(1, 2, 3, 0, 4)
    else:
        d_w_qkv = d_w_qkv.reshape(dealers, D // shards, 3, width).transpose(1, 2, 0, 3)
    d_w_qkv = d_w_qkv.astype(F32).reshape(D // shards, 3 * D)

    out_own = dot_tn(pick, scatter(out_part, "ctx"))
    x = tokens[0].astype(F32)
    out_act = (x + out_own + (ob + db)[None]).astype(BF)
    dn = dot_tn(pick, scatter(d_normed, "ctx"))
    mean = jnp.mean(x, axis=-1, keepdims=True)
    centered = x - mean
    variance = jnp.mean(centered * centered, axis=-1, keepdims=True)
    inverse = lax.rsqrt(variance + 1e-05)
    standard = centered * inverse
    grad = dn * gain[None]
    d_tokens = cotangent[0].astype(F32) + inverse * (
        grad
        - jnp.mean(grad, axis=-1, keepdims=True)
        - standard * jnp.mean(grad * standard, axis=-1, keepdims=True)
    )

    def place(vector, pieces):
        piece = vector.shape[0] // pieces
        mine = (jnp.arange(dealers) == me)[None, :, None]
        vector = vector.reshape(pieces, 1, piece)
        return jnp.where(mine, vector, 0.0).reshape(pieces * dealers * piece)

    head_pieces = shards if spread else 1
    sums = jnp.concatenate(
        [
            jnp.sum(dn * standard, axis=0),
            jnp.sum(dn, axis=0),
            jnp.sum(cotangent[0].astype(F32), axis=0),
            place(jnp.sum(d_qkv.astype(F32), axis=0), 3 * head_pieces),
            place(jnp.sum(d_hidden.astype(F32), axis=0), shards),
        ]
    )
    sums = lax.psum(sums, ("ctx", "fsdp"))

    def mine(vector):
        piece = vector.shape[0] // shards
        return lax.dynamic_slice_in_dim(vector, shard * piece, piece, 0)

    gain_sum, shift_sum, dy_sum, qkv_sum, up_sum = (
        sums[:D], sums[D : 2 * D], sums[2 * D : 3 * D], sums[3 * D : 6 * D], sums[6 * D :],
    )
    k_sum = qkv_sum[D : 2 * D].reshape(HEADS, HD)[:, :ROT].reshape(HEADS * ROT)
    return (
        out_act[None], d_tokens[None], mine(gain_sum), mine(shift_sum),
        d_w_qkv, mine(qkv_sum[:D]), mine(k_sum), mine(qkv_sum[2 * D :]),
        d_out, mine(dy_sum), d_up, mine(up_sum), d_down, mine(dy_sum),
    )


def solution(mesh):
    row, vector = P("fsdp", None), P("fsdp")
    split = P("fsdp", "ctx", None)
    in_specs = (
        split, split, row, row, vector, vector, row, vector,
        vector, vector, row, vector, row, vector, row, vector,
    )
    out_specs = (
        split, split, vector, vector, row, vector, vector, vector,
        row, vector, row, vector, row, vector,
    )
    dealers, shards = mesh.shape["ctx"], mesh.shape["fsdp"]
    fast = shards == 4 and dealers % 2 == 0 and D // (dealers * shards) == HD
    step = functools.partial(body if fast else general_body, dealers, shards)
    return jax.shard_map(
        step, mesh=mesh, in_specs=in_specs, out_specs=out_specs, check_vma=False
    )
```

```python
import functools

import jax
import jax.numpy as jnp
import numpy as np
from jax import lax
from jax.experimental import pallas as pl
from jax.experimental.pallas import tpu as pltpu
from jax.sharding import PartitionSpec as P

D = 2048
HEADS = 32
HD = 64
ROT = 32
FF = 8192
LANES = 128
VMEM_BYTES = 56 * 2**20
BF = jnp.bfloat16
F32 = jnp.float32


def dot_nn(a, b):
    return lax.dot_general(a, b, (((1,), (0,)), ((), ())), preferred_element_type=F32)


def dot_nt(a, b):
    return lax.dot_general(a, b, (((1,), (1,)), ((), ())), preferred_element_type=F32)


def dot_tn(a, b):
    return lax.dot_general(a, b, (((0,), (0,)), ((), ())), preferred_element_type=F32)


def wide(table, width):
    return jnp.concatenate([table] * (width // LANES), axis=1)


def partner(values):
    width = values.shape[1]
    lane = lax.broadcasted_iota(jnp.int32, values.shape, 1) % HD
    half = ROT // 2
    return jnp.where(
        lane < half, pltpu.roll(values, width - half, 1), pltpu.roll(values, half, 1)
    )


def sort_norm_project(
    x_ref, rank_ref, gain_ref, shift_ref, w_ref, bias_ref, cos_ref, sin_ref,
    normed_ref, q_ref, k_ref, v_ref,
):
    rows = x_ref.shape[1]
    width = q_ref.shape[2]
    place = lax.broadcasted_iota(jnp.int32, (rows, rows), 0)
    pick = jnp.where(rank_ref[0] == place, 1.0, 0.0).astype(BF)
    x = dot_nn(pick, x_ref[0])
    mean = jnp.mean(x, axis=1, keepdims=True)
    centered = x - mean
    variance = jnp.mean(centered * centered, axis=1, keepdims=True)
    normed = (centered * lax.rsqrt(variance + 1e-05) * gain_ref[...] + shift_ref[...]).astype(BF)
    normed_ref[0] = normed
    projected = dot_nn(normed, w_ref[...]) + bias_ref[...]
    cosine, sine = wide(cos_ref[0], width), wide(sin_ref[0], width)
    q = projected[:, :width]
    k = projected[:, width : 2 * width]
    q = (q * cosine + partner(q) * sine).astype(BF)
    q_ref[0] = (q.astype(F32) * 0.125).astype(BF)
    k_ref[0] = (k * cosine + partner(k) * sine).astype(BF)
    v_ref[0] = projected[:, 2 * width :].astype(BF)


def qkv_call(x_all, rank, gain, shift, weights, bias, cosine, sine):
    dealers, rows, _ = x_all.shape
    width = weights.shape[1] // 3
    whole = lambda *shape: pl.BlockSpec(shape, lambda i: (0,) * len(shape))
    each = lambda *shape: pl.BlockSpec((1,) + shape, lambda i: (i, 0, 0))
    out = lambda w: jax.ShapeDtypeStruct((dealers, rows, w), BF)
    return pl.pallas_call(
        sort_norm_project,
        name="sort_norm_project",
        grid=(dealers,),
        in_specs=[
            each(rows, D), each(1, rows), whole(1, D), whole(1, D),
            whole(D, 3 * width), whole(1, 3 * width), each(rows, LANES), each(rows, LANES),
        ],
        out_specs=[each(rows, D)] + [each(rows, width)] * 3,
        out_shape=[out(D), out(width), out(width), out(width)],
        compiler_params=pltpu.CompilerParams(vmem_limit_bytes=VMEM_BYTES),
    )(x_all, rank, gain, shift, weights, bias, cosine, sine)


def flash_forward(low_ref, q_ref, col_ref, row_ref, k_ref, v_ref, o_ref, of_ref, lse_ref):
    block = pl.program_id(0)
    dealers, rounds, width = q_ref.shape
    size = dealers * rounds
    heads = width // HD
    q = q_ref[...].reshape(size, width)
    col = col_ref[...].reshape(size, 2)
    top, bottom = col[:, 0:1], col[:, 1:2]
    head_of = lax.broadcasted_iota(jnp.int32, (size, width), 1) // HD
    q_of = [jnp.where(head_of == h, q, jnp.zeros_like(q)) for h in range(heads)]

    def step(j, carry):
        at = block - j
        running, total, mixed = carry
        window = pl.ds(pl.multiple_of(at * rounds, rounds), rounds)
        k = k_ref[:, window, :].reshape(size, width)
        v = v_ref[:, window, :].reshape(size, width)
        order = row_ref[at]
        allowed = (order <= top) & (order >= bottom)
        new_running, new_total = [], []
        for h in range(heads):
            scores = jnp.where(allowed, dot_nt(q_of[h], k), -1e30)
            peak = jnp.maximum(running[h], jnp.max(scores, axis=1, keepdims=True))
            probs = jnp.exp(scores - peak)
            scale = jnp.exp(running[h] - peak)
            new_running.append(peak)
            new_total.append(total[h] * scale + jnp.sum(probs, axis=1, keepdims=True))
            mixed = jnp.where(head_of == h, mixed * scale + dot_nn(probs.astype(BF), v), mixed)
        return (new_running, new_total, mixed)

    start = (
        [jnp.full((size, 1), -1e30, F32)] * heads,
        [jnp.zeros((size, 1), F32)] * heads,
        jnp.zeros((size, width), F32),
    )
    running, total, mixed = lax.fori_loop(0, block - low_ref[block] + 1, step, start)
    weight = jnp.zeros((size, width), F32)
    for h in range(heads):
        weight = jnp.where(head_of == h, 1.0 / total[h], weight)
    mixed = mixed * weight
    o_ref[...] = mixed.astype(BF).reshape(dealers, rounds, width)
    of_ref[...] = mixed.reshape(dealers, rounds, width)
    lse = [running[h] + jnp.log(total[h]) for h in range(heads)]
    lse_ref[...] = jnp.concatenate(lse, axis=1).reshape(dealers, rounds, heads)


def flash_forward_call(low, q, k, v, col, row, after=()):
    dealers, rows, width = q.shape
    rounds = 256 // dealers
    heads = width // HD
    part = lambda w: pl.BlockSpec((dealers, rounds, w), lambda i, low: (0, i, 0))
    whole = lambda shape: pl.BlockSpec(shape, lambda i, low: (0, 0, 0))
    return pl.pallas_call(
        behind(flash_forward, len(after), 1),
        name="flash_forward",
        cost_estimate=takes(21),
        grid_spec=pltpu.PrefetchScalarGridSpec(
            num_scalar_prefetch=1,
            grid=(rows // rounds,),
            in_specs=[HBM] * len(after)
            + [part(width), part(2), whole(row.shape), whole(k.shape), whole(v.shape)],
            out_specs=[part(width), part(width), part(heads)],
        ),
        out_shape=[
            jax.ShapeDtypeStruct(q.shape, BF),
            jax.ShapeDtypeStruct(q.shape, F32),
            jax.ShapeDtypeStruct((dealers, rows, heads), F32),
        ],
        compiler_params=pltpu.CompilerParams(vmem_limit_bytes=VMEM_BYTES),
    )(low, *after, q, col, row, k, v)


def flash_backward(
    low_ref, q_ref, da_ref, of_ref, lse_ref, col_ref, row_ref, k_ref, v_ref, cos_ref, sin_ref,
    d_ref, dk_acc, dv_acc,
):
    block = pl.program_id(0)
    dealers, rounds, width = q_ref.shape
    size = dealers * rounds
    heads = width // HD
    blocks = pl.num_programs(0)

    @pl.when(block == 0)
    def clear():
        dk_acc[...] = jnp.zeros_like(dk_acc)
        dv_acc[...] = jnp.zeros_like(dv_acc)

    q = q_ref[...].reshape(size, width)
    da = da_ref[...].reshape(size, width)
    col = col_ref[...].reshape(size, 2)
    lse = lse_ref[...].reshape(size, heads)
    top, bottom = col[:, 0:1], col[:, 1:2]
    head_of = lax.broadcasted_iota(jnp.int32, (size, width), 1) // HD
    product = da.astype(F32) * of_ref[...].reshape(size, width)
    q_of, da_of, delta = [], [], []
    for h in range(heads):
        q_of.append(jnp.where(head_of == h, q, jnp.zeros_like(q)))
        da_of.append(jnp.where(head_of == h, da, jnp.zeros_like(da)))
        delta.append(jnp.sum(jnp.where(head_of == h, product, 0.0), axis=1, keepdims=True))
    q_turned = q.astype(F32).T.astype(BF)
    da_turned = da.astype(F32).T.astype(BF)

    def step(at, dq):
        window = pl.ds(pl.multiple_of(at * rounds, rounds), rounds)
        k = k_ref[:, window, :].reshape(size, width)
        v = v_ref[:, window, :].reshape(size, width)
        order = row_ref[at]
        allowed = (order <= top) & (order >= bottom)
        for h in range(heads):
            scores = jnp.where(allowed, dot_nt(q_of[h], k), -1e30)
            probs = jnp.exp(scores - lse[:, h : h + 1])
            dprobs = dot_nt(da_of[h], v)
            dscores = (probs * (dprobs - delta[h])).astype(BF)
            own = slice(h * HD, (h + 1) * HD)
            dv_acc[at, own, :] += dot_nn(da_turned[own], probs.astype(BF))
            dk_acc[at, own, :] += dot_nn(q_turned[own], dscores)
            dq = jnp.where(head_of == h, dq + dot_nn(dscores, k), dq)
        return dq

    dq = lax.fori_loop(low_ref[block], block + 1, step, jnp.zeros((size, width), F32))

    def revert(grads, at):
        window = pl.ds(pl.multiple_of(at * rounds, rounds), rounds)
        cosine = wide(cos_ref[:, window, :].reshape(size, LANES), width)
        sine = wide(sin_ref[:, window, :].reshape(size, LANES), width)
        return grads * cosine - partner(grads) * sine

    def put(at, part, grads):
        window = pl.ds(pl.multiple_of(at * rounds, rounds), rounds)
        d_ref[:, window, part * width : (part + 1) * width] = grads.astype(BF).reshape(
            dealers, rounds, width
        )

    put(block, 0, revert(dq * 0.125, block))

    @pl.when(block == blocks - 1)
    def finish():
        def each(at, carry):
            put(at, 1, revert(dk_acc[at].T, at))
            put(at, 2, dv_acc[at].T)
            return carry

        lax.fori_loop(0, blocks, each, 0)


class CarriedBackward:
    def __init__(self, operands, d_ref, dk_acc, dv_acc):
        self.q, self.da, self.of, self.lse, self.col, self.row = operands[:6]
        self.k, self.v, self.cos, self.sin = operands[6:]
        self.d_ref, self.dk_acc, self.dv_acc = d_ref, dk_acc, dv_acc
        self.dealers, rows, self.width = self.q.shape
        self.rounds = 256 // self.dealers
        self.blocks = rows // self.rounds
        self.reach = self.dealers * rows // 2 // 256

    def window(self, at):
        return pl.ds(pl.multiple_of(at * self.rounds, self.rounds), self.rounds)

    def load(self, ref, at):
        return ref[:, self.window(at), :].reshape(256, ref.shape[2])

    def put(self, at, part, grads):
        span = slice(part * self.width, (part + 1) * self.width)
        grads = grads.astype(BF).reshape(self.dealers, self.rounds, self.width)
        self.d_ref[:, self.window(at), span] = grads

    def revert(self, grads, at):
        cosine = wide(self.load(self.cos, at), self.width)
        sine = wide(self.load(self.sin, at), self.width)
        return grads * cosine - partner(grads) * sine

    def clear(self):
        self.dk_acc[...] = jnp.zeros_like(self.dk_acc)
        self.dv_acc[...] = jnp.zeros_like(self.dv_acc)

    def block(self, block):
        size, heads = 256, self.width // HD
        q, da = self.load(self.q, block), self.load(self.da, block)
        col, lse = self.load(self.col, block), self.load(self.lse, block)
        top, bottom = col[:, 0:1], col[:, 1:2]
        head_of = lax.broadcasted_iota(jnp.int32, (size, self.width), 1) // HD
        product = da.astype(F32) * self.load(self.of, block)
        q_of, da_of, delta = [], [], []
        for h in range(heads):
            q_of.append(jnp.where(head_of == h, q, jnp.zeros_like(q)))
            da_of.append(jnp.where(head_of == h, da, jnp.zeros_like(da)))
            delta.append(jnp.sum(jnp.where(head_of == h, product, 0.0), axis=1, keepdims=True))
        q_turned = q.astype(F32).T.astype(BF)
        da_turned = da.astype(F32).T.astype(BF)

        def step(at, dq):
            k, v = self.load(self.k, at), self.load(self.v, at)
            order = self.row[at]
            allowed = (order <= top) & (order >= bottom)
            for h in range(heads):
                scores = jnp.where(allowed, dot_nt(q_of[h], k), -1e30)
                probs = jnp.exp(scores - lse[:, h : h + 1])
                dprobs = dot_nt(da_of[h], v)
                dscores = (probs * (dprobs - delta[h])).astype(BF)
                own = slice(h * HD, (h + 1) * HD)
                self.dv_acc[at, own, :] += dot_nn(da_turned[own], probs.astype(BF))
                self.dk_acc[at, own, :] += dot_nn(q_turned[own], dscores)
                dq = jnp.where(head_of == h, dq + dot_nn(dscores, k), dq)
            return dq

        lowest = jnp.maximum(block - self.reach, 0)
        dq = lax.fori_loop(lowest, block + 1, step, jnp.zeros((size, self.width), F32))
        self.put(block, 0, self.revert(dq * 0.125, block))

    def run(self, first, last):
        lax.fori_loop(first, last, lambda at, carry: (self.block(at), carry)[1], 0)

    def finish(self):
        def each(at, carry):
            self.put(at, 1, self.revert(self.dk_acc[at].T, at))
            self.put(at, 2, self.dv_acc[at].T)
            return carry

        lax.fori_loop(0, self.blocks, each, 0)


def flash_backward_call(low, q, da, of, lse, col, row, k, v, cosine, sine, after=()):
    dealers, rows, width = q.shape
    rounds = 256 // dealers
    heads = width // HD
    part = lambda w: pl.BlockSpec((dealers, rounds, w), lambda i, low: (0, i, 0))
    whole = lambda shape: pl.BlockSpec(shape, lambda i, low: (0, 0, 0))
    blocks = rows // rounds
    return pl.pallas_call(
        behind(flash_backward, len(after), 1),
        name="flash_backward",
        cost_estimate=takes(31),
        grid_spec=pltpu.PrefetchScalarGridSpec(
            num_scalar_prefetch=1,
            grid=(blocks,),
            in_specs=[HBM] * len(after)
            + [
                part(width), part(width), part(width), part(heads), part(2), whole(row.shape),
                whole(k.shape), whole(v.shape), whole(cosine.shape), whole(sine.shape),
            ],
            out_specs=whole((dealers, rows, 3 * width)),
            scratch_shapes=[pltpu.VMEM((blocks, width, 256), F32)] * 2,
        ),
        out_shape=jax.ShapeDtypeStruct((dealers, rows, 3 * width), BF),
        compiler_params=pltpu.CompilerParams(vmem_limit_bytes=VMEM_BYTES),
    )(low, *after, q, da, of, lse, col, row, k, v, cosine, sine)


MESH = pl.DeviceIdType.MESH
HBM = pl.BlockSpec(memory_space=pltpu.HBM)


def behind(kernel, waits, scalars=0):
    def run(*refs):
        kernel(*refs[:scalars], *refs[scalars + waits :])

    return run


def tie(value, *waits):
    def nothing(*refs):
        del refs

    return pl.pallas_call(
        nothing,
        name="tie",
        in_specs=[HBM] * (1 + len(waits)),
        out_specs=HBM,
        out_shape=jax.ShapeDtypeStruct(value.shape, value.dtype),
        input_output_aliases={0: 0},
    )(value, *waits)


def takes(microseconds):
    return pl.CostEstimate(
        flops=0, bytes_accessed=int(microseconds * 3.69e3), transcendentals=0
    )


def plane_neighbours(shard):
    return shard + 1 - 2 * (shard % 2), (shard + 2) % 4, 3 - shard


class PlaneGather:
    def __init__(self, out_ref, send_sem, recv_sem, base):
        self.out, self.send_sem, self.recv_sem, self.base = out_ref, send_sem, recv_sem, base
        self.shard = lax.axis_index("fsdp")
        self.half = out_ref.shape[1] // 2

    def copy(self, k, src, dst):
        x, y, _ = plane_neighbours(self.shard)
        return pltpu.make_async_remote_copy(
            src_ref=src,
            dst_ref=dst,
            send_sem=self.send_sem.at[self.base + k],
            recv_sem=self.recv_sem.at[self.base + k],
            device_id={"fsdp": x if k % 2 == 0 else y},
            device_id_type=MESH,
        )

    def part(self, slot, k):
        return self.out.at[slot, pl.ds((k % 2) * self.half, self.half)]

    def first(self, src):
        for k in range(2):
            self.copy(k, src, self.out.at[self.shard]).start()

    def forward(self):
        x, y, _ = plane_neighbours(self.shard)
        for k in range(2):
            self.copy(k, self.out.at[x], self.out.at[(x, y)[k]]).wait_recv()
        for k in range(2):
            piece = self.part((y, x)[k], k)
            self.copy(2 + k, piece, piece).start()

    def finish(self, src):
        x, y, across = plane_neighbours(self.shard)
        for k in range(2):
            self.copy(k, src, self.out.at[self.shard]).wait_send()
            piece = self.part((y, x)[k], k)
            self.copy(2 + k, piece, piece).wait_send()
            self.copy(2 + k, piece, self.part(across, k)).wait_recv()


def rows_of_orders(col_ref, row_ref):
    rounds = 256 // col_ref.shape[0]
    for at in range(row_ref.shape[0]):
        order = col_ref[:, at * rounds : (at + 1) * rounds, :].reshape(256, 2)[:, 0:1]
        order = jnp.broadcast_to(order.astype(F32), (256, LANES)).T[0:1]
        row_ref[at] = order.astype(jnp.int32)


class CarriedForward:
    def __init__(self, q_ref, k_ref, v_ref, col_ref, row_ref, o_ref, of_ref, lse_ref):
        self.q, self.k, self.v, self.col, self.row = q_ref, k_ref, v_ref, col_ref, row_ref
        self.o, self.of, self.lse = o_ref, of_ref, lse_ref
        self.dealers, rows, self.width = q_ref.shape
        self.rounds = 256 // self.dealers
        self.blocks = rows // self.rounds
        self.reach = self.dealers * rows // 2 // 256

    def window(self, at):
        return pl.ds(pl.multiple_of(at * self.rounds, self.rounds), self.rounds)

    def load(self, ref, at):
        return ref[:, self.window(at), :].reshape(256, ref.shape[2])

    def save(self, ref, at, value):
        ref[:, self.window(at), :] = value.reshape(self.dealers, self.rounds, ref.shape[2])

    def block(self, block):
        size, heads = 256, self.width // HD
        q, col = self.load(self.q, block), self.load(self.col, block)
        top, bottom = col[:, 0:1], col[:, 1:2]
        head_of = lax.broadcasted_iota(jnp.int32, (size, self.width), 1) // HD
        q_of = [jnp.where(head_of == h, q, jnp.zeros_like(q)) for h in range(heads)]

        def step(j, carry):
            at = block - j
            running, total, mixed = carry
            k, v = self.load(self.k, at), self.load(self.v, at)
            order = self.row[at]
            allowed = (order <= top) & (order >= bottom)
            new_running, new_total = [], []
            for h in range(heads):
                scores = jnp.where(allowed, dot_nt(q_of[h], k), -1e30)
                peak = jnp.maximum(running[h], jnp.max(scores, axis=1, keepdims=True))
                probs = jnp.exp(scores - peak)
                scale = jnp.exp(running[h] - peak)
                new_running.append(peak)
                new_total.append(total[h] * scale + jnp.sum(probs, axis=1, keepdims=True))
                mixed = jnp.where(head_of == h, mixed * scale + dot_nn(probs.astype(BF), v), mixed)
            return (new_running, new_total, mixed)

        start = (
            [jnp.full((size, 1), -1e30, F32)] * heads,
            [jnp.zeros((size, 1), F32)] * heads,
            jnp.zeros((size, self.width), F32),
        )
        steps = jnp.minimum(block, self.reach) + 1
        running, total, mixed = lax.fori_loop(0, steps, step, start)
        weight = jnp.zeros((size, self.width), F32)
        for h in range(heads):
            weight = jnp.where(head_of == h, 1.0 / total[h], weight)
        mixed = mixed * weight
        self.save(self.o, block, mixed.astype(BF))
        self.save(self.of, block, mixed)
        lse = [running[h] + jnp.log(total[h]) for h in range(heads)]
        self.save(self.lse, block, jnp.concatenate(lse, axis=1))

    def run(self, first, last):
        lax.fori_loop(first, last, lambda at, carry: (self.block(at), carry)[1], 0)


class LineSum:
    def __init__(self, turned, operands, out_ref, buffers):
        self.turned, self.out_ref = turned, out_ref
        self.a, self.b, self.wa, self.wb = operands
        self.mine, self.both, self.arrived, self.passing = buffers[:4]
        self.pair_send, self.pair_recv, self.line_send, self.line_recv = buffers[4:]
        self.me = lax.axis_index("ctx")
        self.chips, self.rows = self.mine.shape[:2]
        self.chip, self.core = self.me // 2, self.me % 2
        self.side = (2 * self.chip) // self.chips
        self.first = 0

    def goal(self, j):
        return (1 - self.side) * (self.chips - 1 - j) + self.side * j

    def products(self, j):
        goal, rows, tile = self.goal(j), self.rows, 1024
        pair = pl.ds(2 * goal, 2)
        a = self.a[pair].reshape(2 * rows, self.a.shape[2])
        b = self.b[pair].reshape(2 * rows, self.b.shape[2])

        def one(t, carry):
            span = pl.ds(pl.multiple_of(t * tile, tile), tile)
            if self.turned:
                value = dot_nt(a, self.wa[span, :]) + dot_nt(b, self.wb[span, :])
            else:
                value = dot_nn(a, self.wa[:, span]) + dot_nn(b, self.wb[:, span])
            self.both[j % 2, :, :, span] = value.astype(BF).reshape(2, rows, tile)
            return carry

        lax.fori_loop(0, D // tile, one, 0)

    def to_pair(self, j):
        return pltpu.make_async_remote_copy(
            src_ref=self.both.at[j % 2, 1 - self.core], dst_ref=self.arrived.at[self.goal(j)],
            send_sem=self.pair_send.at[j], recv_sem=self.pair_recv.at[j],
            device_id={"ctx": self.me + 1 - 2 * self.core}, device_id_type=MESH,
        )

    def add(self, goal, base, extra):
        def one(t, carry):
            span = pl.ds(pl.multiple_of(t * 16, 16), 16)
            value = base[span, :].astype(F32) + extra[span, :].astype(F32)
            self.mine[goal, span, :] = value.astype(BF)
            return carry

        lax.fori_loop(0, self.rows // 16, one, 0)

    def pairwise(self, j):
        if not isinstance(j, int):
            pl.when(j >= self.first + 2)(lambda: self.to_pair(j - 2).wait_send())
        self.products(j)
        self.to_pair(j).start()
        self.to_pair(j).wait_recv()
        goal = self.goal(j)
        self.add(goal, self.both.at[j % 2, self.core], self.arrived.at[goal])

    def way(self, way, s):
        last = self.chips - 1
        place = self.chip if way == 0 else last - self.chip
        goal = last - s + self.chip if way == 0 else s - (last - self.chip)
        copy = pltpu.make_async_remote_copy(
            src_ref=self.mine.at[goal], dst_ref=self.passing.at[way, s],
            send_sem=self.line_send.at[way, s], recv_sem=self.line_recv.at[way, s],
            device_id={"ctx": self.me + 2 if way == 0 else self.me - 2}, device_id_type=MESH,
        )
        return place, goal, copy

    def coming(self, way, s):
        return pltpu.make_async_remote_copy(
            src_ref=self.mine.at[self.chip], dst_ref=self.passing.at[way, s],
            send_sem=self.line_send.at[way, s], recv_sem=self.line_recv.at[way, s],
            device_id={"ctx": self.me - 2 if way == 0 else self.me + 2}, device_id_type=MESH,
        )

    def start(self, s):
        for way in range(2):
            place, _, copy = self.way(way, s)
            pl.when(place == 0)(copy.start)

    def relay(self, s):
        for way in range(2):
            place, goal, copy = self.way(way, s)

            @pl.when((place > 0) & (place <= s))
            def later(way=way, goal=goal, copy=copy):
                self.coming(way, s - 1).wait_recv()
                self.add(goal, self.mine.at[goal], self.passing.at[way, s - 1])
                copy.start()

    def last(self):
        for way in range(2):
            place = self.chip if way == 0 else self.chips - 1 - self.chip
            copy = self.coming(way, self.chips - 2)
            pl.when(place > 0)(copy.wait_recv)

        def one(t, carry):
            span = pl.ds(pl.multiple_of(t * 16, 16), 16)
            self.out_ref[span, :] = self.mine[self.chip, span, :].astype(F32)
            for way in range(2):
                place = self.chip if way == 0 else self.chips - 1 - self.chip

                @pl.when(place > 0)
                def more(way=way):
                    value = self.passing[way, self.chips - 2, span, :]
                    self.out_ref[span, :] += value.astype(F32)

            return carry

        lax.fori_loop(0, self.rows // 16, one, 0)

    def drain(self):
        for j in range(self.chips - 2, self.chips):
            self.to_pair(j).wait_send()
        for s in range(self.chips - 1):
            for way in range(2):
                place, _, copy = self.way(way, s)
                pl.when(place <= s)(copy.wait_send)


class LineGather:
    def __init__(self, own_ref, out_ref, line_send, line_recv, pair_send, pair_recv, keep_sem):
        self.own_ref, self.out_ref = own_ref, out_ref
        self.line_send, self.line_recv = line_send, line_recv
        self.pair_send, self.pair_recv, self.keep_sem = pair_send, pair_recv, keep_sem
        self.me = lax.axis_index("ctx")
        self.chips = out_ref.shape[0] // 2
        self.chip, self.core = self.me // 2, self.me % 2

    def place(self, way):
        return self.chip if way == 0 else self.chips - 1 - self.chip

    def slot(self, way, h):
        return self.me - 2 * h if way == 0 else self.me + 2 * h

    def on(self, way, h):
        slot = self.slot(way, h)
        src = self.own_ref if h == 0 else self.out_ref.at[slot]
        return pltpu.make_async_remote_copy(
            src_ref=src, dst_ref=self.out_ref.at[slot],
            send_sem=self.line_send.at[way, h], recv_sem=self.line_recv.at[way, h],
            device_id={"ctx": self.me + 2 if way == 0 else self.me - 2}, device_id_type=MESH,
        )

    def arriving(self, way, h):
        slot = self.slot(way, h)
        return pltpu.make_async_remote_copy(
            src_ref=self.own_ref, dst_ref=self.out_ref.at[slot],
            send_sem=self.line_send.at[way, h - 1], recv_sem=self.line_recv.at[way, h - 1],
            device_id={"ctx": self.me - 2 if way == 0 else self.me + 2}, device_id_type=MESH,
        )

    def across(self, chip, slot, src):
        return pltpu.make_async_remote_copy(
            src_ref=src, dst_ref=self.out_ref.at[slot],
            send_sem=self.pair_send.at[chip], recv_sem=self.pair_recv.at[chip],
            device_id={"ctx": self.me + 1 - 2 * self.core}, device_id_type=MESH,
        )

    def keep(self):
        return pltpu.make_async_copy(self.own_ref, self.out_ref.at[self.me], self.keep_sem)

    def start(self):
        for place in range(self.chips - 1):
            self.launch(place)
        self.stay()

    def launch(self, place):
        for way in range(2):
            pl.when(self.place(way) == place)(self.on(way, 0).start)

    def stay(self):
        self.across(self.chip, self.me, self.own_ref).start()
        self.keep().start()

    def step(self, h):
        for way in range(2):

            @pl.when(self.place(way) >= h)
            def come(way=way):
                self.arriving(way, h).wait_recv()
                pl.when(self.place(way) < self.chips - 1)(self.on(way, h).start)
                slot = self.slot(way, h)
                self.across(slot // 2, slot, self.out_ref.at[slot]).start()

    def come(self, chip):
        slot = 2 * chip + 1 - self.core
        self.across(chip, slot, self.out_ref.at[slot]).wait_recv()

    def finish(self, came=False):
        for h in range(self.chips - 1):
            for way in range(2):
                pl.when((self.place(way) < self.chips - 1) & (self.place(way) >= h))(
                    self.on(way, h).wait_send
                )
        for chip in range(self.chips):
            slot = 2 * chip + self.core
            self.across(chip, slot, self.out_ref.at[slot]).wait_send()
            if not came:
                self.come(chip)
        if not came:
            self.keep().wait()


def greet_all(across=False):
    me = lax.axis_index("ctx")
    chips = lax.axis_size("ctx") // 2
    chip = me // 2
    barrier = pltpu.get_barrier_semaphore()
    x, y, far = plane_neighbours(lax.axis_index("fsdp"))
    greet = lambda axis, who: pl.semaphore_signal(
        barrier, inc=1, device_id={axis: who}, device_id_type=MESH
    )
    greet("fsdp", x)
    greet("fsdp", y)
    if across:
        greet("fsdp", far)
    greet("ctx", me + 1 - 2 * (me % 2))
    pl.when(chip > 0)(lambda: greet("ctx", me - 2))
    pl.when(chip < chips - 1)(lambda: greet("ctx", me + 2))
    plane = 3 if across else 2
    line = 1 + (chip + chips - 1) // chips + (2 * chips - 2 - chip) // chips
    pl.semaphore_wait(barrier, plane + line)


def greet_line():
    me = lax.axis_index("ctx")
    chips = lax.axis_size("ctx") // 2
    chip = me // 2
    barrier = pltpu.get_barrier_semaphore()
    greet = lambda who: pl.semaphore_signal(
        barrier, inc=1, device_id={"ctx": who}, device_id_type=MESH
    )
    greet(me + 1 - 2 * (me % 2))
    pl.when(chip > 0)(lambda: greet(me - 2))
    pl.when(chip < chips - 1)(lambda: greet(me + 2))
    pl.semaphore_wait(barrier, 1 + (chip + chips - 1) // chips + (2 * chips - 2 - chip) // chips)


class Staged:
    def __init__(self, hbm_refs, vmem_refs, sem):
        self.copies = [
            pltpu.make_async_copy(src, dst, sem.at[i])
            for i, (src, dst) in enumerate(zip(hbm_refs, vmem_refs))
        ]

    def start(self):
        for copy in self.copies:
            copy.start()

    def wait(self, first, last):
        for copy in self.copies[first:last]:
            copy.wait()


class PlaneSum:
    def __init__(self, sent, come, send_sem, recv_sem):
        self.sent, self.come, self.send_sem, self.recv_sem = sent, come, send_sem, recv_sem
        self.shard, self.half = lax.axis_index("fsdp"), sent.shape[1] // 2

    def owner(self, r):
        across_x = (self.shard % 2 + r % 2) % 2
        across_y = (self.shard // 2 + r // 2) % 2
        return 2 * across_y + across_x

    def part(self, ref, slot, lower):
        return ref.at[slot, pl.ds(lower * self.half, self.half)]

    def copy(self, i):
        block, slot, lower, along = (
            (1, 0, 0, 0), (3, 1, 0, 0), (2, 0, 1, 1), (3, 1, 1, 1), (2, 2, 0, 1), (1, 2, 1, 0),
        )[i]
        x, y, _ = plane_neighbours(self.shard)
        return pltpu.make_async_remote_copy(
            src_ref=self.part(self.sent, block, lower), dst_ref=self.part(self.come, slot, lower),
            send_sem=self.send_sem.at[i], recv_sem=self.recv_sem.at[i],
            device_id={"fsdp": y if along else x}, device_id_type=MESH,
        )

    def fill(self, block):
        def one(r, carry):
            self.sent[r] = block(self.owner(r))
            return carry

        lax.fori_loop(0, self.sent.shape[0], one, 0)

    def start(self):
        for i in range(4):
            self.copy(i).start()

    def add(self, block, slot, lower):
        def one(t, carry):
            span = pl.ds(pl.multiple_of(lower * self.half + t * 16, 16), 16)
            value = self.sent[block, span, :].astype(F32) + self.come[slot, span, :].astype(F32)
            self.sent[block, span, :] = value.astype(BF)
            return carry

        lax.fori_loop(0, self.half // 16, one, 0)

    def relay(self):
        for lower, passed in ((0, 2), (1, 1)):
            self.copy(2 * lower + 1).wait_recv()
            self.add(passed, 1, lower)
            self.copy(4 + lower).start()
            self.copy(2 * lower).wait_recv()
            self.add(0, 0, lower)

    def total(self, target):
        for i in (4, 5):
            self.copy(i).wait_recv()

        def add(t, carry):
            span = pl.ds(pl.multiple_of(t * 16, 16), 16)
            value = self.sent[0, span, :].astype(F32) + self.come[2, span, :].astype(F32)
            target[span, :] = value.astype(BF)
            return carry

        lax.fori_loop(0, 2 * self.half // 16, add, 0)

    def drain(self):
        for i in range(6):
            self.copy(i).wait_send()


def plane_scratch(shards, rows, columns):
    sem = pltpu.SemaphoreType.DMA((6,))
    return [
        pltpu.VMEM((shards, rows, columns), BF), pltpu.VMEM((3, rows, columns), BF), sem, sem,
    ]


def line_scratch(chips, rows):
    return [
        pltpu.VMEM((chips, rows, D), BF),
        pltpu.VMEM((2, 2, rows, D), BF),
        pltpu.VMEM((chips, rows, D), BF),
        pltpu.VMEM((2, chips - 1, rows, D), BF),
        pltpu.SemaphoreType.DMA((chips,)),
        pltpu.SemaphoreType.DMA((chips,)),
        pltpu.SemaphoreType.DMA((2, chips - 1)),
        pltpu.SemaphoreType.DMA((2, chips - 1)),
    ]


def gather_scratch(chips):
    line = pltpu.SemaphoreType.DMA((2, chips - 1))
    pair = pltpu.SemaphoreType.DMA((chips,))
    return [line, line, pair, pair, pltpu.SemaphoreType.DMA]


def taker(refs):
    refs = list(refs)

    def take(count):
        taken = refs[:count]
        del refs[:count]
        return taken

    return take


def sum_out(own_ref, *refs):
    take = taker(refs)
    (far,), given = take(1), take(14)
    out_ref, all_ref, d_ref = take(3)
    line, gathering, held, (stage_sem, far_sem), accs = take(8), take(5), take(14), take(2), take(2)
    staged = Staged(given, held, stage_sem)
    job = LineSum(False, held[:4], out_ref, line)
    job.first = 1
    ready = pltpu.make_async_copy(far, job.mine.at[job.goal(0)], far_sem)
    gather = LineGather(own_ref, all_ref, *gathering)
    back = CarriedBackward(held[4:], d_ref, *accs)
    chips = job.chips
    ready.start()
    staged.start()
    greet_line()
    gather.start()
    ready.wait()
    job.start(0)
    staged.wait(0, 4)
    lax.fori_loop(1, chips, lambda j, carry: (job.pairwise(j), carry)[1], 0)
    for s in range(1, chips - 1):
        job.start(s)
    staged.wait(4, 14)
    back.clear()
    half, late = back.blocks // 2, back.blocks - 1
    gather.step(1)
    back.run(0, half)
    for s in range(1, chips - 2):
        job.relay(s)
        gather.step(s + 1)
    back.run(half, late)
    if chips > 2:
        job.relay(chips - 2)
    back.run(late, back.blocks)
    if chips > 2:
        gather.step(chips - 1)
    back.finish()
    job.last()
    job.drain()
    gather.finish()


def sum_out_call(own, far, operands, carried):
    dealers, rows, _ = operands[0].shape
    chips, width = dealers // 2, carried[0].shape[2]
    vmem = pl.BlockSpec(memory_space=pltpu.VMEM)
    given = (*operands, *carried)
    return pl.pallas_call(
        sum_out,
        name="sum_out",
        in_specs=[HBM] * (2 + len(given)),
        out_specs=[vmem, HBM, vmem],
        out_shape=[
            jax.ShapeDtypeStruct((rows, D), F32),
            jax.ShapeDtypeStruct((dealers,) + own.shape, own.dtype),
            jax.ShapeDtypeStruct((dealers, rows, 3 * width), BF),
        ],
        scratch_shapes=line_scratch(chips, rows)
        + gather_scratch(chips)
        + [pltpu.VMEM(value.shape, value.dtype) for value in given]
        + [pltpu.SemaphoreType.DMA((len(given),)), pltpu.SemaphoreType.DMA]
        + [pltpu.VMEM((dealers * rows // 256, width, 256), F32)] * 2,
        compiler_params=pltpu.CompilerParams(
            collective_id=2, has_side_effects=True, vmem_limit_bytes=VMEM_BYTES
        ),
    )(own, far, *given)


def sum_back(own_ref, *refs):
    take = taker(refs)
    given = take(5)
    out_ref, all_ref, qkv_ref = take(3)
    line, gathering, held, (stage_sem,), plane = take(8), take(5), take(5), take(1), take(4)
    staged = Staged(given, held, stage_sem)
    job = LineSum(True, held[:4], out_ref, line)
    gather = LineGather(own_ref, all_ref, *gathering)
    weights = PlaneSum(*plane)
    chips = job.chips
    d_qkv, normed = held[0], held[4]
    staged.start()
    greet_all()
    gather.start()
    staged.wait(0, 4)
    job.pairwise(0)
    job.start(0)
    lax.fori_loop(1, chips, lambda j, carry: (job.pairwise(j), carry)[1], 0)
    for s in range(1, chips - 1):
        job.start(s)
    staged.wait(4, 5)
    lines = qkv_ref.shape[0]
    grads = d_qkv[...].reshape(normed.shape[0], d_qkv.shape[2])

    def block(owner):
        span = pl.ds(pl.multiple_of(owner * lines, lines), lines)
        return dot_tn(normed[:, span], grads).astype(BF)

    gather.step(1)
    if chips > 2:
        job.relay(1)
    weights.fill(block)
    weights.start()
    for s in range(2, chips):
        gather.step(s)
        if s == 2:
            weights.relay()
        if s < chips - 1:
            job.relay(s)
    weights.total(qkv_ref)
    job.last()
    job.drain()
    gather.finish()
    weights.drain()


def sum_back_call(shards, own, operands, normed, after=()):
    dealers, rows, width = operands[0].shape
    chips = dealers // 2
    vmem = pl.BlockSpec(memory_space=pltpu.VMEM)
    given = (*operands, normed)
    return pl.pallas_call(
        behind(sum_back, len(after)),
        name="sum_back",
        in_specs=[HBM] * (len(after) + 1 + len(given)),
        out_specs=[vmem, HBM, vmem],
        out_shape=[
            jax.ShapeDtypeStruct((rows, D), F32),
            jax.ShapeDtypeStruct((dealers,) + own.shape, own.dtype),
            jax.ShapeDtypeStruct((D // shards, width), BF),
        ],
        scratch_shapes=line_scratch(chips, rows)
        + gather_scratch(chips)
        + [pltpu.VMEM(value.shape, value.dtype) for value in given]
        + [pltpu.SemaphoreType.DMA((len(given),))]
        + plane_scratch(shards, D // shards, width),
        compiler_params=pltpu.CompilerParams(
            collective_id=3, has_side_effects=True, vmem_limit_bytes=VMEM_BYTES
        ),
    )(*after, own, *given)


class Rows:
    def __init__(self, src_ref, dst_ref, sem):
        self.src, self.dst, self.sem = src_ref, dst_ref, sem

    def copy(self, chip):
        span = pl.ds(2 * chip, 2)
        return pltpu.make_async_copy(self.src.at[span], self.dst.at[span], self.sem.at[chip])

    def finish(self):
        for chip in range(self.src.shape[0] // 2):
            self.copy(chip).wait()


def paired(left, right, odd):
    lane = lax.broadcasted_iota(jnp.int32, left.shape, 1)
    left = jnp.where(odd, pltpu.roll(left, HD, 1), left)
    right = jnp.where(odd, right, pltpu.roll(right, HD, 1))
    return jnp.where(lane < HD, left, right)


def phase_one(*refs):
    take = taker(refs)
    lengths, orders, turn_ref = take(3)
    vectors = take(8)
    x_hbm, dy_hbm, w_qkv, w_up, w_out, w_down = take(6)
    small, col_ref, row_ref, attn_ref, attn_f_ref, lse_ref = take(6)
    q_out, k_out, v_out, cos_out, sin_out = take(5)
    normed_out, act_out, slope_out, dy_out, qkv_out, up_out, wo_out, wd_out = take(8)
    q_ref, k_ref, v_ref, cos_ref, sin_ref = take(5)
    x_all, normed, act, slope, qkv, up, raw, dy_raw, dy_own, small_own = take(10)
    tile_sem, up_sem, own_sem, send_sem, recv_sem, keep_sem = take(6)
    normed_sem, act_sem, slope_sem, q_sem, k_sem, v_sem = take(6)
    x_sems, dy_sems = take(5), take(5)
    (order_ref,) = take(1)
    me, shard = lax.axis_index("ctx"), lax.axis_index("fsdp")
    dealers, rows, width = q_ref.shape
    for dealer in range(dealers):
        order_ref[dealer] = orders[:, dealer * rows : (dealer + 1) * rows]
    chips, shards, units = dealers // 2, qkv.shape[0], act.shape[2]
    unit, heads, lines = units // shards, wo_out.shape[1], wd_out.shape[1]
    odd = me % 2 == 1

    tiles = []
    for i in range(3 * shards):
        column = (i // shards) * D + (i % shards) * (D // shards) + (me // 2) * LANES
        tiles.append(
            pltpu.make_async_copy(
                w_qkv.at[:, pl.ds(pl.multiple_of(column, LANES), LANES)],
                raw.at[:, pl.ds(i * LANES, LANES)],
                tile_sem.at[i],
            )
        )
    slices = []
    for j in range(shards):
        column = pl.multiple_of(j * (FF // shards) + me * unit, LANES)
        slices.append(
            pltpu.make_async_copy(
                w_up.at[:, pl.ds(column, unit)],
                up.at[shard, :, pl.ds(j * unit, unit)],
                up_sem.at[j],
            )
        )
    load_dy = pltpu.make_async_copy(dy_hbm, dy_raw, own_sem.at[0])
    wo_own = w_out.at[pl.ds(me * heads, heads)]
    wd_own = w_down.at[pl.ds(me * lines, lines)]
    owns = [
        pltpu.make_async_copy(wo_own, wo_out.at[shard], own_sem.at[1]),
        pltpu.make_async_copy(wd_own, wd_out.at[shard], own_sem.at[2]),
    ]
    for copy in (*tiles, *slices, load_dy):
        copy.start()
    x = LineGather(x_hbm, x_all, *x_sems)
    dy = LineGather(dy_own, dy_out, *dy_sems)
    gathers = [
        PlaneGather(out, send_sem, recv_sem, 4 * i)
        for i, out in enumerate((small, qkv, up, wd_out, wo_out))
    ]
    small_gather, qkv_gather, up_gather, wd_gather, wo_gather = gathers
    greet_all()
    x.start()

    at, starts = 0, []
    for vector in vectors:
        starts.append(at)
        small_own[at : at + vector.shape[0], :] = vector[...].astype(F32)
        at += vector.shape[0]
    small_own[at:, :] = jnp.zeros((small_own.shape[0] - at, LANES), F32)
    small[shard] = small_own[...]
    small_gather.first(small_own)
    for tile in tiles:
        tile.wait()
    for i in range(3 * shards // 2):
        left = raw[:, 2 * i * LANES : (2 * i + 1) * LANES].astype(F32)
        right = raw[:, (2 * i + 1) * LANES : (2 * i + 2) * LANES].astype(F32)
        qkv[shard, :, i * LANES : (i + 1) * LANES] = paired(left, right, odd).astype(BF)
    qkv_gather.first(qkv.at[shard])
    for own in owns:
        own.start()

    place = lax.broadcasted_iota(jnp.int32, (rows, rows), 0)
    load_dy.wait()
    pick = jnp.where(order_ref[me] // dealers == place, 1.0, 0.0).astype(BF)
    dy_own[...] = dot_nn(pick, dy_raw[...]).astype(BF)

    def tables(dealer, carry):
        order_row = order_ref[dealer]
        chosen = order_row // dealers == place
        order = jnp.sum(jnp.where(chosen, order_row.astype(F32), 0.0), axis=1, keepdims=True)
        order = order.astype(jnp.int32)
        start = jnp.zeros_like(order)
        bound = 0
        for i in range(lengths.shape[1]):
            start = jnp.where(order >= bound, bound, start)
            bound = bound + lengths[0, i]
        col_ref[dealer] = jnp.concatenate([order, start], axis=1)
        angles = (order - start).astype(F32) * turn_ref[0:1]
        cos_ref[dealer] = jnp.cos(angles)
        sin_ref[dealer] = jnp.sin(angles) * turn_ref[1:2]
        return carry

    small_gather.forward()
    lax.fori_loop(0, dealers, tables, 0)
    rows_of_orders(col_ref, row_ref)
    turned = [
        pltpu.make_async_copy(cos_ref, cos_out, keep_sem.at[2]),
        pltpu.make_async_copy(sin_ref, sin_out, keep_sem.at[3]),
    ]
    for copy in turned:
        copy.start()
    small_gather.finish(small_own)

    def line(base, count):
        return jnp.concatenate(
            [small[j, base + i : base + i + 1, :] for j in range(shards) for i in range(count)], axis=1
        )

    def heads_of(base):
        row = pl.ds(base + me // 2, 1)
        return [paired(small[j, row, :], small[j + 1, row, :], odd) for j in range(0, shards, 2)]

    def turned_heads(base):
        lane = lax.broadcasted_iota(jnp.int32, (1, LANES), 1)
        found = []
        for j in range(shards):
            value = small[j, pl.ds(base + me * ROT // LANES, 1), :]
            moved = jnp.zeros_like(value)
            for i in range(LANES // ROT):
                here = me % (LANES // ROT) == i
                moved = jnp.where(here, pltpu.roll(value, (LANES - i * ROT) % LANES, 1), moved)
            moved = jnp.where(lane < ROT, moved, 0.0)
            found.append(pltpu.roll(moved, HD, 1) if j % 2 else moved)
        return [found[j] + found[j + 1] for j in range(0, shards, 2)]

    gain, shift = line(starts[0], 4), line(starts[1], 4)
    bias = jnp.concatenate(heads_of(starts[2]) + turned_heads(starts[3]) + heads_of(starts[4]), axis=1)
    up_bias = jnp.concatenate(
        [
            small[j, pl.ds(starts[6] + me * (unit // LANES) + i, 1), :]
            for j in range(shards)
            for i in range(unit // LANES)
        ],
        axis=1,
    )

    chip = me // 2
    side = (2 * chip) // chips
    near = (1 - side) * chip + side * (chips - 1 - chip)

    def nth(j):
        zigzag = near + j // 2 if j % 2 == 0 else near - (j + 1) // 2
        close = (2 * near - j + 2 * chips) // (2 * chips)
        found = close * zigzag + (1 - close) * j
        return (1 - side) * found + side * (chips - 1 - found)

    qkv_w = qkv.reshape(D, 3 * width)
    up_w = up.reshape(D, units)
    normed_rows = Rows(normed, normed_out, normed_sem)
    act_rows, slope_rows = Rows(act, act_out, act_sem), Rows(slope, slope_out, slope_sem)
    projected_rows = [
        Rows(q_ref, q_out, q_sem), Rows(k_ref, k_out, k_sem), Rows(v_ref, v_out, v_sem),
    ]

    def project(j):
        def one(core, carry):
            dealer = 2 * nth(j) + core
            chosen = order_ref[dealer] // dealers == place
            value = dot_nn(jnp.where(chosen, 1.0, 0.0).astype(BF), x_all[dealer])
            mean = jnp.mean(value, axis=1, keepdims=True)
            centered = value - mean
            variance = jnp.mean(centered * centered, axis=1, keepdims=True)
            value = centered * lax.rsqrt(variance + 1e-05) * gain + shift
            normed[dealer] = value.astype(BF)
            projected = dot_nn(normed[dealer], qkv_w[...]) + bias
            cosine, sine = wide(cos_ref[dealer], width), wide(sin_ref[dealer], width)
            q = projected[:, :width]
            k = projected[:, width : 2 * width]
            q = (q * cosine + partner(q) * sine).astype(BF)
            q_ref[dealer] = (q.astype(F32) * 0.125).astype(BF)
            k_ref[dealer] = (k * cosine + partner(k) * sine).astype(BF)
            v_ref[dealer] = projected[:, 2 * width :].astype(BF)
            return carry

        if j == 0:
            x.keep().wait()
        x.come(nth(j))
        lax.fori_loop(0, 2, one, 0)
        for kept in (normed_rows, *projected_rows):
            kept.copy(nth(j)).start()

    def expand(at, carry):
        pair = pl.ds(2 * at, 2)
        hidden = dot_nn(normed[pair].reshape(2 * rows, D), up_w[...]) + up_bias
        square = hidden * hidden
        factor = 0.7978845608028654
        bent = jnp.tanh(factor * (hidden + 0.044715 * (hidden * square)))
        half = 0.5 * (1.0 + bent)
        act[pair] = (hidden * half).astype(BF).reshape(2, rows, units)
        grad = half + 0.5 * hidden * (1.0 - bent * bent) * (
            factor * (1.0 + 3.0 * 0.044715 * square)
        )
        slope[pair] = grad.astype(BF).reshape(2, rows, units)
        act_rows.copy(at).start()
        slope_rows.copy(at).start()
        return carry

    for copy in slices:
        copy.wait()
    x.step(1)
    dy.stay()
    dy.launch(0)
    qkv_gather.forward()
    up_gather.first(up.at[shard])
    qkv_gather.finish(qkv.at[shard])
    project(0)
    if chips > 2:
        x.step(2)
        dy.launch(1)
    for j in range(1, chips - 1):
        project(j)
    up_gather.forward()
    wd_gather.first(wd_own)
    wo_gather.first(wo_own)
    for h in range(3, chips):
        x.step(h)
        dy.launch(h - 1)
    project(chips - 1)
    x.finish(True)
    up_gather.finish(up.at[shard])
    keeps = [
        pltpu.make_async_copy(qkv, qkv_out, keep_sem.at[0]),
        pltpu.make_async_copy(up, up_out, keep_sem.at[1]),
    ]
    for keep in keeps:
        keep.start()
    flash = CarriedForward(q_ref, k_ref, v_ref, col_ref, row_ref, attn_ref, attn_f_ref, lse_ref)
    cut = flash.blocks // 2
    lax.fori_loop(0, chips // 2, expand, 0)
    dy.step(1)
    lax.fori_loop(chips // 2, chips, expand, 0)
    flash.run(0, cut)
    for h in range(2, chips - 1):
        dy.step(h)
    wd_gather.forward()
    wo_gather.forward()
    flash.run(cut, flash.blocks - 1)
    dy.step(chips - 1)
    flash.run(flash.blocks - 1, flash.blocks)
    dy.finish()
    wd_gather.finish(wd_own)
    wo_gather.finish(wo_own)
    for copy in (*owns, *keeps, *turned):
        copy.wait()
    for kept in (normed_rows, act_rows, slope_rows, *projected_rows):
        kept.finish()


def phase_one_call(shards, lengths, order, turn, vectors, x, dy, w_qkv, w_up, w_out, w_down):
    rows = x.shape[0]
    dealers = order.shape[1] // rows
    chips, blocks = dealers // 2, dealers * rows // 256
    width, units, lines = D // dealers, FF // dealers, D // shards
    vmem = pl.BlockSpec(memory_space=pltpu.VMEM)
    out = lambda kind, *shape: jax.ShapeDtypeStruct(shape, kind)
    small = sum(vector.shape[0] for vector in vectors)
    small += -small % 16
    per_row = lambda kind, w: out(kind, dealers, rows, w)
    dma = lambda *shape: pltpu.SemaphoreType.DMA(shape)
    return pl.pallas_call(
        phase_one,
        name="phase_one",
        in_specs=[pl.BlockSpec(memory_space=pltpu.SMEM)] + [vmem] * 10 + [HBM] * 6,
        out_specs=[vmem] * 6 + [HBM] * 13,
        out_shape=[
            out(F32, shards, small, LANES), per_row(jnp.int32, 2), out(jnp.int32, blocks, 1, 256),
            per_row(BF, width), per_row(F32, width), per_row(F32, width // HD),
            per_row(BF, width), per_row(BF, width), per_row(BF, width),
            per_row(F32, LANES), per_row(F32, LANES),
            per_row(BF, D), per_row(BF, units), per_row(BF, units), per_row(BF, D),
            out(BF, shards, lines, 3 * width), out(BF, shards, lines, units),
            out(BF, shards, width // shards, D), out(BF, shards, units // shards, D),
        ],
        scratch_shapes=[pltpu.VMEM((dealers, rows, width), BF)] * 3
        + [pltpu.VMEM((dealers, rows, LANES), F32)] * 2
        + [
            pltpu.VMEM((dealers, rows, D), BF), pltpu.VMEM((dealers, rows, D), BF),
            pltpu.VMEM((dealers, rows, units), BF), pltpu.VMEM((dealers, rows, units), BF),
            pltpu.VMEM((shards, lines, 3 * width), BF), pltpu.VMEM((shards, lines, units), BF),
            pltpu.VMEM((lines, 3 * shards * LANES), BF),
            pltpu.VMEM((rows, D), BF), pltpu.VMEM((rows, D), BF), pltpu.VMEM((small, LANES), F32),
            dma(3 * shards), dma(shards), dma(3), dma(20), dma(20), dma(4),
        ]
        + [dma(chips)] * 6
        + gather_scratch(chips)
        + gather_scratch(chips)
        + [pltpu.VMEM((dealers, 1, rows), jnp.int32)],
        compiler_params=pltpu.CompilerParams(
            collective_id=0, has_side_effects=True, vmem_limit_bytes=VMEM_BYTES
        ),
    )(lengths, order, turn, *vectors, x, dy, w_qkv, w_up, w_out, w_down)


def hidden_grads(*refs):
    take = taker(refs)
    given = take(7)
    d_attn_ref, second_ref, d_up_out, d_hidden_out, far_out, first_all, out_all = take(7)
    d_up_ref, d_hidden_ref = take(2)
    held, (stage_sem, up_sem, keep_sem) = take(7), take(3)
    *parts, out_sum = [PlaneSum(*take(4)) for _ in range(3)]
    first_ref, out_own, d_out = take(3)
    far, (far_send, far_recv) = take(3), take(2)
    dy, attn, act, wo, wd, slope, normed = held
    units, half = first_ref.shape
    count, shards = dy.shape[0], parts[0].sent.shape[0]
    staged = Staged(given, held, stage_sem)
    gather = LineGather(first_ref, first_all, *take(5))
    out_gather = LineGather(out_own, out_all, *take(5))
    chips = gather.chips
    width, dealers = attn.shape[1], 2 * chips
    rows = count // dealers
    job = LineSum(
        False,
        (attn.reshape(dealers, rows, width), act.reshape(dealers, rows, act.shape[1]), wo, wd),
        None,
        (*far, None, far_send, far_recv, None, None),
    )
    staged.start()
    greet_all()
    staged.wait(0, 2)

    def down_block(part):
        columns = slice(0, half) if part == 0 else slice(half, D)

        def block(owner):
            span = pl.ds(pl.multiple_of(owner * units, units), units)
            return dot_tn(act[:, span], dy[:, columns]).astype(BF)

        return block

    some = count // chips

    def attn_rows(t, carry):
        span = pl.ds(pl.multiple_of(t * some, some), some)
        d_attn_ref[span, :] = dot_nt(dy[span, :], wo[...]).astype(BF)
        return carry

    def hidden_rows(t, carry):
        span = pl.ds(pl.multiple_of(t * some, some), some)
        value = dot_nt(dy[span, :], wd[...]) * slope[span, :].astype(F32)
        d_hidden_ref[span, :] = value.astype(BF)
        return carry

    lines = normed.shape[1] // shards

    def up_rows(t, carry):
        span = pl.ds(pl.multiple_of(t * lines, lines), lines)
        value = dot_tn(normed[:, span], d_hidden_ref[...])
        d_up_ref[t] = value.astype(BF)
        leave_up(t).start()
        return carry

    def leave_up(t):
        return pltpu.make_async_copy(d_up_ref.at[t], d_up_out.at[t], up_sem.at[t])

    piece = attn.shape[1] // shards

    def out_block(owner):
        return d_out[pl.ds(pl.multiple_of(owner * piece, piece), piece), :]

    d_out[...] = dot_tn(attn[...], dy[...]).astype(BF)
    out_sum.fill(out_block)
    out_sum.start()
    staged.wait(2, 3)
    parts[0].fill(down_block(0))
    out_sum.relay()
    parts[0].start()
    parts[1].fill(down_block(1))
    out_sum.total(out_own)
    out_gather.start()
    staged.wait(3, 4)
    lax.fori_loop(0, chips, attn_rows, 0)
    parts[0].relay()
    parts[1].start()
    staged.wait(4, 6)
    out_gather.step(1)
    lax.fori_loop(0, chips // 2, hidden_rows, 0)
    parts[0].total(first_ref)
    gather.start()
    lax.fori_loop(chips // 2, chips, hidden_rows, 0)
    leave_hidden = pltpu.make_async_copy(d_hidden_ref, d_hidden_out, keep_sem.at[0])
    leave_hidden.start()
    for h in range(2, chips - 1):
        out_gather.step(h)
    job.pairwise(0)
    leave_far = pltpu.make_async_copy(job.mine.at[job.goal(0)], far_out, keep_sem.at[1])
    leave_far.start()
    parts[1].relay()
    staged.wait(6, 7)
    lax.fori_loop(0, shards // 2, up_rows, 0)
    out_gather.step(chips - 1)
    gather.step(1)
    lax.fori_loop(shards // 2, shards, up_rows, 0)
    for h in range(2, chips - 1):
        gather.step(h)
    parts[1].total(second_ref)
    gather.step(chips - 1)
    out_sum.drain()
    out_gather.finish()
    job.to_pair(0).wait_send()
    for copy in (leave_hidden, leave_far, *(leave_up(t) for t in range(shards))):
        copy.wait()
    for part in parts:
        part.drain()
    gather.finish()


def hidden_grads_call(shards, dy, attn, act, wo, wd, slope, normed):
    count, units = act.shape
    width = wo.shape[0]
    dealers = FF // units
    chips, rows, unit, first = dealers // 2, count // dealers, units // shards, D // 4
    vmem = pl.BlockSpec(memory_space=pltpu.VMEM)
    out = lambda *shape: jax.ShapeDtypeStruct(shape, BF)
    given = (dy, attn, act, wo, wd, slope, normed)
    piece = width // shards
    return pl.pallas_call(
        hidden_grads,
        name="hidden_grads",
        in_specs=[HBM] * len(given),
        out_specs=[vmem] * 2 + [HBM] * 5,
        out_shape=[
            out(count, width), out(unit, D - first), out(shards, D // shards, units),
            out(count, units), out(rows, D), out(dealers, unit, first), out(dealers, piece, D),
        ],
        scratch_shapes=[
            pltpu.VMEM((shards, D // shards, units), BF), pltpu.VMEM((count, units), BF),
        ]
        + [pltpu.VMEM(value.shape, value.dtype) for value in given]
        + [pltpu.SemaphoreType.DMA((count,)) for count in (len(given), shards, 2)]
        + plane_scratch(shards, unit, first)
        + plane_scratch(shards, unit, D - first)
        + plane_scratch(shards, piece, D)
        + [pltpu.VMEM((unit, first), BF), pltpu.VMEM((piece, D), BF), pltpu.VMEM((width, D), BF)]
        + [
            pltpu.VMEM((chips, rows, D), BF), pltpu.VMEM((2, 2, rows, D), BF),
            pltpu.VMEM((chips, rows, D), BF),
            pltpu.SemaphoreType.DMA((chips,)), pltpu.SemaphoreType.DMA((chips,)),
        ]
        + gather_scratch(chips)
        + gather_scratch(chips),
        compiler_params=pltpu.CompilerParams(
            collective_id=5, has_side_effects=True, vmem_limit_bytes=VMEM_BYTES
        ),
    )(*given)


def small_sum(in_ref, out_ref, from_plane, total, from_line, send_sem, recv_sem):
    me, shard = lax.axis_index("ctx"), lax.axis_index("fsdp")
    shards, dealers = from_plane.shape[0], from_line.shape[0]
    barrier = pltpu.get_barrier_semaphore()
    others = [("fsdp", i, lax.rem(shard + i, shards)) for i in range(1, shards)]
    others += [("ctx", i, lax.rem(me + i, dealers)) for i in range(1, dealers)]
    for axis, _, who in others:
        pl.semaphore_signal(barrier, inc=1, device_id={axis: who}, device_id_type=MESH)
    pl.semaphore_wait(barrier, len(others))

    def copy(axis, i, who):
        plane = axis == "fsdp"
        k = i - 1 if plane else shards - 2 + i
        return pltpu.make_async_remote_copy(
            src_ref=in_ref.at[who] if plane else total,
            dst_ref=(from_plane if plane else from_line).at[i],
            send_sem=send_sem.at[k],
            recv_sem=recv_sem.at[k],
            device_id={axis: who},
            device_id_type=MESH,
        )

    copies = [copy(*other) for other in others]
    for one in copies[: shards - 1]:
        one.start()
    for one in copies[: shards - 1]:
        one.wait()
    value = in_ref[shard]
    for i in range(1, shards):
        value = value + from_plane[i]
    total[...] = value
    for one in copies[shards - 1 :]:
        one.start()
    for one in copies[shards - 1 :]:
        one.wait()
    for i in range(1, dealers):
        value = value + from_line[i]
    out_ref[...] = value


def small_sum_call(dealers, value):
    shards, rows, _ = value.shape
    vmem = pl.BlockSpec(memory_space=pltpu.VMEM)
    return pl.pallas_call(
        small_sum,
        name="small_sum",
        in_specs=[vmem],
        out_specs=vmem,
        out_shape=jax.ShapeDtypeStruct((rows, LANES), F32),
        scratch_shapes=[
            pltpu.VMEM((shards, rows, LANES), F32),
            pltpu.VMEM((rows, LANES), F32),
            pltpu.VMEM((dealers, rows, LANES), F32),
            pltpu.SemaphoreType.DMA((shards + dealers - 2,)),
            pltpu.SemaphoreType.DMA((shards + dealers - 2,)),
        ],
        compiler_params=pltpu.CompilerParams(collective_id=4, has_side_effects=True),
    )(value)


def place_up(in_ref, out_ref):
    unit = in_ref.shape[2]
    for i in range(in_ref.shape[0]):
        out_ref[:, i * unit : (i + 1) * unit] = in_ref[i].astype(F32)


def place_up_call(shards, grads, after=()):
    dealers, _, units = grads.shape
    rows, unit = D // shards, units // shards
    return pl.pallas_call(
        behind(place_up, len(after)),
        name="place_up",
        cost_estimate=takes(8),
        grid=(shards,),
        in_specs=[HBM] * len(after) + [pl.BlockSpec((dealers, rows, unit), lambda j: (0, 0, j))],
        out_specs=pl.BlockSpec((rows, dealers * unit), lambda j: (0, j)),
        out_shape=jax.ShapeDtypeStruct((rows, FF), F32),
        compiler_params=pltpu.CompilerParams(vmem_limit_bytes=VMEM_BYTES),
    )(*after, grads)


def place_parts(*refs):
    at, out_ref = 0, refs[-1]
    for ref in refs[:-1]:
        out_ref[:, at : at + ref.shape[2]] = ref[0].astype(F32)
        at += ref.shape[2]


def place_parts_call(*parts, after=()):
    dealers, rows, _ = parts[0].shape
    return pl.pallas_call(
        behind(place_parts, len(after)),
        name="place_parts",
        grid=(dealers,),
        in_specs=[HBM] * len(after)
        + [pl.BlockSpec((1, rows, part.shape[2]), lambda i: (i, 0, 0)) for part in parts],
        out_specs=pl.BlockSpec((rows, D), lambda i: (i, 0)),
        out_shape=jax.ShapeDtypeStruct((dealers * rows, D), F32),
        compiler_params=pltpu.CompilerParams(vmem_limit_bytes=VMEM_BYTES),
    )(*after, *parts)


def place_qkv(shards, in_ref, out_ref):
    dealers, rows, _ = in_ref.shape
    lane = lax.broadcasted_iota(jnp.int32, (rows, LANES), 1)
    for i in range(3 * shards):
        tile = slice((i // 2) * LANES, (i // 2 + 1) * LANES)
        at = (i // shards) * D + (i % shards) * (D // shards)
        for t in range(dealers // 2):
            left = in_ref[2 * t, :, tile].astype(F32)
            right = in_ref[2 * t + 1, :, tile].astype(F32)
            if i % 2 == 0:
                right = pltpu.roll(right, HD, 1)
            else:
                left = pltpu.roll(left, HD, 1)
            out_ref[:, at + t * LANES : at + (t + 1) * LANES] = jnp.where(lane < HD, left, right)


def place_qkv_call(shards, grads, after=()):
    dealers, rows, width = grads.shape
    some = rows // 4
    return pl.pallas_call(
        behind(functools.partial(place_qkv, shards), len(after)),
        name="place_qkv",
        cost_estimate=takes(9),
        grid=(rows // some,),
        in_specs=[HBM] * len(after) + [pl.BlockSpec((dealers, some, width), lambda i: (0, i, 0))],
        out_specs=pl.BlockSpec((some, 3 * D), lambda i: (i, 0)),
        out_shape=jax.ShapeDtypeStruct((rows, 3 * D), F32),
        compiler_params=pltpu.CompilerParams(vmem_limit_bytes=VMEM_BYTES),
    )(*after, grads)


def body(dealers, shards, *args):
    (
        tokens, cotangent, seq_lengths, token_order, ln_gain, ln_bias, w_qkv, q_bias, k_bias,
        v_bias, w_out, out_bias, w_up, up_bias, w_down, down_bias,
    ) = args
    rows = tokens.shape[1]
    count = dealers * rows
    me = lax.axis_index("ctx")
    shard = lax.axis_index("fsdp")
    width, units = D // dealers, FF // dealers
    head_piece, unit_piece = width // shards, units // shards

    def over_ctx(value):
        return lax.all_gather(value, "ctx", axis=0, tiled=False)

    scatter = functools.partial(
        lax.psum_scatter, axis_name="fsdp", scatter_dimension=0, tiled=True
    )
    order_rows = token_order.reshape(dealers, 1, rows)
    frequency = 10000.0 ** (-np.arange(ROT // 2) * 2.0 / ROT)
    zeros = np.zeros(HD - ROT)
    sign = np.concatenate([-np.ones(ROT // 2), np.ones(ROT // 2), zeros])
    turn = np.stack([np.concatenate([frequency, frequency, zeros]), sign]).astype(np.float32)
    turn = jnp.asarray(np.tile(turn, (1, LANES // HD)))
    parts = (ln_gain, ln_bias, q_bias, k_bias, v_bias, out_bias, up_bias, down_bias)
    parts = [part.reshape(-1, LANES) for part in parts]
    (
        small, col, row, attn, attn_f, lse, q, k, v, cosine, sine,
        normed, act, slope, dy_all, qkv_full, up_full, out_full, down_full,
    ) = phase_one_call(
        shards, seq_lengths, token_order, turn, parts, tokens[0], cotangent[0],
        w_qkv, w_up, w_out, w_down,
    )
    qkv_full = qkv_full.reshape(D, 3 * width)
    up_full = up_full.reshape(D, units)
    vectors, at = [], 0
    for part in parts:
        vectors.append(small[:, at : at + part.shape[0]].reshape(-1))
        at += part.shape[0]
    gain, ob, db = vectors[0], vectors[5], vectors[7]
    flat = lambda value: value.reshape(count, value.shape[2])
    normed_flat = flat(normed)
    dy_all = flat(dy_all)
    out_full = out_full.reshape(width, D)
    down_full = down_full.reshape(units, D)
    rank = lax.dynamic_index_in_dim(order_rows, me, 0).reshape(rows) // dealers
    pick = (rank[None, :] == jnp.arange(rows, dtype=jnp.int32)[:, None]).astype(BF)

    d_attn, second_own, d_up, d_hidden, out_far, first_all, out_all = hidden_grads_call(
        shards, dy_all, flat(attn), flat(act), out_full, down_full, flat(slope), normed_flat
    )
    up_own = scatter(d_up.reshape(-1, units))
    out_own, second_all, d_qkv = sum_out_call(
        second_own, out_far, (attn, act, out_full, down_full),
        (q, d_attn.reshape(q.shape), attn_f, lse, col, row, k, v, cosine, sine),
    )
    dn, up_all, qkv_own = sum_back_call(
        shards, up_own, (d_qkv, d_hidden.reshape(act.shape), qkv_full, up_full), normed_flat,
        after=(out_own,),
    )
    qkv_all = over_ctx(qkv_own)
    d_w_down = place_parts_call(first_all, second_all, after=(qkv_own,))
    d_w_up = place_up_call(shards, up_all)
    d_w_out = place_parts_call(out_all, after=(qkv_own,))
    d_w_qkv = place_qkv_call(shards, qkv_all, after=(d_w_up, d_w_out, d_w_down))
    x = tokens[0].astype(F32)
    out_own = dot_tn(pick, out_own.astype(BF))
    out_act = (x + out_own + (ob + db)[None]).astype(BF)
    dn = dot_tn(pick, dn.astype(BF))
    mean = jnp.mean(x, axis=-1, keepdims=True)
    centered = x - mean
    variance = jnp.mean(centered * centered, axis=-1, keepdims=True)
    inverse = lax.rsqrt(variance + 1e-05)
    standard = centered * inverse
    grad = dn * gain[None]
    d_tokens = cotangent[0].astype(F32) + inverse * (
        grad
        - jnp.mean(grad, axis=-1, keepdims=True)
        - standard * jnp.mean(grad * standard, axis=-1, keepdims=True)
    )

    def place(vector, count):
        mine = (jnp.arange(dealers) == me)[None, :, None]
        vector = jnp.where(mine, vector.reshape(count, 1, -1), 0.0)
        return vector.reshape(count // shards, shards, -1)

    d_qkv_sum = place(jnp.sum(flat(d_qkv).astype(F32), axis=0), 3 * shards)
    d_up_sum = place(jnp.sum(d_hidden.astype(F32), axis=0), shards)
    own = lambda vector: vector.reshape(shards, -1)
    sums = jnp.concatenate(
        [
            own(jnp.sum(dn * standard, axis=0)),
            own(jnp.sum(dn, axis=0)),
            d_qkv_sum[0], d_qkv_sum[1], d_qkv_sum[2], d_up_sum[0],
            own(jnp.sum(cotangent[0].astype(F32), axis=0)),
        ],
        axis=1,
    )
    size = sums.shape[1]
    sums = sums.reshape(shards, -1, LANES)
    sums = jnp.pad(sums, ((0, 0), (0, -sums.shape[1] % 8), (0, 0)))
    sums = small_sum_call(dealers, sums).reshape(-1)[:size]
    piece = D // shards
    gain_sum, shift_sum, q_sum, k_sum, v_sum = (
        sums[i * piece : (i + 1) * piece] for i in range(5)
    )
    up_sum, dy_sum = sums[5 * piece : -piece], sums[-piece:]
    k_sum = k_sum.reshape(-1, HD)[:, :ROT].reshape(-1)
    return (
        out_act[None], d_tokens[None], gain_sum, shift_sum, d_w_qkv, q_sum, k_sum, v_sum,
        d_w_out, dy_sum, d_w_up, up_sum, d_w_down, dy_sum,
    )


def general_body(dealers, shards, *args):
    (
        tokens, cotangent, seq_lengths, token_order, ln_gain, ln_bias, w_qkv, q_bias, k_bias,
        v_bias, w_out, out_bias, w_up, up_bias, w_down, down_bias,
    ) = args
    rows = tokens.shape[1]
    count = dealers * rows
    me = lax.axis_index("ctx")
    shard = lax.axis_index("fsdp")
    width = D // dealers
    spread = HEADS % (dealers * shards) == 0
    head_piece = width // shards if spread else width
    unit_piece = FF // (dealers * shards)

    def over_ctx(value):
        return lax.all_gather(value, "ctx", axis=0, tiled=False)

    def over_fsdp(value):
        return lax.all_gather(value, "fsdp", axis=0, tiled=True)

    x_all = over_ctx(tokens[0])

    order_rows = token_order.reshape(dealers, rows)
    rank = order_rows // dealers
    places = jnp.arange(rows, dtype=jnp.int32)
    order = jnp.sum(
        jnp.where(rank[:, None, :] == places[None, :, None], order_rows[:, None, :], 0), axis=2
    )
    bounds = jnp.cumsum(seq_lengths[0])
    starts = bounds - seq_lengths[0]
    inside = (order[..., None] >= starts) & (order[..., None] < bounds)
    start = jnp.sum(jnp.where(inside, starts, 0), axis=-1)
    position = order - start
    frequency = 10000.0 ** (-jnp.arange(ROT // 2, dtype=F32) * 2.0 / ROT)
    zeros = jnp.zeros((HD - ROT,), F32)
    lane_frequency = jnp.tile(jnp.concatenate([frequency, frequency, zeros]), LANES // HD)
    sign = jnp.concatenate([-jnp.ones((ROT // 2,), F32), jnp.ones((ROT // 2,), F32), zeros])
    angles = position.astype(F32)[..., None] * lane_frequency
    cosine = jnp.cos(angles)
    sine = jnp.sin(angles) * jnp.tile(sign, LANES // HD)
    rounds = 256 // dealers
    blocks = rows // rounds
    row = order.reshape(dealers, blocks, rounds).transpose(1, 0, 2).reshape(blocks, 1, 256)
    col = jnp.stack([order, start], axis=-1)
    low = jnp.min(start.reshape(dealers, blocks, rounds), axis=(0, 2)) // 256

    own_rank = lax.dynamic_index_in_dim(rank, me, 0, keepdims=False)
    pick = (own_rank[None, :] == places[:, None]).astype(BF)
    dy_sorted = dot_nn(pick, cotangent[0]).astype(BF)
    dy_all = over_ctx(dy_sorted).reshape(count, D)

    small = jnp.concatenate(
        [ln_gain, ln_bias, q_bias, k_bias, v_bias, out_bias, up_bias, down_bias]
    )
    small = lax.all_gather(small, "fsdp", axis=0, tiled=False).astype(F32)
    vectors, at = [], 0
    for part in (ln_gain, ln_bias, q_bias, k_bias, v_bias, out_bias, up_bias, down_bias):
        vectors.append(small[:, at : at + part.shape[0]].reshape(shards * part.shape[0]))
        at += part.shape[0]
    gain, shift, qb, kb, vb, ob, ub, db = vectors
    kb = jnp.pad(kb.reshape(HEADS, ROT), ((0, 0), (0, HD - ROT))).reshape(D)

    def own_heads(matrix, axis):
        if not spread:
            return lax.dynamic_slice_in_dim(matrix, me * width, width, axis)
        return jnp.concatenate(
            [
                lax.dynamic_slice_in_dim(
                    matrix, j * (D // shards) + me * head_piece, head_piece, axis
                )
                for j in range(shards)
            ],
            axis=axis,
        )

    def own_units(matrix, axis):
        return jnp.concatenate(
            [
                lax.dynamic_slice_in_dim(
                    matrix, j * (FF // shards) + me * unit_piece, unit_piece, axis
                )
                for j in range(shards)
            ],
            axis=axis,
        )

    qkv_own = jnp.concatenate(
        [own_heads(w_qkv[:, i * D : (i + 1) * D], 1) for i in range(3)], axis=1
    )
    qkv_full = over_fsdp(qkv_own)
    bias_own = jnp.concatenate([own_heads(b, 0) for b in (qb, kb, vb)])
    up_full = over_fsdp(own_units(w_up, 1))
    up_bias_own = own_units(ub, 0)
    down_own = lax.dynamic_slice_in_dim(w_down, me * unit_piece, unit_piece, 0)
    if spread:
        out_own = lax.dynamic_slice_in_dim(w_out, me * head_piece, head_piece, 0)
        both = over_fsdp(jnp.concatenate([out_own, down_own], axis=0))
        both = both.reshape(shards, head_piece + unit_piece, D)
        out_full = both[:, :head_piece].reshape(width, D)
        down_full = both[:, head_piece:].reshape(FF // dealers, D)
    else:
        per = D // shards // width
        mine = lax.dynamic_slice_in_dim(w_out, (me % per) * width, width, 0)
        mine = jnp.where(me // per == shard, mine, jnp.zeros_like(mine))
        out_full = lax.psum(mine, "fsdp")
        down_full = over_fsdp(down_own)

    normed, q, k, v = qkv_call(
        x_all, rank[:, None, :], gain[None], shift[None], qkv_full, bias_own[None], cosine, sine
    )
    normed = normed.reshape(count, D)
    attn, attn_f, lse = flash_forward_call(low, q, k, v, col, row)
    attn = attn.reshape(count, width)
    hidden = dot_nn(normed, up_full) + up_bias_own[None]
    act, gelu_back = jax.vjp(lambda inner: jax.nn.gelu(inner, approximate=True), hidden)
    act = act.astype(BF)
    out_part = (dot_nn(attn, out_full) + dot_nn(act, down_full)).astype(BF)

    d_out = dot_tn(attn, dy_all).astype(BF)
    d_down = dot_tn(act, dy_all).astype(BF)
    scatter = functools.partial(lax.psum_scatter, scatter_dimension=0, tiled=True)
    if spread:
        d_both = jnp.concatenate(
            [d_out.reshape(shards, head_piece, D), d_down.reshape(shards, unit_piece, D)], axis=1
        )
        d_both = over_ctx(scatter(d_both.reshape(shards * (head_piece + unit_piece), D), "fsdp"))
        d_out = d_both[:, :head_piece].astype(F32).reshape(dealers * head_piece, D)
        d_down = d_both[:, head_piece:].astype(F32).reshape(dealers * unit_piece, D)
    else:
        d_out = lax.psum(d_out, "fsdp")
        d_out = jnp.where(me // per == shard, d_out, jnp.zeros_like(d_out))
        spot = jnp.zeros((per * width, D), BF)
        d_out = lax.dynamic_update_slice_in_dim(spot, d_out, (me % per) * width, 0)
        d_out = lax.psum(d_out, "ctx").astype(F32)
        d_down = over_ctx(scatter(d_down, "fsdp")).astype(F32).reshape(dealers * unit_piece, D)
    d_act = dot_nt(dy_all, down_full)
    d_hidden = gelu_back(d_act)[0].astype(BF)
    d_up = over_ctx(scatter(dot_tn(normed, d_hidden).astype(BF), "fsdp"))
    d_up = d_up.reshape(dealers, D // shards, shards, unit_piece).transpose(1, 2, 0, 3)
    d_up = d_up.astype(F32).reshape(D // shards, FF)

    d_attn = dot_nt(dy_all, out_full).astype(BF).reshape(dealers, rows, width)
    d_qkv = flash_backward_call(low, q, d_attn, attn_f, lse, col, row, k, v, cosine, sine)
    d_qkv = d_qkv.reshape(count, 3 * width)
    d_normed = (dot_nt(d_qkv, qkv_full) + dot_nt(d_hidden, up_full)).astype(BF)
    d_w_qkv = over_ctx(scatter(dot_tn(normed, d_qkv).astype(BF), "fsdp"))
    if spread:
        d_w_qkv = d_w_qkv.reshape(dealers, D // shards, 3, shards, head_piece)
        d_w_qkv = d_w_qkv.transpose(1, 2, 3, 0, 4)
    else:
        d_w_qkv = d_w_qkv.reshape(dealers, D // shards, 3, width).transpose(1, 2, 0, 3)
    d_w_qkv = d_w_qkv.astype(F32).reshape(D // shards, 3 * D)

    out_own = dot_tn(pick, scatter(out_part, "ctx"))
    x = tokens[0].astype(F32)
    out_act = (x + out_own + (ob + db)[None]).astype(BF)
    dn = dot_tn(pick, scatter(d_normed, "ctx"))
    mean = jnp.mean(x, axis=-1, keepdims=True)
    centered = x - mean
    variance = jnp.mean(centered * centered, axis=-1, keepdims=True)
    inverse = lax.rsqrt(variance + 1e-05)
    standard = centered * inverse
    grad = dn * gain[None]
    d_tokens = cotangent[0].astype(F32) + inverse * (
        grad
        - jnp.mean(grad, axis=-1, keepdims=True)
        - standard * jnp.mean(grad * standard, axis=-1, keepdims=True)
    )

    def place(vector, pieces):
        piece = vector.shape[0] // pieces
        mine = (jnp.arange(dealers) == me)[None, :, None]
        vector = vector.reshape(pieces, 1, piece)
        return jnp.where(mine, vector, 0.0).reshape(pieces * dealers * piece)

    head_pieces = shards if spread else 1
    sums = jnp.concatenate(
        [
            jnp.sum(dn * standard, axis=0),
            jnp.sum(dn, axis=0),
            jnp.sum(cotangent[0].astype(F32), axis=0),
            place(jnp.sum(d_qkv.astype(F32), axis=0), 3 * head_pieces),
            place(jnp.sum(d_hidden.astype(F32), axis=0), shards),
        ]
    )
    sums = lax.psum(sums, ("ctx", "fsdp"))

    def mine(vector):
        piece = vector.shape[0] // shards
        return lax.dynamic_slice_in_dim(vector, shard * piece, piece, 0)

    gain_sum, shift_sum, dy_sum, qkv_sum, up_sum = (
        sums[:D], sums[D : 2 * D], sums[2 * D : 3 * D], sums[3 * D : 6 * D], sums[6 * D :],
    )
    k_sum = qkv_sum[D : 2 * D].reshape(HEADS, HD)[:, :ROT].reshape(HEADS * ROT)
    return (
        out_act[None], d_tokens[None], mine(gain_sum), mine(shift_sum),
        d_w_qkv, mine(qkv_sum[:D]), mine(k_sum), mine(qkv_sum[2 * D :]),
        d_out, mine(dy_sum), d_up, mine(up_sum), d_down, mine(dy_sum),
    )


def solution(mesh):
    row, vector = P("fsdp", None), P("fsdp")
    split = P("fsdp", "ctx", None)
    in_specs = (
        split, split, row, row, vector, vector, row, vector,
        vector, vector, row, vector, row, vector, row, vector,
    )
    out_specs = (
        split, split, vector, vector, row, vector, vector, vector,
        row, vector, row, vector, row, vector,
    )
    dealers, shards = mesh.shape["ctx"], mesh.shape["fsdp"]
    fast = shards == 4 and dealers % 2 == 0 and D // (dealers * shards) == HD
    step = functools.partial(body if fast else general_body, dealers, shards)
    return jax.shard_map(
        step, mesh=mesh, in_specs=in_specs, out_specs=out_specs, check_vma=False
    )
```
